32 devices in a mesh: dp: 16 (over z, x, core), mp: 2 (over y).
Axes of the slice: x: 2, y: 2, z: 4, core: 2. Of those that a mesh axis runs over, the one named last changes fastest.
Arguments:
- inputs: bfloat16 [16, 2048, 768], P('dp', 'mp'), may hold values from -6 to 6
- seg_ids: int32 [16, 2048], P('dp'), may hold values from 0 to 7, as said below
- omega: float32 [64, 32], replicated, may hold values from -5 to 5
- norm1_gain: float32 [768], replicated, may hold values from 0.1 to 1.9
- qkv_weight: bfloat16 [768, 3, 768], P(None, None, 'mp'), may hold values from -0.21875 to 0.21875
- out_weight: bfloat16 [768, 768], P('mp'), may hold values from -3.5 to 3.5
- norm2_gain: float32 [768], replicated, may hold values from 0.1 to 1.9
- up_weight: bfloat16 [768, 3072], P(None, 'mp'), may hold values from -0.21875 to 0.21875
- down_weight: bfloat16 [3072, 768], P('mp'), may hold values from -0.109375 to 0.109375
- out_grad: bfloat16 [16, 2048, 768], P('dp', 'mp'), may hold values from -6 to 6
Outputs:
- output: bfloat16 [16, 2048, 768], P('dp', 'mp')
- input_grad: float32 [16, 2048, 768], P('dp', 'mp')
- norm1_gain_grad: float32 [768], P(('dp', 'mp'))
- qkv_weight_grad: float32 [768, 3, 768], P('dp', None, 'mp')
- out_weight_grad: float32 [768, 768], P('mp', 'dp')
- norm2_gain_grad: float32 [768], P(('dp', 'mp'))
- up_weight_grad: float32 [768, 3072], P('dp', 'mp')
- down_weight_grad: float32 [3072, 768], P('mp', 'dp')
The draws below stay inside these ranges and needn't reach their ends.
Inputs may be any that keep to these rules, and one draw needn't show every extreme that they name: `seg_ids`: along each sequence the document number never falls, starts at 0 and ends at 7; no document boundary lies in the middle half of a sequence.
All inputs are finite; a program needn't handle non-finite values.
Results may differ from the reference program's by a relative error of at most 0.0095.
Values may be sent and summed in bfloat16 or wider, within the bound.
No kernel may reach another device: no remote copies, remote signals or barrier semaphores. Data moves between devices by JAX's collectives and lax.ppermute only.
A program may use at most 192 MiB of HBM per device.

```python
import jax
import jax.numpy as jnp
from jax import lax

D = 768
HEADS = 12
HD = 64
FF = 3072
FEAT = 32
SEGS = 8
LEN = 2048
SEQS = 16


def draw_seg_ids(key, part):
    key = jax.random.fold_in(key, 11)
    seq_keys = jax.random.split(key, SEQS)
    lower_count = LEN // 4 - 1

    def one_sequence(seq_key):
        picks = jax.random.randint(seq_key, (SEGS - 1,), 0, LEN // 2 - 1)
        cuts = jnp.where(picks < lower_count, picks + 1, picks - lower_count + 3 * (LEN // 4))
        places = jnp.arange(LEN)
        return jnp.sum((places[:, None] >= cuts[None, :]).astype(jnp.int32), axis=1).astype(jnp.int32)
    return jax.vmap(one_sequence)(seq_keys)


def spiked(drawn, own_key, source, target, blocks, factor):
    owner, partner = [(jnp.arange(drawn.shape[axis_at]) // (drawn.shape[axis_at] // blocks)).reshape([-1 if axis == axis_at else 1 for axis in range(drawn.ndim)]) for axis_at in (source, target)]
    chosen = jax.random.permutation(own_key, blocks)[partner]
    strong = (owner == chosen) | (owner == (partner + blocks // 2) % blocks)
    return jnp.where(strong, factor * drawn, drawn)


def steps_of(stream_key, shape, pieces, low, high):
    level = 1.0
    for position, blocks in pieces:
        draws = jax.random.uniform(jax.random.fold_in(jax.random.fold_in(stream_key, 6), position), (blocks,), jnp.float32, low / len(pieces), high / len(pieces))
        level = level * jnp.repeat(jnp.exp(draws), shape[position] // blocks).reshape((-1,) + (1,) * (len(shape) - 1 - position))
    return level


def gaussian(own_key, dims, width, bound, cuts=(), kind=jnp.bfloat16):
    loudness = steps_of(own_key, dims, cuts, -0.22, 0.18) if cuts else 1.0
    array = jax.random.normal(own_key, dims, jnp.float32) * width * loudness
    return jnp.minimum(jnp.maximum(array, -bound), bound).astype(kind)


def gaussian_with(key, shape, scale, limit, cuts, heavy, held_as=jnp.bfloat16):
    entries = scale * jax.random.normal(key, shape, jnp.float32)
    if cuts:
        entries = entries * steps_of(key, shape, cuts, -0.22, 0.18)
    return jnp.clip(spiked(entries, jax.random.fold_in(key, 3), *heavy), -limit, limit).astype(held_as)


def setup_inputs(seed: int = 0) -> dict:
    streams_of = jax.random.split(jax.random.key(seed), 11)
    inputs = gaussian(streams_of[0], (SEQS, LEN, D), 1.0, 6.0, ((0, 16), (1, 2)))
    seg_ids = draw_seg_ids(jax.random.fold_in(streams_of[10], 71), 0)
    omega = gaussian(streams_of[2], (HD, FEAT), 1.0, 5.0, (), jnp.float32)
    norm1_gain = jnp.clip(1.0 + 0.18 * jax.random.normal(streams_of[3], (D,), jnp.float32), 0.1, 1.9)
    qkv_weight = gaussian(streams_of[4], (D, 3, HEADS * HD), D ** -0.5, 0.21875, ((2, 2),))
    out_weight = gaussian(streams_of[5], (HEADS * HD, D), (max(1, HEADS * HD * SEGS // LEN)) ** -0.5, 3.5, ((0, 2),))
    norm2_gain = jnp.clip(1.0 + 0.18 * jax.random.normal(streams_of[6], (D,), jnp.float32), 0.1, 1.9)
    up_weight = gaussian(streams_of[7], (D, FF), D ** -0.5, 0.21875, ((1, 2),))
    down_weight = gaussian(streams_of[8], (FF, D), FF ** -0.5, 0.109375, ((0, 2),))
    out_grad = gaussian_with(streams_of[9], (SEQS, LEN, D), 1.0, 6.0, ((0, 16), (1, 2)), (0, 2, 16, 2.0))
    return {"inputs": inputs, "seg_ids": seg_ids, "omega": omega, "norm1_gain": norm1_gain, "qkv_weight": qkv_weight, "out_weight": out_weight, "norm2_gain": norm2_gain, "up_weight": up_weight, "down_weight": down_weight, "out_grad": out_grad}


@jax.custom_vjp
def low(v):
    return lax.optimization_barrier(v.astype(jnp.bfloat16)).astype(jnp.float32)

@jax.custom_vjp
def low_back(v):
    return v

def low_keep(v):
    return (low(v), None)

def low_pass(kept, grad):
    return (grad,)

def back_keep(v):
    return (v, None)

def back_low(kept, grad):
    return (low(grad),)
low.defvjp(low_keep, low_pass)
low_back.defvjp(back_keep, back_low)
HIGH = lax.Precision.HIGHEST

def layer_norm(values, gain):
    middle = lax.optimization_barrier(jnp.mean(values, axis=-1, keepdims=True))
    centred = values - middle
    spread = lax.optimization_barrier(jnp.mean(centred * centred, axis=-1, keepdims=True))
    return centred * lax.rsqrt(spread + 1e-05) * gain

def rotary_tables(total, head_size):
    places = jnp.arange(total).astype(jnp.float32)
    rates = 10000.0 ** (-(jnp.arange(head_size // 2).astype(jnp.float32) * 2.0 / head_size))
    angles = places[:, None] * rates[None, :]
    return (jnp.cos(angles)[:, None, :], jnp.sin(angles)[:, None, :])

def rotate(vectors, cosine, sine_table):
    half = vectors.shape[-1] // 2
    first = vectors[..., :half]
    second = vectors[..., half:]
    return jnp.concatenate([first * cosine - second * sine_table, second * cosine + first * sine_table], axis=-1)

def attend(qkv, onehot, omega, cosine, sine_table):
    total = qkv.shape[0]
    head_size = omega.shape[0]
    parts = qkv.reshape(total, 3, -1, head_size)
    scale = head_size ** (-0.25)
    query_rot = rotate(parts[:, 0], cosine, sine_table) * scale
    key_rot = rotate(parts[:, 1], cosine, sine_table) * scale
    values = parts[:, 2]
    query_feat = jax.nn.softplus(jnp.einsum('lhd,df->lhf', query_rot, omega, precision=HIGH))
    key_feat = jax.nn.softplus(jnp.einsum('lhd,df->lhf', key_rot, omega, precision=HIGH))
    key_doc = onehot[:, :, None, None] * key_feat[:, None]
    state = jnp.einsum('lshf,lhe->hsfe', key_doc, values, precision=HIGH)
    totals = jnp.einsum('ls,lhf->hsf', onehot, key_feat, precision=HIGH)
    query_doc = onehot[:, :, None, None] * query_feat[:, None]
    numer = jnp.einsum('lshf,hsfe->lhe', query_doc, state, precision=HIGH)
    denom = jnp.einsum('lshf,hsf->lh', query_doc, totals, precision=HIGH)
    return (numer / denom[:, :, None]).reshape(total, -1)

def reference(inputs, seg_ids, omega, norm1_gain, qkv_weight, out_weight, norm2_gain, up_weight, down_weight, out_grad):
    weights = tuple((w.astype(jnp.float32) for w in (norm1_gain, qkv_weight, out_weight, norm2_gain, up_weight, down_weight)))
    cosine, sine_table = rotary_tables(LEN, HD)
    omega_f = omega.astype(jnp.float32)

    def sequence_step(carry, item):
        rows_in, segment, cotangent = item
        onehot = (segment[:, None] == jnp.arange(SEGS)[None, :]).astype(jnp.float32)

        def forward(xrows, gain_one, wqkv, wout, gain_two, wup, wdown):
            first = low(layer_norm(xrows, gain_one))
            qkv = low_back(jnp.dot(first, wqkv.reshape(D, -1), precision=HIGH))
            attn = low(attend(qkv, onehot, omega_f, cosine, sine_table))
            branch = low_back(jnp.dot(attn, wout, precision=HIGH))
            middle = xrows + branch
            second = low(layer_norm(middle, gain_two))
            hpre = low_back(jnp.dot(second, wup, precision=HIGH))
            hact = low(jax.nn.gelu(hpre))
            ffn = low_back(jnp.dot(hact, wdown, precision=HIGH))
            return middle + ffn
        result, backward = jax.vjp(forward, rows_in.astype(jnp.float32), *weights)
        grads = backward(cotangent.astype(jnp.float32))
        carry = tuple((c + g for c, g in zip(carry, grads[1:])))
        return (carry, (result.astype(jnp.bfloat16), grads[0]))
    zeros = tuple((jnp.zeros_like(w) for w in weights))
    sums, (outputs, input_grads) = lax.scan(sequence_step, zeros, (inputs, seg_ids, out_grad))
    return (outputs, input_grads, sums[0], sums[1], sums[2], sums[3], sums[4], sums[5])
```

```python
import functools

import jax
import jax.numpy as jnp
from jax import lax
from jax.experimental import pallas as pl
from jax.experimental.pallas import tpu as pltpu
from jax.sharding import PartitionSpec as P

SEGS = 8
BR = 256
PIECES = 16
F32 = jnp.float32
BF16 = jnp.bfloat16
MIB = 1 << 20


def mm(a, b):
    return lax.dot_general(a, b, (((1,), (0,)), ((), ())), preferred_element_type=F32)


def mm_t(a, b):
    return lax.dot_general(a, b, (((1,), (1,)), ((), ())), preferred_element_type=F32)


def norm_parts(v):
    mean = jnp.mean(v, axis=-1, keepdims=True)
    centred = v - mean
    var = jnp.mean(centred * centred, axis=-1, keepdims=True)
    rstd = lax.rsqrt(var + 1e-5)
    return centred * rstd, rstd


def norm_back(da, xhat, rstd, gain):
    dxhat = da * gain
    m1 = jnp.mean(dxhat, axis=-1, keepdims=True)
    m2 = jnp.mean(dxhat * xhat, axis=-1, keepdims=True)
    return rstd * (dxhat - m1 - xhat * m2)


def row_sums(v):
    r, n = v.shape
    return jnp.sum(v.reshape(r // 8, 8, n), axis=0)


def swap_halves(u):
    lane = lax.broadcasted_iota(jnp.int32, u.shape, 1)
    return jnp.where((lane & 63) < 32, pltpu.roll(u, 96, 1), pltpu.roll(u, 32, 1))


def rope(u, cos, sin):
    out = []
    for g in range(u.shape[1] // 128):
        part = u[:, 128 * g : 128 * (g + 1)]
        out.append(part * cos + swap_halves(part) * sin)
    return jnp.concatenate(out, axis=1)


def rope_back(g_, cos, sin):
    out = []
    for g in range(g_.shape[1] // 128):
        part = g_[:, 128 * g : 128 * (g + 1)]
        out.append(part * cos + swap_halves(part * sin))
    return jnp.concatenate(out, axis=1)


def softplus(z):
    return jnp.maximum(z, 0.0) + jnp.log1p(jnp.exp(-jnp.abs(z)))


def head_masks(nf):
    row = lax.broadcasted_iota(jnp.int32, (nf, 128), 0) // 32
    lane = lax.broadcasted_iota(jnp.int32, (nf, 128), 1) // 64
    own = (row & 1) == lane
    masks = [jnp.where(own & (row // 2 == g), 1.0, 0.0).astype(F32) for g in range(nf // 64)]
    other = jnp.where(own, 0.0, 1.0).astype(F32)
    return masks, other


def expand(state, masks):
    turned = pltpu.roll(state, 64, 1)
    parts = [state * m for m in masks] + [turned * m for m in masks]
    return jnp.concatenate(parts, axis=1).astype(BF16)


def fold(wide, masks):
    n = len(masks)
    first = sum(wide[:, 128 * g : 128 * (g + 1)] * m for g, m in enumerate(masks))
    second = sum(wide[:, 128 * (n + g) : 128 * (n + g + 1)] * m for g, m in enumerate(masks))
    return first + pltpu.roll(second, 64, 1)


def store_turned(value, scratch, out_ref, order):
    d = value.shape[1]
    step = d // PIECES
    scratch[...] = jnp.transpose(value).astype(BF16)
    for p in range(PIECES):
        at = pl.multiple_of(order[p] * step, 16)
        out_ref[p * step : (p + 1) * step, :] = scratch[pl.ds(at, step), :]


S_DOC, S_QUARTER, S_LOW = 16, 17, 18


def doc_range(sp, i, nb):
    return sp[S_LOW + i], sp[S_LOW + nb + i] + 1


def assemble_kernel(sp, a, b, c, d, out):
    for k, ref in enumerate((a, b, c, d)):

        @pl.when(pl.program_id(0) == k)
        def _(ref=ref):
            out[...] = ref[...]


def turn_kernel(sp, x, out, scratch):
    store_turned(x[...].astype(F32), scratch, out, sp)


def project(a1, w, cos, sin, om_hi, om_lo, seg_row, sp, pq_o, pk_o, v_o, st_o, i, nb):
    half = w.shape[1] // 3
    nf = om_hi.shape[1]
    c, s = cos[...], sin[...]

    def feature(u):
        turned = rope(u, c, s)
        hi = turned.astype(BF16)
        lo = (turned - hi.astype(F32)).astype(BF16)
        return softplus(mm(hi, om_hi[...]) + mm(lo, om_hi[...]) + mm(hi, om_lo[...]))

    pq_o[...] = feature(mm(a1, w[:, :half]))
    pk = feature(mm(a1, w[:, half : 2 * half]))
    pk_o[...] = pk
    vals = mm(a1, w[:, 2 * half :]).astype(BF16)
    v_o[...] = vals
    masks, other = head_masks(nf)
    pk_t = jnp.transpose(pk)
    right = jnp.concatenate([vals, jnp.ones((vals.shape[0], 128), BF16)], axis=1)

    @pl.when(i == 0)
    def _():
        st_o[...] = jnp.zeros_like(st_o)

    lo_doc, hi_doc = doc_range(sp, i, nb)

    def body(doc, carry):
        left = jnp.where(seg_row[...] == doc, pk_t, 0.0).astype(BF16)
        wide = mm(left, right)
        part = wide[:, half:] * other
        for g, m in enumerate(masks):
            part = part + wide[:, 128 * g : 128 * (g + 1)] * m
        st_o[doc] = st_o[doc] + part
        return carry

    lax.fori_loop(lo_doc, hi_doc, body, 0)


def qkv_first_kernel(
    sp, x, g1, w, cos, sin, om_hi, om_lo, seg_row, a1_o, a1t_o, pq_o, pk_o, v_o, st_o, scratch, *, nb
):
    i = pl.program_id(0)
    xhat, _ = norm_parts(x[...].astype(F32))
    a1f = xhat * g1[...]
    a1 = a1f.astype(BF16)
    a1_o[...] = a1
    store_turned(a1f, scratch, a1t_o, sp)
    project(a1, w, cos, sin, om_hi, om_lo, seg_row, sp, pq_o, pk_o, v_o, st_o, i, nb)


def qkv_second_kernel(
    sp, a1, w, cos, sin, om_hi, om_lo, seg_row, pq_o, pk_o, v_o, st_o, *, nb
):
    i = pl.program_id(0)
    project(a1[...], w, cos, sin, om_hi, om_lo, seg_row, sp, pq_o, pk_o, v_o, st_o, i, nb)


def expand_all(sp, st, other_half, wide, nb):
    masks, _ = head_masks(st.shape[1])

    def body(doc, carry):
        share = jnp.where(doc == sp[S_DOC], 1.0, 0.0)
        wide[doc] = expand(st[doc] + other_half[...] * share, masks)
        return carry

    lax.fori_loop(sp[S_LOW], sp[S_LOW + 2 * nb - 1] + 1, body, 0)


def attend_kernel(
    sp, x, g2, seg_col, pq_l, pq_r, st_l, st_r, ex_l, ex_r, wo_l, wo_r,
    at_l, at_r, x2_o, a2_o, a2t_o, wide_l, wide_r, acc, scratch, *, nb,
):
    i = pl.program_id(0)

    @pl.when(i == 0)
    def _():
        expand_all(sp, st_l, ex_l, wide_l, nb)
        expand_all(sp, st_r, ex_r, wide_r, nb)

    lo_doc, hi_doc = doc_range(sp, i, nb)
    x2 = x[...].astype(F32)
    for pq, wide, wo, at in ((pq_l, wide_l, wo_l, at_l), (pq_r, wide_r, wo_r, at_r)):
        half = wo.shape[0]
        pqb = pq[...].astype(BF16)

        def body(doc, carry, pqb=pqb, wide=wide, half=half):
            nd = mm(pqb, wide[doc])
            acc[...] = jnp.where(seg_col[...] == doc, nd[:, :half] / nd[:, half:], acc[...])
            return carry

        lax.fori_loop(lo_doc, hi_doc, body, 0)
        attn = acc[...].astype(BF16)
        at[...] = attn
        x2 = x2 + mm(attn, wo[...])
    x2_o[...] = x2
    xhat, _ = norm_parts(x2)
    a2f = xhat * g2[...]
    a2_o[...] = a2f.astype(BF16)
    store_turned(a2f, scratch, a2t_o, sp)


GC = 0.7978845608028654


def mlp_kernel(
    a2, a2t, dy, dyt, wu, wd, out_in, da_in,
    out_o, da_o, gu_o, gd_o, hact, dhp, acc_o, acc_d, *, last, has_da,
):
    j = pl.program_id(0)
    nj = pl.num_programs(0)
    rows = a2.shape[0]

    def chunk(r, carry):
        rs = pl.ds(pl.multiple_of(r * BR, BR), BR)
        h = mm(a2[rs, :], wu[...])
        d = mm_t(dy[rs, :], wd[...])
        sq = h * h
        t = jnp.tanh(h * (GC + (GC * 0.044715) * sq))
        half1 = 0.5 + 0.5 * t
        act = (h * half1).astype(BF16)
        slope = half1 + (0.5 * h) * (1.0 - t * t) * (GC + (3 * GC * 0.044715) * sq)
        back = (d * slope).astype(BF16)
        hact[rs, :] = act
        dhp[rs, :] = back
        po = mm(act, wd[...])
        pd = mm_t(back, wu[...])

        @pl.when(j == 0)
        def _():
            acc_o[rs, :] = out_in[rs, :] + po
            if has_da:
                acc_d[rs, :] = da_in[rs, :] + pd
            else:
                acc_d[rs, :] = pd

        @pl.when(j > 0)
        def _():
            acc_o[rs, :] = acc_o[rs, :] + po
            acc_d[rs, :] = acc_d[rs, :] + pd

        @pl.when(j == nj - 1)
        def _():
            out_o[rs, :] = acc_o[rs, :].astype(out_o.dtype)
            da_o[rs, :] = acc_d[rs, :]

        return carry

    lax.fori_loop(0, rows // BR, chunk, 0)

    def grads(r, carry):
        rs = pl.ds(pl.multiple_of(r * BR, BR), BR)
        gu_o[rs, :] = mm(a2t[rs, :], dhp[...]).astype(BF16)
        gd_o[rs, :] = mm(dyt[rs, :], hact[...]).astype(BF16)
        return carry

    lax.fori_loop(0, a2t.shape[0] // BR, grads, 0)


def back_one_kernel(
    sp, x2, da2, dy, g2, seg_col, seg_row, cos, sin, om, pq_l, pq_r, st_l, st_r, ex_l, ex_r, wo_l, wo_r,
    dx2_o, dbt_o, gain_o, dq_l, dq_r, dst_l, dst_r, wide_l, wide_r, attn_s, inv_s, dpq_s, scratch, *, nb,
):
    i = pl.program_id(0)

    @pl.when(i == 0)
    def _():
        expand_all(sp, st_l, ex_l, wide_l, nb)
        expand_all(sp, st_r, ex_r, wide_r, nb)
        gain_o[...] = jnp.zeros_like(gain_o)
        dst_l[...] = jnp.zeros_like(dst_l)
        dst_r[...] = jnp.zeros_like(dst_r)

    xhat, rstd = norm_parts(x2[...])
    da = da2[...]
    gain_o[...] += row_sums(da * xhat)
    dx2 = dy[...].astype(F32) + norm_back(da, xhat, rstd, g2[...])
    dx2_o[...] = dx2
    datt = dx2.astype(BF16)
    store_turned(dx2, scratch, dbt_o, sp)
    lo_doc, hi_doc = doc_range(sp, i, nb)
    for pq, wide, wo, dq, dst in (
        (pq_l, wide_l, wo_l, dq_l, dst_l),
        (pq_r, wide_r, wo_r, dq_r, dst_r),
    ):
        half = wo.shape[0]
        masks, _ = head_masks(pq.shape[1])
        pqf = pq[...]
        pqb = pqf.astype(BF16)

        def first(doc, carry, pqb=pqb, wide=wide, half=half):
            nd = mm(pqb, wide[doc])
            here = seg_col[...] == doc
            inv = 1.0 / nd[:, half:]
            attn_s[...] = jnp.where(here, nd[:, :half] * inv, attn_s[...])
            inv_s[...] = jnp.where(here, inv, inv_s[...])
            return carry

        lax.fori_loop(lo_doc, hi_doc, first, 0)
        dnum = mm_t(datt, wo[...]) * inv_s[...]
        both = jnp.concatenate([dnum, -dnum * attn_s[...]], axis=1).astype(BF16)
        pq_t = jnp.transpose(pqf)

        def second(doc, carry, both=both, pq_t=pq_t, wide=wide, dst=dst, masks=masks):
            dpq_s[...] = jnp.where(seg_col[...] == doc, mm_t(both, wide[doc]), dpq_s[...])
            left = jnp.where(seg_row[...] == doc, pq_t, 0.0).astype(BF16)
            dst[doc] = dst[doc] + fold(mm(left, both), masks)
            return carry

        lax.fori_loop(lo_doc, hi_doc, second, 0)
        dz = (dpq_s[...] * (1.0 - jnp.exp(-pqf))).astype(BF16)
        dq[...] = rope_back(mm_t(dz, om[...]), cos[...], sin[...]).astype(BF16)


def back_two_kernel(
    sp, seg_col, cos, sin, om, pk_l, pk_r, v_l, v_r, dst_l, dst_r, ex_l, ex_r,
    dk_l, dv_l, dk_r, dv_r, wide_l, wide_r, dpk_s, dv_s, *, nb,
):
    i = pl.program_id(0)

    @pl.when(i == 0)
    def _():
        expand_all(sp, dst_l, ex_l, wide_l, nb)
        expand_all(sp, dst_r, ex_r, wide_r, nb)

    lo_doc, hi_doc = doc_range(sp, i, nb)
    for pk, v, wide, dk, dv in (
        (pk_l, v_l, wide_l, dk_l, dv_l),
        (pk_r, v_r, wide_r, dk_r, dv_r),
    ):
        half = v.shape[1]
        pkf = pk[...]
        pkb = pkf.astype(BF16)
        right = jnp.concatenate([v[...], jnp.ones(v.shape, BF16)], axis=1)

        def body(doc, carry, pkb=pkb, right=right, wide=wide, half=half):
            here = seg_col[...] == doc
            dpk_s[...] = jnp.where(here, mm_t(right, wide[doc]), dpk_s[...])
            dv_s[...] = jnp.where(here, mm(pkb, wide[doc, :, :half]), dv_s[...])
            return carry

        lax.fori_loop(lo_doc, hi_doc, body, 0)
        dv[...] = dv_s[...].astype(BF16)
        dz = (dpk_s[...] * (1.0 - jnp.exp(-pkf))).astype(BF16)
        dk[...] = rope_back(mm_t(dz, om[...]), cos[...], sin[...]).astype(BF16)


def input_kernel(x, g1, dx2, dq_l, dk_l, dv_l, dq_r, dk_r, dv_r, w_l, w_r, dx_o, gain_o):
    i = pl.program_id(0)
    half = w_l.shape[1] // 3

    @pl.when(i == 0)
    def _():
        gain_o[...] = jnp.zeros_like(gain_o)

    da = None
    for w, parts in ((w_l, (dq_l, dk_l, dv_l)), (w_r, (dq_r, dk_r, dv_r))):
        for k, part in enumerate(parts):
            term = mm_t(part[...], w[:, half * k : half * (k + 1)])
            da = term if da is None else da + term
    xhat, rstd = norm_parts(x[...].astype(F32))
    gain_o[...] += row_sums(da * xhat)
    dx_o[...] = dx2[...] + norm_back(da, xhat, rstd, g1[...])


def whole(shape):
    zeros = (0,) * len(shape)
    return pl.BlockSpec(tuple(shape), lambda i, *_: zeros)


def by_rows(shape, br=BR):
    return pl.BlockSpec((br, shape[1]), lambda i, *_: (i, 0))


def by_cols(shape, bc=BR):
    return pl.BlockSpec((shape[0], bc), lambda i, *_: (0, i))


def call(kernel, grid, scalars, ins, outs, scratch, flops, vmem=56):
    args = [a for a, _ in ins]
    moved = sum(a.size * a.dtype.itemsize for a in args)
    for shape, dtype, _ in outs:
        size = 1
        for n in shape:
            size *= n
        moved += size * jnp.dtype(dtype).itemsize
    prefetch = [] if scalars is None else [scalars]
    return pl.pallas_call(
        kernel,
        out_shape=[jax.ShapeDtypeStruct(s, d) for s, d, _ in outs],
        grid_spec=pltpu.PrefetchScalarGridSpec(
            num_scalar_prefetch=len(prefetch),
            grid=grid,
            in_specs=[s for _, s in ins],
            out_specs=[s for _, _, s in outs],
            scratch_shapes=scratch,
        ),
        compiler_params=pltpu.CompilerParams(
            dimension_semantics=("arbitrary",) * len(grid), vmem_limit_bytes=vmem * MIB
        ),
        cost_estimate=pl.CostEstimate(flops=flops, bytes_accessed=moved, transcendentals=0),
    )(*prefetch, *args)


class Links:
    def __init__(self, n_dp, n_mp):
        self.n_dp, self.n_mp = n_dp, n_mp
        self.fine = n_dp // PIECES

    def dp_xor(self, v, bits):
        pairs = [(d, d ^ bits) for d in range(self.n_dp)]
        return lax.ppermute(v, "dp", pairs)

    def mp_swap(self, v):
        return lax.ppermute(v, "mp", [(m, m ^ 1) for m in range(self.n_mp)])


def add(a, b):
    return (a.astype(F32) + b.astype(F32)).astype(BF16)


def gather_other(links, w, quarter):
    n = w.shape[0] // 4
    own = lax.dynamic_slice_in_dim(w, quarter * n, n, 0)
    first = links.mp_swap(own)
    second = links.dp_xor(first, 2)
    third = links.dp_xor(first, 1)
    fourth = links.dp_xor(second, 1)
    return first, third, second, fourth


def assemble(pieces, scalars):
    n, cols = pieces[0].shape
    out = pl.BlockSpec((n, cols), lambda i, sp: (sp[S_QUARTER] ^ i, 0))
    return call(
        assemble_kernel, (4,), scalars, [(p, whole(p.shape)) for p in pieces],
        [((4 * n, cols), BF16, out)], [], 0,
    )[0]


def finish(links, part):
    fine = links.fine
    step = part.shape[0] // 4
    total = part[:step].astype(F32)
    for r, bits in ((1, 8), (2, 4), (3, 12)):
        total = total + links.dp_xor(part[r * step : (r + 1) * step], bits * fine).astype(F32)
    bit = fine // 2
    me = lax.axis_index("dp")
    while bit:
        half = total.shape[0] // 2
        upper = (me // bit) % 2
        send = lax.dynamic_slice_in_dim(total, (1 - upper) * half, half, 0)
        keep = lax.dynamic_slice_in_dim(total, upper * half, half, 0)
        total = keep + links.dp_xor(send, bit)
        bit //= 2
    return total


def reduce_core(links, g):
    half = g.shape[0] // 2
    return add(g[:half], links.dp_xor(g[half:], links.fine))


def reduce_x(links, g):
    half = g.shape[0] // 2
    return add(g[:half], links.dp_xor(g[half:], 2 * links.fine))


def reduce_rows_first(links, mine, other):
    mine, other = reduce_core(links, mine), reduce_core(links, other)
    both = add(mine, links.mp_swap(other))
    return finish(links, reduce_x(links, both))


def reduce_cols_first(links, mine, other):
    mine, other = reduce_core(links, mine), reduce_core(links, other)
    mine, other = reduce_x(links, mine), reduce_x(links, other)
    return finish(links, add(mine, links.mp_swap(other)))


def sum_everywhere(links, v):
    bit = 1
    while bit < links.n_dp:
        v = v + links.dp_xor(v, bit)
        bit *= 2
    return v + links.mp_swap(v)


def rotary_tables(first, rows, head_size):
    places = first + jnp.arange(rows)
    rates = 10000.0 ** (-(jnp.arange(head_size // 2).astype(F32) * 2.0 / head_size))
    angles = places.astype(F32)[:, None] * rates[None, :]
    cos, sin = jnp.cos(angles), jnp.sin(angles)
    return jnp.concatenate([cos] * 4, 1), jnp.concatenate([-sin, sin, -sin, sin], 1)


def block_omega(omega, heads):
    hd, feat = omega.shape
    scaled = omega * hd ** (-0.25)
    eye = jnp.eye(heads, dtype=F32)
    wide = (eye[:, None, :, None] * scaled[None, :, None, :]).reshape(heads * hd, heads * feat)
    hi = wide.astype(BF16)
    lo = (wide - hi.astype(F32)).astype(BF16)
    return hi, lo


def on_device(
    n_dp, n_mp, inputs, seg_ids, omega, norm1_gain, qkv_weight, out_weight, norm2_gain, up_weight, down_weight, out_grad
):
    links = Links(n_dp, n_mp)
    x, dy = inputs[0], out_grad[0]
    rows, width = x.shape
    nb = rows // BR
    dp, mp = lax.axis_index("dp"), lax.axis_index("mp")
    quarter = dp % 4
    half = out_weight.shape[0]
    heads = half // omega.shape[0]
    nf = heads * omega.shape[1]
    ff = up_weight.shape[1]

    wq_mine = qkv_weight.reshape(width, -1)
    wq_pieces = gather_other(links, wq_mine, quarter)
    wo_pieces = gather_other(links, out_weight, quarter)
    wu_pieces = gather_other(links, up_weight, quarter)
    wd_pieces = gather_other(links, down_weight, quarter)

    seg_all = seg_ids[0]
    seg = lax.dynamic_slice_in_dim(seg_all, mp * rows, rows, 0)
    shared = jnp.where(seg_all[rows - 1] == seg_all[rows], seg_all[rows], -1)
    coarse = dp // links.fine
    order = [int(format(p, "04b")[::-1], 2) for p in range(PIECES)]
    by_block = seg.reshape(nb, BR)
    scalars = jnp.concatenate(
        [jnp.array(order, jnp.int32) ^ coarse, jnp.stack([shared, quarter]), by_block[:, 0], by_block[:, -1]]
    ).astype(jnp.int32)
    seg_col, seg_row = seg.reshape(rows, 1), seg.reshape(1, rows)
    cos, sin = rotary_tables(mp * rows, rows, omega.shape[0])
    om_hi, om_lo = block_omega(omega, heads)
    g1, g2 = norm1_gain.reshape(1, -1), norm2_gain.reshape(1, -1)
    turn_scratch = pltpu.VMEM((width, BR), BF16)
    turned_out = ((width, rows), BF16, by_cols((width, rows)))

    def rowed(n, dtype):
        return ((rows, n), dtype, by_rows((rows, n)))

    def ws(a):
        return (a, whole(a.shape))

    def rs(a):
        return (a, by_rows(a.shape))

    def cs(a):
        return (a, by_cols(a.shape))

    state_out = ((SEGS, nf, 128), F32, whole((SEGS, nf, 128)))
    side = [rs(cos), rs(sin), ws(om_hi), ws(om_lo), cs(seg_row)]
    one_flops = 2 * rows * width * 3 * half
    a1, a1t, pq_l, pk_l, v_l, st_l = call(
        functools.partial(qkv_first_kernel, nb=nb), (nb,), scalars,
        [rs(x), ws(g1), ws(wq_mine)] + side,
        [rowed(width, BF16), turned_out, rowed(nf, F32), rowed(nf, F32), rowed(half, BF16), state_out],
        [turn_scratch], one_flops,
    )
    dyt = call(turn_kernel, (nb,), scalars, [rs(dy)], [turned_out], [turn_scratch], 0)[0]

    def exchange(state):
        return links.mp_swap(lax.dynamic_index_in_dim(state, seg_all[rows - 1], 0, keepdims=False))

    ex_r = exchange(st_l)
    wq_other = assemble(wq_pieces, scalars)
    pq_r, pk_r, v_r, st_r = call(
        functools.partial(qkv_second_kernel, nb=nb), (nb,), scalars,
        [rs(a1), ws(wq_other)] + side,
        [rowed(nf, F32), rowed(nf, F32), rowed(half, BF16), state_out],
        [], one_flops,
    )
    ex_l = exchange(st_r)
    wo_other = assemble(wo_pieces, scalars)
    wide_scratch = pltpu.VMEM((SEGS, nf, 2 * half), BF16)
    at_l, at_r, x2, a2, a2t = call(
        functools.partial(attend_kernel, nb=nb), (nb,), scalars,
        [rs(x), ws(g2), rs(seg_col), rs(pq_l), rs(pq_r), ws(st_l), ws(st_r), ws(ex_l), ws(ex_r),
         ws(out_weight), ws(wo_other)],
        [rowed(half, BF16), rowed(half, BF16), rowed(width, F32), rowed(width, BF16), turned_out],
        [wide_scratch, wide_scratch, pltpu.VMEM((BR, half), F32), turn_scratch],
        2 * rows * width * 2 * half,
    )

    bf = 512
    wu_other = assemble(wu_pieces, scalars)
    wd_other = assemble(wd_pieces, scalars)

    def mlp(wu, wd, out_in, da_in, last):
        has_da = da_in is not None
        da_arg = [ws(da_in)] if has_da else []
        kernel = functools.partial(mlp_kernel, last=last, has_da=has_da)
        if not has_da:

            def kernel(a2_, a2t_, dy_, dyt_, wu_, wd_, oi_, *rest):
                return mlp_kernel(a2_, a2t_, dy_, dyt_, wu_, wd_, oi_, None, *rest, last=last, has_da=False)

        return call(
            kernel, (ff // bf,), None,
            [ws(a2), ws(a2t), ws(dy), ws(dyt), (wu, by_cols(wu.shape, bf)), (wd, by_rows(wd.shape, bf)), ws(out_in)]
            + da_arg,
            [((rows, width), BF16 if last else F32, whole((rows, width))), ((rows, width), F32, whole((rows, width))),
             ((width, ff), BF16, by_cols((width, ff), bf)), ((width, ff), BF16, by_cols((width, ff), bf))],
            [pltpu.VMEM((rows, bf), BF16), pltpu.VMEM((rows, bf), BF16),
             pltpu.VMEM((rows, width), F32), pltpu.VMEM((rows, width), F32)],
            6 * 2 * rows * width * ff,
        )

    part_out, part_da, gu_r, gd_r = mlp(wu_other, wd_other, x2, None, False)
    output, da2, gu_l, gd_l = mlp(up_weight, down_weight, part_out, part_da, True)
    down_sum = jnp.transpose(reduce_rows_first(links, gd_l, gd_r))
    up_sum = reduce_cols_first(links, gu_l, gu_r)

    gain8 = ((8, width), F32, whole((8, width)))
    dx2, dbt, gain2, dq_l, dq_r, dst_l, dst_r = call(
        functools.partial(back_one_kernel, nb=nb), (nb,), scalars,
        [rs(x2), rs(da2), rs(dy), ws(g2), rs(seg_col), cs(seg_row), rs(cos), rs(sin), ws(om_hi),
         rs(pq_l), rs(pq_r), ws(st_l), ws(st_r), ws(ex_l), ws(ex_r), ws(out_weight), ws(wo_other)],
        [rowed(width, F32), turned_out, gain8, rowed(half, BF16), rowed(half, BF16), state_out, state_out],
        [wide_scratch, wide_scratch, pltpu.VMEM((BR, half), F32), pltpu.VMEM((BR, half), F32),
         pltpu.VMEM((BR, nf), F32), turn_scratch],
        2 * rows * width * 2 * half,
    )
    dex_r, dex_l = exchange(dst_l), exchange(dst_r)

    def outer(left, right):
        return lax.dot_general(left, right, (((1,), (0,)), ((), ())), preferred_element_type=F32).astype(BF16)

    out_sum = jnp.transpose(reduce_rows_first(links, outer(dbt, at_l), outer(dbt, at_r)))
    gq_l, gq_r = outer(a1t, dq_l), outer(a1t, dq_r)
    q_sum = reduce_cols_first(links, gq_l, gq_r)
    dk_l, dv_l, dk_r, dv_r = call(
        functools.partial(back_two_kernel, nb=nb), (nb,), scalars,
        [rs(seg_col), rs(cos), rs(sin), ws(om_hi), rs(pk_l), rs(pk_r), rs(v_l), rs(v_r),
         ws(dst_l), ws(dst_r), ws(dex_l), ws(dex_r)],
        [rowed(half, BF16)] * 4,
        [wide_scratch, wide_scratch, pltpu.VMEM((BR, nf), F32), pltpu.VMEM((BR, half), F32)],
        2 * rows * width * half,
    )
    k_sum = reduce_cols_first(links, outer(a1t, dk_l), outer(a1t, dk_r))
    v_sum = reduce_rows_first(links, outer(a1t, dv_l), outer(a1t, dv_r))
    input_grad, gain1 = call(
        input_kernel, (nb,), None,
        [rs(x), ws(g1), rs(dx2), rs(dq_l), rs(dk_l), rs(dv_l), rs(dq_r), rs(dk_r), rs(dv_r), ws(wq_mine), ws(wq_other)],
        [rowed(width, F32), gain8], [], 2 * one_flops,
    )
    gains = sum_everywhere(links, jnp.stack([gain1.sum(0), gain2.sum(0)]))
    share = width // (n_dp * n_mp)
    gains = lax.dynamic_slice_in_dim(gains, (dp * n_mp + mp) * share, share, 1)
    qkv_sum = jnp.stack([q_sum, k_sum, v_sum], axis=1)
    return (output[None], input_grad[None], gains[0], qkv_sum, out_sum, gains[1], up_sum, down_sum)


def solution(mesh):
    n_dp, n_mp = mesh.shape["dp"], mesh.shape["mp"]
    return jax.shard_map(
        functools.partial(on_device, n_dp, n_mp),
        mesh=mesh,
        in_specs=(
            P("dp", "mp", None),
            P("dp", None),
            P(),
            P(),
            P(None, None, "mp"),
            P("mp", None),
            P(),
            P(None, "mp"),
            P("mp", None),
            P("dp", "mp", None),
        ),
        out_specs=(
            P("dp", "mp", None),
            P("dp", "mp", None),
            P(("dp", "mp")),
            P("dp", None, "mp"),
            P("mp", "dp"),
            P(("dp", "mp")),
            P("dp", "mp"),
            P("mp", "dp"),
        ),
        check_vma=False,
    )
```

```python
import functools

import jax
import jax.numpy as jnp
import numpy as np
from jax import lax
from jax.experimental import pallas as pl
from jax.experimental.pallas import tpu as pltpu
from jax.sharding import PartitionSpec as P

SEGS = 8
BR = 512
BF = 768
PIECES = 16
F32 = jnp.float32
BF16 = jnp.bfloat16
MIB = 1 << 20
ORDER = [int(format(p, "04b")[::-1], 2) for p in range(PIECES)]

S_DOC, S_QUARTER, S_COARSE, S_MP = 9, 10, 11, 12


def mm(a, b):
    return lax.dot_general(a, b, (((1,), (0,)), ((), ())), preferred_element_type=F32)


def mm_t(a, b):
    return lax.dot_general(a, b, (((1,), (1,)), ((), ())), preferred_element_type=F32)


def t_mm(a, b):
    return lax.dot_general(a, b, (((0,), (0,)), ((), ())), preferred_element_type=F32)


def norm_parts(v):
    mean = jnp.mean(v, axis=-1, keepdims=True)
    centred = v - mean
    var = jnp.mean(centred * centred, axis=-1, keepdims=True)
    rstd = lax.rsqrt(var + 1e-5)
    return centred * rstd, rstd


def norm_back(da, xhat, rstd, gain):
    dxhat = da * gain
    m1 = jnp.mean(dxhat, axis=-1, keepdims=True)
    m2 = jnp.mean(dxhat * xhat, axis=-1, keepdims=True)
    return rstd * (dxhat - m1 - xhat * m2)


def row_sums(v):
    r, n = v.shape
    return jnp.sum(v.reshape(r // 8, 8, n), axis=0)


def lanes(v, g):
    return v[:, 128 * g : 128 * (g + 1)]


def swap_halves(u):
    lane = lax.broadcasted_iota(jnp.int32, u.shape, 1)
    return jnp.where((lane & 63) < 32, pltpu.roll(u, 96, 1), pltpu.roll(u, 32, 1))


def softplus(z):
    e = jnp.exp(-jnp.abs(z))
    series = e * (1.0 + e * (e * (1.0 / 3.0) - 0.5))
    return jnp.maximum(z, 0.0) + jnp.where(e < 0.01, series, jnp.log(1.0 + e))


def gate(p):
    return jnp.where(p < 0.01, p * (1.0 + p * (p * (1.0 / 6.0) - 0.5)), 1.0 - jnp.exp(-p))


def omega_pair(om):
    rows = jnp.concatenate([om, om], axis=0)
    wide = jnp.concatenate([rows, rows], axis=1)
    r = lax.broadcasted_iota(jnp.int32, wide.shape, 0) // 64
    c = lax.broadcasted_iota(jnp.int32, wide.shape, 1) // 32
    return jnp.where(r == c, wide, 0.0)


def omega_split(om):
    pair = omega_pair(om)
    hi = pair.astype(BF16)
    lo = (pair - hi.astype(F32)).astype(BF16)
    top = jnp.concatenate([hi, hi, lo, lo], axis=1)
    bottom = jnp.concatenate([hi, hi, jnp.zeros_like(hi), jnp.zeros_like(hi)], axis=1)
    return jnp.concatenate([top, bottom], axis=0)


def omega_back(om):
    pair = omega_pair(om).astype(BF16)
    return jnp.concatenate([pair, jnp.zeros_like(pair)], axis=1)


def doc_mask(sp, i):
    parts = []
    for t in range(SEGS // 2):
        lane = lax.broadcasted_iota(jnp.int32, (BR, 128), 1) < 64
        row = lax.broadcasted_iota(jnp.int32, (BR, 128), 0) + i * BR
        low = jnp.where(lane, sp[2 * t], sp[2 * t + 1])
        high = jnp.where(lane, sp[2 * t + 1], sp[2 * t + 2])
        parts.append(jnp.where((row >= low) & (row < high), 1.0, 0.0).astype(F32))
    return jnp.concatenate(parts, axis=1)


def spread(feat, mask):
    return jnp.concatenate([feat] * (SEGS // 2), axis=1) * mask


def collect(wide, mask):
    masked = wide * mask
    total = sum(lanes(masked, t) for t in range(SEGS // 2))
    return total + pltpu.roll(total, 64, 1)


def own_lanes(n):
    row = lax.broadcasted_iota(jnp.int32, (n, 128), 0) // 32
    lane = lax.broadcasted_iota(jnp.int32, (n, 128), 1) // 64
    return jnp.where((row & 1) == lane, 1.0, 0.0).astype(F32)


def expand(state, own):
    return jnp.concatenate([state * own, pltpu.roll(state, 64, 1) * own], axis=1).astype(BF16)


def store_pieces(value, scratch, keep_ref, send_ref, sp):
    d = value.shape[0]
    step = d // PIECES
    scratch[...] = value.astype(BF16)
    for p in range(PIECES):
        at = pl.multiple_of((ORDER[p] ^ sp[S_COARSE]) * step, 16)
        ref = keep_ref if p < PIECES // 2 else send_ref
        q = p % (PIECES // 2)
        ref[q * step : (q + 1) * step, :] = scratch[pl.ds(at, step), :]


def put_quarters(sp, pieces, out):
    n = pieces[0].shape[0]
    for k, piece in enumerate(pieces):
        out[pl.ds(pl.multiple_of((sp[S_QUARTER] ^ k) * n, 16), n), :] = piece[...]


def project(sp, i, a1, w, cos, sin, om, pq_o, pk_o, v_o, st_o, sm_o):
    c, s = cos[...], sin[...]
    split = omega_split(om[...])
    mask = doc_mask(sp, i).astype(BF16)
    ones = jnp.ones((BR, 128), BF16)

    def feature(u):
        turned = u * c + swap_halves(u) * s
        hi = turned.astype(BF16)
        lo = (turned - hi.astype(F32)).astype(BF16)
        z = mm(jnp.concatenate([hi, lo], axis=1), split)
        return softplus(lanes(z, 0) + lanes(z, 1)).astype(BF16)

    @pl.when(i == 0)
    def _():
        st_o[...] = jnp.zeros_like(st_o)

    q, k, v = mm(a1, w(0)), mm(a1, w(1)), mm(a1, w(2)).astype(BF16)
    v_o[...] = v
    own = own_lanes(64 * SEGS)
    for g in range(q.shape[1] // 128):
        pq_o[:, 128 * g : 128 * (g + 1)] = feature(lanes(q, g))
        pk = feature(lanes(k, g))
        pk_o[:, 128 * g : 128 * (g + 1)] = pk
        wide = t_mm(spread(pk, mask), jnp.concatenate([lanes(v, g), ones], axis=1))
        st_o[g] += lanes(wide, 0) * own + lanes(wide, 1) * (1.0 - own)

    @pl.when(i == pl.num_programs(0) - 1)
    def _():
        for g in range(st_o.shape[0]):
            sm_o[g] = st_o[g, pl.ds(pl.multiple_of(sp[S_DOC] * 64, 64), 64), :]


def qkv_first_kernel(sp, x, g1, w, cos, sin, om, a1_o, pq_o, pk_o, v_o, st_o, sm_o):
    xhat, _ = norm_parts(x[...].astype(F32))
    a1 = (xhat * g1[...]).astype(BF16)
    a1_o[...] = a1
    project(sp, pl.program_id(0), a1, lambda k: w[k], cos, sin, om, pq_o, pk_o, v_o, st_o, sm_o)


def qkv_second_kernel(sp, a1, w0, w1, w2, w3, cos, sin, om, pq_o, pk_o, v_o, st_o, sm_o, w_o):
    i = pl.program_id(0)

    @pl.when(i == 0)
    def _():
        n = w_o.shape[1] // 4
        for k in range(3):
            put_quarters(sp, [w.at[pl.ds(k * n, n), :] for w in (w0, w1, w2, w3)], w_o.at[k])

    project(sp, i, a1[...], lambda k: w_o[k], cos, sin, om, pq_o, pk_o, v_o, st_o, sm_o)


def expand_states(sp, states, extra, out, scratch):
    own = own_lanes(64 * SEGS)
    at = pl.ds(pl.multiple_of(sp[S_DOC] * 64, 64), 64)
    for g in range(states.shape[0]):
        scratch[...] = states[g]
        scratch[at, :] += extra[g]
        out[g] = expand(scratch[...], own)


def attend_kernel(
    sp, x, g2, pq_l, pq_r, st_l, st_r, ex_l, ex_r, wo_l, w0, w1, w2, w3,
    at_l, at_r, x2_o, a2_o, wo_o, wide_l, wide_r, scratch,
):
    i = pl.program_id(0)

    @pl.when(i == 0)
    def _():
        expand_states(sp, st_l, ex_l, wide_l, scratch)
        expand_states(sp, st_r, ex_r, wide_r, scratch)
        n, cols = wo_o.shape[0] // 4, w0.shape[1]
        first = w0.shape[0] - 2 * n
        for k in range(2):
            quarters = [w.at[pl.ds(first + k * n, n), :] for w in (w0, w1, w2, w3)]
            put_quarters(sp, quarters, wo_o.at[:, pl.ds(k * cols, cols)])

    mask = doc_mask(sp, i).astype(BF16)
    x2 = x[...].astype(F32)
    for pq, wide, wo, at in ((pq_l, wide_l, wo_l, at_l), (pq_r, wide_r, wo_o, at_r)):
        parts = []
        for g in range(wide.shape[0]):
            nd = mm(spread(lanes(pq, g), mask), wide[g])
            parts.append((lanes(nd, 0) / lanes(nd, 1)).astype(BF16))
        attn = jnp.concatenate(parts, axis=1)
        at[...] = attn
        x2 = x2 + mm(attn, wo[...])
    x2_o[...] = x2
    xhat, _ = norm_parts(x2)
    a2_o[...] = (xhat * g2[...]).astype(BF16)


GC = 0.7978845608028654
CHUNK = 512


def mlp_kernel(
    sp, a2, dy, wu, wd, w0, w1, w2, w3, out_in, *rest, last,
):
    if last:
        da_in, *rest = rest
    out_o, da_o, keep, send, wu_s, wd_s, hact, dhp, acc, perm = rest
    j = pl.program_id(0)
    nj = pl.num_programs(0)
    rows, width = a2.shape

    @pl.when(j == 0)
    def _():
        acc[...] = out_in[...]
        if last:
            da_o[...] = da_in[...]
        else:
            da_o[...] = jnp.zeros_like(da_o)
        wu_s[...] = wu[...]
        wd_s[...] = wd[...]

    @pl.when(j == 1)
    def _():
        n = w0.shape[0] // 2
        put_quarters(sp, [w.at[pl.ds(0, n), :] for w in (w0, w1, w2, w3)], wu_s)
        put_quarters(sp, [w.at[pl.ds(n, n), :] for w in (w0, w1, w2, w3)], wd_s)

    for r in range(rows // CHUNK):
        rs = pl.ds(r * CHUNK, CHUNK)
        h = mm(a2[rs, :], wu_s[...])
        d = mm_t(dy[rs, :], wd_s[...])
        sq = h * h
        t = jnp.tanh(h * (GC + (GC * 0.044715) * sq))
        half1 = 0.5 + 0.5 * t
        act = (h * half1).astype(BF16)
        slope = half1 + (0.5 * h) * (1.0 - t * t) * (GC + (3 * GC * 0.044715) * sq)
        back = (d * slope).astype(BF16)
        hact[rs, :] = act
        dhp[rs, :] = back
        acc[rs, :] += mm(act, wd_s[...])
        da_o[rs, :] += mm_t(back, wu_s[...])

    store_pieces(t_mm(a2[...], dhp[...]), perm, keep.at[0], send.at[0], sp)
    store_pieces(t_mm(dy[...], hact[...]), perm, keep.at[1], send.at[1], sp)

    @pl.when(j == nj - 1)
    def _():
        out_o[...] = acc[...].astype(out_o.dtype)


def back_one_kernel(
    sp, x2, da2, dy, g2, cos, sin, om, pq_l, pq_r, st_l, st_r, ex_l, ex_r, wo_l, wo_r,
    dx2_o, db_o, gain_o, dq_l, dq_r, dst_l, dst_r, dsm_l, dsm_r, wide_l, wide_r, scratch,
):
    i = pl.program_id(0)

    @pl.when(i == 0)
    def _():
        expand_states(sp, st_l, ex_l, wide_l, scratch)
        expand_states(sp, st_r, ex_r, wide_r, scratch)
        gain_o[...] = jnp.zeros_like(gain_o)
        dst_l[...] = jnp.zeros_like(dst_l)
        dst_r[...] = jnp.zeros_like(dst_r)

    xhat, rstd = norm_parts(x2[...])
    da = da2[...]
    gain_o[...] += row_sums(da * xhat)
    dx2 = dy[...].astype(F32) + norm_back(da, xhat, rstd, g2[...])
    dx2_o[...] = dx2
    datt = dx2.astype(BF16)
    db_o[...] = datt
    mask = doc_mask(sp, i)
    mask_b = mask.astype(BF16)
    own = own_lanes(64 * SEGS)
    back = omega_back(om[...])
    c, s = cos[...], sin[...]
    for pq, wide, wo, dq, dst in (
        (pq_l, wide_l, wo_l, dq_l, dst_l),
        (pq_r, wide_r, wo_r, dq_r, dst_r),
    ):
        dattn = mm_t(datt, wo[...])
        for g in range(wide.shape[0]):
            feat = lanes(pq, g)
            sprd = spread(feat, mask_b)
            nd = mm(sprd, wide[g])
            inv = 1.0 / lanes(nd, 1)
            attn = lanes(nd, 0) * inv
            dnum = lanes(dattn, g) * inv
            both = jnp.concatenate([dnum, -dnum * attn], axis=1).astype(BF16)
            dpq = collect(mm_t(both, wide[g]), mask)
            dwide = t_mm(sprd, both)
            dst[g] += lanes(dwide, 0) * own + pltpu.roll(lanes(dwide, 1) * own, 64, 1)
            dz = (dpq * gate(feat.astype(F32))).astype(BF16)
            dr = mm_t(dz, back)
            dq[:, 128 * g : 128 * (g + 1)] = (dr * c + swap_halves(dr * s)).astype(BF16)

    @pl.when(i == pl.num_programs(0) - 1)
    def _():
        at = pl.ds(pl.multiple_of(sp[S_DOC] * 64, 64), 64)
        for g in range(dst_l.shape[0]):
            dsm_l[g] = dst_l[g, at, :]
            dsm_r[g] = dst_r[g, at, :]


def back_two_kernel(
    sp, cos, sin, om, pk_l, pk_r, v_l, v_r, dst_l, dst_r, ex_l, ex_r,
    dk_l, dv_l, dk_r, dv_r, wide_l, wide_r, scratch,
):
    i = pl.program_id(0)

    @pl.when(i == 0)
    def _():
        expand_states(sp, dst_l, ex_l, wide_l, scratch)
        expand_states(sp, dst_r, ex_r, wide_r, scratch)

    mask = doc_mask(sp, i)
    mask_b = mask.astype(BF16)
    back = omega_back(om[...])
    c, s = cos[...], sin[...]
    ones = jnp.ones((BR, 128), BF16)
    for pk, v, wide, dk, dv in (
        (pk_l, v_l, wide_l, dk_l, dv_l),
        (pk_r, v_r, wide_r, dk_r, dv_r),
    ):
        for g in range(wide.shape[0]):
            feat = lanes(pk, g)
            dpk = collect(mm_t(jnp.concatenate([lanes(v, g), ones], axis=1), wide[g]), mask)
            dv[:, 128 * g : 128 * (g + 1)] = mm(spread(feat, mask_b), wide[g, :, :128]).astype(BF16)
            dz = (dpk * gate(feat.astype(F32))).astype(BF16)
            dr = mm_t(dz, back)
            dk[:, 128 * g : 128 * (g + 1)] = (dr * c + swap_halves(dr * s)).astype(BF16)


def outer_kernel(sp, left0, l0, r0, left1, l1, r1, keep, send, perm):
    for t, (left, sides) in enumerate(((left0, (l0, r0)), (left1, (l1, r1)))):
        for k, right in enumerate(sides):
            store_pieces(t_mm(left[...], right[...]), perm, keep.at[t, k], send.at[t, k], sp)


def input_kernel(x, g1, dx2, dq_l, dk_l, dv_l, dq_r, dk_r, dv_r, w_l, w_r, dx_o, gain_o):
    i = pl.program_id(0)

    @pl.when(i == 0)
    def _():
        gain_o[...] = jnp.zeros_like(gain_o)

    da = None
    for w, parts in ((w_l, (dq_l, dk_l, dv_l)), (w_r, (dq_r, dk_r, dv_r))):
        for k, part in enumerate(parts):
            term = mm_t(part[...], w[k])
            da = term if da is None else da + term
    xhat, rstd = norm_parts(x[...].astype(F32))
    gain_o[...] += row_sums(da * xhat)
    dx_o[...] = dx2[...] + norm_back(da, xhat, rstd, g1[...])


def whole(a, once=True):
    shape = tuple(a.shape)
    zeros = (0,) * len(shape)
    mode = dict(pipeline_mode=pl.Buffered(1)) if once else {}
    return pl.BlockSpec(shape, lambda i, *_: zeros, **mode)


def by_rows(a, br=BR):
    return pl.BlockSpec((br, a.shape[1]), lambda i, *_: (i, 0))


def call(kernel, grid, scalars, ins, outs, scratch, flops, vmem=50, into=None):
    args = [a for a, _ in ins]
    moved = sum(a.size * a.dtype.itemsize for a in args)
    moved += sum(s.size * s.dtype.itemsize for s, _ in outs)
    n_in = len(args) + 1
    extra = [] if into is None else [into]
    n_dep = len(extra)

    def body(*refs):
        return kernel(*refs[:n_in], *refs[n_in + n_dep :])

    return pl.pallas_call(
        body,
        out_shape=[s for s, _ in outs],
        grid_spec=pltpu.PrefetchScalarGridSpec(
            num_scalar_prefetch=1,
            grid=grid,
            in_specs=[s for _, s in ins] + [pl.BlockSpec(memory_space=pl.ANY)] * n_dep,
            out_specs=[s for _, s in outs],
            scratch_shapes=scratch,
        ),
        compiler_params=pltpu.CompilerParams(
            dimension_semantics=("arbitrary",) * len(grid), vmem_limit_bytes=vmem * MIB
        ),
        cost_estimate=pl.CostEstimate(flops=flops, bytes_accessed=moved, transcendentals=0),
            input_output_aliases={n_in: 0} if extra else {},
    )(scalars, *args, *extra)


def struct(shape, dtype):
    return jax.ShapeDtypeStruct(tuple(shape), dtype)


class Links:
    def __init__(self, n_dp, n_mp):
        self.n_dp, self.n_mp = n_dp, n_mp
        self.fine = n_dp // PIECES

    def dp_xor(self, v, bits):
        return lax.ppermute(v, "dp", [(d, d ^ bits) for d in range(self.n_dp)])

    def mp_swap(self, v):
        return lax.ppermute(v, "mp", [(m, m ^ 1) for m in range(self.n_mp)])


def add(a, b):
    return (a.astype(F32) + b.astype(F32)).astype(BF16)


def after(v, *deps):
    return lax.optimization_barrier((v,) + deps)[0]


class Sum:
    def __init__(self, links, keep, send):
        self.links, self.stage = links, 0
        self.keep, self.leave = (keep,), (send,)

    def launch(self):
        links, fine = self.links, self.links.fine
        x, y = (lambda v: links.dp_xor(v, 2 * fine)), links.mp_swap
        ways = (
            [lambda v: links.dp_xor(v, fine)],
            [x, y],
            [y, x],
            [lambda v: links.dp_xor(v, 4 * fine)],
            [lambda v: links.dp_xor(v, 8 * fine)],
        )[self.stage]
        self.flight = [way(v) for way, v in zip(ways, self.leave)]

    def land(self):
        stage, got = self.stage, self.flight
        self.stage, self.flight = stage + 1, []
        if stage == 0:
            (keep,), (got,) = self.keep, got
            half = keep.shape[2] // 2
            self.keep = (add(keep[0, :, :half], got[0, :, :half]), add(keep[1, 0], got[1, 0]))
            self.leave = (add(keep[0, :, half:], got[0, :, half:]), add(keep[1, 1], got[1, 1]))
        elif stage == 1:
            (a, b), (ga, gb) = self.keep, got
            half = b.shape[0] // 2
            self.keep = (add(a[0], ga[0]), add(b[:half], gb[:half]))
            self.leave = (add(a[1], ga[1]), add(b[half:], gb[half:]))
        elif stage == 2:
            (a, b), (ga, gb) = self.keep, got
            half = a.shape[0] // 2
            self.keep = (jnp.stack([add(a[:half], ga[:half]), add(b[:half], gb[:half])]),)
            self.leave = (jnp.stack([add(a[half:], ga[half:]), add(b[half:], gb[half:])]),)
        elif stage == 3:
            (a,), (ga,) = self.keep, got
            half = a.shape[1] // 2
            self.keep, self.leave = (add(a[:, :half], ga[:, :half]),), (add(a[:, half:], ga[:, half:]),)
        else:
            self.keep, self.leave = (self.keep[0].astype(F32) + got[0].astype(F32),), ()
        return self.keep + self.leave

    def result(self):
        total, bit = self.keep[0], self.links.fine // 2
        me = lax.axis_index("dp")
        while bit:
            half = total.shape[1] // 2
            upper = (me // bit) % 2
            out = lax.dynamic_slice_in_dim(total, (1 - upper) * half, half, 1)
            stay = lax.dynamic_slice_in_dim(total, upper * half, half, 1)
            total = stay + self.links.dp_xor(out, bit)
            bit //= 2
        return total


class Everywhere:
    def __init__(self, links, v):
        self.links, self.value = links, v
        self.steps = [functools.partial(links.dp_xor, bits=1 << b) for b in range(links.n_dp.bit_length() - 1)]
        self.steps.append(links.mp_swap)

    def launch(self):
        self.flight = [self.steps.pop(0)(self.value)] if self.steps else []

    def land(self):
        for got in self.flight:
            self.value = self.value + got
        self.flight = []
        return (self.value,)

    def result(self):
        while self.steps:
            self.launch()
            self.land()
        return self.value


def settle(done, *chains):
    flat = list(done) + [v for c in chains for v in c.flight]
    flat = list(lax.optimization_barrier(tuple(flat)))
    done, flat = flat[: len(done)], flat[len(done) :]
    sums = []
    for c in chains:
        c.flight, flat = flat[: len(c.flight)], flat[len(c.flight) :]
        sums.extend(c.land())
    return done, sums


def launch(*chains):
    for c in chains:
        c.launch()


def rotary_tables(total, head_size):
    places = np.arange(total, dtype=np.float32)
    steps = np.arange(head_size // 2, dtype=np.float32) * np.float32(2.0) / np.float32(head_size)
    rates = np.power(np.float32(10000.0), -steps).astype(np.float32)
    angles = (places[:, None] * rates[None, :]).astype(np.float64)
    cos, sin = np.cos(angles).astype(np.float32), np.sin(angles).astype(np.float32)
    return np.concatenate([cos] * 4, 1), np.concatenate([-sin, sin, -sin, sin], 1)


def on_device(
    n_dp, n_mp, inputs, seg_ids, omega, norm1_gain, qkv_weight, out_weight, norm2_gain, up_weight, down_weight, out_grad
):
    links = Links(n_dp, n_mp)
    x, dy = inputs[0], out_grad[0]
    rows, width = x.shape
    nb = rows // BR
    dp, mp = lax.axis_index("dp"), lax.axis_index("mp")
    quarter = dp % 4
    half = out_weight.shape[0]
    hd = omega.shape[0]
    groups = half // (2 * hd)
    ff = up_weight.shape[1]
    n_mlp = ff // BF
    scale = hd ** (-0.25)

    seg_all = seg_ids[0]
    starts = jnp.sum((seg_all[None, :] < jnp.arange(SEGS + 1)[:, None]).astype(jnp.int32), axis=1) - mp * rows
    scalars = jnp.concatenate(
        [starts, jnp.stack([seg_all[rows], quarter, dp // links.fine, mp])]
    ).astype(jnp.int32)
    wq_mine = jnp.transpose(qkv_weight, (1, 0, 2))

    def quarter_of(w, axis=0):
        n = w.shape[axis] // 4
        return lax.dynamic_slice_in_dim(w, quarter * n, n, axis)

    def spread_quarters(first):
        second = links.dp_xor(first, 2)
        third = links.dp_xor(first, 1)
        fourth = links.dp_xor(second, 1)
        return first, third, second, fourth

    wq_rows = quarter_of(wq_mine, 1).reshape(-1, half)
    wo_rows = quarter_of(out_weight)
    packed = jnp.concatenate([wq_rows] + [wo_rows[:, c : c + half] for c in range(0, width, half)], axis=0)
    qkvo_y = links.mp_swap(packed)
    mlp_packed = []
    for k in range(n_mlp):
        cols = slice(k * BF, (k + 1) * BF)
        mlp_packed.append(jnp.concatenate([quarter_of(up_weight[:, cols]), quarter_of(down_weight[cols])], axis=0))

    cos_np, sin_np = rotary_tables(seg_all.shape[0], hd)
    table = pl.BlockSpec((BR, 128), lambda i, sp: (sp[S_MP] * nb + i, 0))
    tables = [(jnp.asarray(cos_np), table), (jnp.asarray(sin_np), table)]
    om = (omega * scale, whole(omega))
    g1, g2 = norm1_gain.reshape(1, -1), norm2_gain.reshape(1, -1)

    def rowed(n, dtype):
        s = struct((rows, n), dtype)
        return (s, by_rows(s))

    def kept(shape, dtype):
        s = struct(shape, dtype)
        return (s, whole(s))

    def ws(a):
        return (a, whole(a))

    def rs(a):
        return (a, by_rows(a))

    state_out = kept((groups, 64 * SEGS, 128), F32)
    small_out = kept((groups, 64, 128), F32)
    one_flops = 2 * rows * width * 3 * half
    a1, pq_l, pk_l, v_l, st_l, sm_l = call(
        qkv_first_kernel, (nb,), scalars,
        [rs(x), ws(g1), ws(wq_mine)] + tables + [om],
        [rowed(width, BF16), rowed(half, BF16), rowed(half, BF16), rowed(half, BF16), state_out, small_out],
        [], one_flops,
    )
    qkvo_y = after(qkvo_y, a1)
    qkvo_pieces = spread_quarters(qkvo_y)
    mlp_y = links.mp_swap(after(mlp_packed[0], qkvo_y))
    ex_r = links.mp_swap(sm_l)
    a1, mlp_y, ex_r = lax.optimization_barrier((a1, mlp_y, ex_r))
    pq_r, pk_r, v_r, st_r, sm_r, wq_other = call(
        qkv_second_kernel, (nb,), scalars,
        [rs(a1)] + [ws(p) for p in qkvo_pieces] + tables + [om],
        [rowed(half, BF16), rowed(half, BF16), rowed(half, BF16), state_out, small_out, kept(wq_mine.shape, BF16)],
        [], one_flops,
    )
    ex_l = links.mp_swap(sm_r)
    mlp_x, mlp_c = links.dp_xor(mlp_y, 2), links.dp_xor(mlp_y, 1)
    next_y = links.mp_swap(after(mlp_packed[1], mlp_y))
    ex_l, mlp_x, mlp_c, next_y, pq_r = lax.optimization_barrier((ex_l, mlp_x, mlp_c, next_y, pq_r))
    mlp_pieces = [(mlp_y, mlp_c, mlp_x, links.dp_xor(mlp_x, 1))]
    next_x = links.dp_xor(next_y, 2)
    wide_scratch = pltpu.VMEM((groups, 64 * SEGS, 256), BF16)
    state_scratch = pltpu.VMEM((64 * SEGS, 128), F32)
    at_l, at_r, x2, a2, wo_other = call(
        attend_kernel, (nb,), scalars,
        [rs(x), ws(g2), rs(pq_l), rs(pq_r), ws(st_l), ws(st_r), ws(ex_l), ws(ex_r), ws(out_weight)]
        + [ws(p) for p in qkvo_pieces],
        [rowed(half, BF16), rowed(half, BF16), rowed(width, F32), rowed(width, BF16), kept(out_weight.shape, BF16)],
        [wide_scratch, wide_scratch, state_scratch], 2 * rows * width * 2 * half,
    )

    next_x, a2 = lax.optimization_barrier((next_x, a2))
    mlp_pieces.append((next_y, links.dp_xor(next_y, 1), next_x, links.dp_xor(next_x, 1)))
    grad_scratch = pltpu.VMEM((width, BF), BF16)

    def mlp(k, out_in, da_in):
        last = da_in is not None
        grad = struct((2, 2, width // 2, BF), BF16)
        grad_out = (grad, pl.BlockSpec((2, None, width // 2, BF), lambda j, *_: (0, j, 0, 0)))
        mine_u = pl.BlockSpec((width, BF), lambda j, *_: (0, k), pipeline_mode=pl.Buffered(1))
        mine_d = pl.BlockSpec((BF, width), lambda j, *_: (k, 0), pipeline_mode=pl.Buffered(1))
        return call(
            functools.partial(mlp_kernel, last=last), (2,), scalars,
            [ws(a2), ws(dy), (up_weight, mine_u), (down_weight, mine_d)] + [ws(p) for p in mlp_pieces[k]]
            + [ws(out_in)] + ([ws(da_in)] if last else []),
            [kept((rows, width), BF16 if last else F32), kept((rows, width), F32)] + [grad_out] * 2,
            [grad_scratch, pltpu.VMEM((BF, width), BF16), pltpu.VMEM((rows, BF), BF16), pltpu.VMEM((rows, BF), BF16),
             pltpu.VMEM((rows, width), F32), grad_scratch],
            2 * 6 * 2 * rows * width * BF, vmem=58,
        )

    part_out, part_da, *grads = mlp(0, x2, None)
    sum_a = Sum(links, *grads)
    launch(sum_a)
    output, da2, *grads = mlp(1, part_out, part_da)
    sum_b = Sum(links, *grads)
    (da2,), sums = settle((da2,), sum_a)
    da2 = after(da2, *sums)
    launch(sum_a, sum_b)

    gain8 = kept((8, width), F32)
    dx2, db, gain2, dq_l, dq_r, dst_l, dst_r, dsm_l, dsm_r = call(
        back_one_kernel, (nb,), scalars,
        [rs(x2), rs(da2), rs(dy), ws(g2)] + tables
        + [om, rs(pq_l), rs(pq_r), ws(st_l), ws(st_r), ws(ex_l), ws(ex_r), ws(out_weight), ws(wo_other)],
        [rowed(width, F32), rowed(width, BF16), gain8, rowed(half, BF16), rowed(half, BF16),
         state_out, state_out, small_out, small_out],
        [wide_scratch, wide_scratch, state_scratch], 2 * rows * width * 2 * half,
    )
    (db, dsm_l, dsm_r), sums = settle((db, dsm_l, dsm_r), sum_a, sum_b)
    db = after(db, *sums)
    dex_r, dex_l = links.mp_swap(dsm_l), links.mp_swap(dsm_r)
    launch(sum_a, sum_b)

    def outer(first, second):
        n = first[1].shape[1]
        out = kept((2, 2, width // 2, n), BF16)
        return call(
            outer_kernel, (1,), scalars, [ws(a) for a in first + second], [out, out],
            [pltpu.VMEM((width, n), BF16)], 4 * 2 * rows * width * n,
        )

    grads = outer((db, at_l, at_r), (a1, dq_l, dq_r))
    (keep, send, dex_l, dex_r), sums = settle((*grads, dex_l, dex_r), sum_a)
    sum_c = Sum(links, keep, send)
    dex_l = after(dex_l, *sums)
    launch(sum_a, sum_c)
    dk_l, dv_l, dk_r, dv_r = call(
        back_two_kernel, (nb,), scalars,
        tables + [om, rs(pk_l), rs(pk_r), rs(v_l), rs(v_r), ws(dst_l), ws(dst_r), ws(dex_l), ws(dex_r)],
        [rowed(half, BF16)] * 4, [wide_scratch, wide_scratch, state_scratch], 2 * rows * width * half,
    )
    (dk_l, dk_r, dv_l, dv_r), sums = settle((dk_l, dk_r, dv_l, dv_r), sum_a, sum_b, sum_c)
    dk_l = after(dk_l, *sums)
    launch(sum_a, sum_b)
    grads = outer((a1, dk_l, dk_r), (a1, dv_l, dv_r))
    (keep, send), sums = settle(grads, sum_a, sum_b)
    sum_d = Sum(links, keep, send)
    dx2 = after(dx2, keep, *sums)
    launch(sum_d, sum_c, sum_b)

    def inward(part, dx2, so_far):
        n = nb // 2
        first = part * n

        def at(a):
            return (a, pl.BlockSpec((BR, a.shape[1]), lambda i, *_: (first + i, 0)))

        def body(sp, *refs):
            input_kernel(*refs)

        s = struct((rows, width), F32)
        return call(
            body, (n,), scalars,
            [at(x), ws(g1), at(dx2), at(dq_l), at(dk_l), at(dv_l), at(dq_r), at(dk_r), at(dv_r), ws(wq_mine), ws(wq_other)],
            [(s, at(s)[1]), gain8], [], one_flops, into=so_far,
        )

    input_grad, gain1a = inward(0, dx2, None)
    (input_grad, gain1a), sums = settle((input_grad, gain1a), sum_d, sum_c, sum_b)
    dx2 = after(dx2, *sums)
    launch(sum_d, sum_c, sum_b)
    input_grad, gain1b = inward(1, dx2, input_grad)
    (gain1b,), sums = settle((gain1b,), sum_d, sum_c, sum_b)
    gains = Everywhere(links, jnp.stack([(gain1a + gain1b).sum(0), gain2.sum(0)]))
    launch(sum_d, sum_c, gains)
    settle((), sum_d, sum_c, gains)
    launch(sum_d, sum_c, gains)
    settle((), sum_d, sum_c, gains)
    launch(sum_d, gains)
    settle((), sum_d, gains)
    mlp_sums = [sum_a.result(), sum_b.result()]
    out_sum, q_sum = sum_c.result()
    k_sum, v_sum = sum_d.result()
    up_sum = jnp.concatenate([m[0] for m in mlp_sums], axis=1)
    down_sum = jnp.transpose(jnp.concatenate([m[1] for m in mlp_sums], axis=1))
    out_sum = jnp.transpose(out_sum)
    share = width // (n_dp * n_mp)
    gains = lax.dynamic_slice_in_dim(gains.result(), (dp * n_mp + mp) * share, share, 1)
    qkv_sum = jnp.stack([q_sum, k_sum, v_sum], axis=1)
    return (output[None], input_grad[None], gains[0], qkv_sum, out_sum, gains[1], up_sum, down_sum)


def solution(mesh):
    n_dp, n_mp = mesh.shape["dp"], mesh.shape["mp"]
    return jax.shard_map(
        functools.partial(on_device, n_dp, n_mp),
        mesh=mesh,
        in_specs=(
            P("dp", "mp", None),
            P("dp", None),
            P(),
            P(),
            P(None, None, "mp"),
            P("mp", None),
            P(),
            P(None, "mp"),
            P("mp", None),
            P("dp", "mp", None),
        ),
        out_specs=(
            P("dp", "mp", None),
            P("dp", "mp", None),
            P(("dp", "mp")),
            P("dp", None, "mp"),
            P("mp", "dp"),
            P(("dp", "mp")),
            P("dp", "mp"),
            P("mp", "dp"),
        ),
        check_vma=False,
    )
```

```python
import functools

import jax
import jax.numpy as jnp
import numpy as np
from jax import lax
from jax.experimental import pallas as pl
from jax.experimental.pallas import tpu as pltpu
from jax.sharding import PartitionSpec as P

SEGS = 8
BR = 512
BF = 768
PIECES = 16
F32 = jnp.float32
BF16 = jnp.bfloat16
MIB = 1 << 20
ORDER = [int(format(p, "04b")[::-1], 2) for p in range(PIECES)]

S_DOC, S_QUARTER, S_COARSE, S_MP = 9, 10, 11, 12


def mm(a, b):
    return lax.dot_general(a, b, (((1,), (0,)), ((), ())), preferred_element_type=F32)


def mm_t(a, b):
    return lax.dot_general(a, b, (((1,), (1,)), ((), ())), preferred_element_type=F32)


def t_mm(a, b):
    return lax.dot_general(a, b, (((0,), (0,)), ((), ())), preferred_element_type=F32)


def norm_parts(v):
    mean = jnp.mean(v, axis=-1, keepdims=True)
    centred = v - mean
    var = jnp.mean(centred * centred, axis=-1, keepdims=True)
    rstd = lax.rsqrt(var + 1e-5)
    return centred * rstd, rstd


def norm_back(da, xhat, rstd, gain):
    dxhat = da * gain
    m1 = jnp.mean(dxhat, axis=-1, keepdims=True)
    m2 = jnp.mean(dxhat * xhat, axis=-1, keepdims=True)
    return rstd * (dxhat - m1 - xhat * m2)


def row_sums(v):
    r, n = v.shape
    return jnp.sum(v.reshape(r // 8, 8, n), axis=0)


def lanes(v, g):
    return v[:, 128 * g : 128 * (g + 1)]


def swap_halves(u):
    lane = lax.broadcasted_iota(jnp.int32, u.shape, 1)
    return jnp.where((lane & 63) < 32, pltpu.roll(u, 96, 1), pltpu.roll(u, 32, 1))


def softplus(z):
    e = jnp.exp(-jnp.abs(z))
    series = e * (1.0 + e * (e * (1.0 / 3.0) - 0.5))
    return jnp.maximum(z, 0.0) + jnp.where(e < 0.01, series, jnp.log(1.0 + e))


def gate(p):
    return jnp.where(p < 0.01, p * (1.0 + p * (p * (1.0 / 6.0) - 0.5)), 1.0 - jnp.exp(-p))


def omega_pair(om):
    rows = jnp.concatenate([om, om], axis=0)
    wide = jnp.concatenate([rows, rows], axis=1)
    r = lax.broadcasted_iota(jnp.int32, wide.shape, 0) // 64
    c = lax.broadcasted_iota(jnp.int32, wide.shape, 1) // 32
    return jnp.where(r == c, wide, 0.0)


def omega_split(om):
    pair = omega_pair(om)
    hi = pair.astype(BF16)
    lo = (pair - hi.astype(F32)).astype(BF16)
    top = jnp.concatenate([hi, hi, lo, lo], axis=1)
    bottom = jnp.concatenate([hi, hi, jnp.zeros_like(hi), jnp.zeros_like(hi)], axis=1)
    return jnp.concatenate([top, bottom], axis=0)


def omega_back(om):
    pair = omega_pair(om).astype(BF16)
    return jnp.concatenate([pair, jnp.zeros_like(pair)], axis=1)


def doc_mask(sp, i):
    parts = []
    for t in range(SEGS // 2):
        lane = lax.broadcasted_iota(jnp.int32, (BR, 128), 1) < 64
        row = lax.broadcasted_iota(jnp.int32, (BR, 128), 0) + i * BR
        low = jnp.where(lane, sp[2 * t], sp[2 * t + 1])
        high = jnp.where(lane, sp[2 * t + 1], sp[2 * t + 2])
        parts.append(jnp.where((row >= low) & (row < high), 1.0, 0.0).astype(F32))
    return jnp.concatenate(parts, axis=1)


def spread(feat, mask):
    return jnp.concatenate([feat] * (SEGS // 2), axis=1) * mask


def collect(wide, mask):
    masked = wide * mask
    total = sum(lanes(masked, t) for t in range(SEGS // 2))
    return total + pltpu.roll(total, 64, 1)


def own_lanes(n):
    row = lax.broadcasted_iota(jnp.int32, (n, 128), 0) // 32
    lane = lax.broadcasted_iota(jnp.int32, (n, 128), 1) // 64
    return jnp.where((row & 1) == lane, 1.0, 0.0).astype(F32)


def expand(state, own):
    return jnp.concatenate([state * own, pltpu.roll(state, 64, 1) * own], axis=1).astype(BF16)


def store_pieces(value, scratch, keep_ref, send_ref, sp):
    d = value.shape[0]
    step = d // PIECES
    scratch[...] = value.astype(BF16)
    for p in range(PIECES):
        at = pl.multiple_of((ORDER[p] ^ sp[S_COARSE]) * step, 16)
        ref = keep_ref if p < PIECES // 2 else send_ref
        q = p % (PIECES // 2)
        ref[q * step : (q + 1) * step, :] = scratch[pl.ds(at, step), :]


def put_quarters(sp, pieces, out):
    n = pieces[0].shape[0]
    for k, piece in enumerate(pieces):
        out[pl.ds(pl.multiple_of((sp[S_QUARTER] ^ k) * n, 16), n), :] = piece[...]


def project(sp, i, a1, w, cos, sin, om, pq_o, pk_o, v_o, st_o, sm_o):
    c, s = cos[...], sin[...]
    split = omega_split(om[...])
    mask = doc_mask(sp, i).astype(BF16)
    ones = jnp.ones((BR, 128), BF16)

    def feature(u):
        turned = u * c + swap_halves(u) * s
        hi = turned.astype(BF16)
        lo = (turned - hi.astype(F32)).astype(BF16)
        z = mm(jnp.concatenate([hi, lo], axis=1), split)
        return softplus(lanes(z, 0) + lanes(z, 1)).astype(BF16)

    @pl.when(i == 0)
    def _():
        st_o[...] = jnp.zeros_like(st_o)

    q, k, v = mm(a1, w(0)), mm(a1, w(1)), mm(a1, w(2)).astype(BF16)
    v_o[...] = v
    own = own_lanes(64 * SEGS)
    for g in range(q.shape[1] // 128):
        pq_o[:, 128 * g : 128 * (g + 1)] = feature(lanes(q, g))
        pk = feature(lanes(k, g))
        pk_o[:, 128 * g : 128 * (g + 1)] = pk
        wide = t_mm(spread(pk, mask), jnp.concatenate([lanes(v, g), ones], axis=1))
        st_o[g] += lanes(wide, 0) * own + lanes(wide, 1) * (1.0 - own)

    @pl.when(i == pl.num_programs(0) - 1)
    def _():
        for g in range(st_o.shape[0]):
            sm_o[g] = st_o[g, pl.ds(pl.multiple_of(sp[S_DOC] * 64, 64), 64), :]


def qkv_first_kernel(sp, x, g1, w, cos, sin, om, a1_o, pq_o, pk_o, v_o, st_o, sm_o):
    xhat, _ = norm_parts(x[...].astype(F32))
    a1 = (xhat * g1[...]).astype(BF16)
    a1_o[...] = a1
    project(sp, pl.program_id(0), a1, lambda k: w[k], cos, sin, om, pq_o, pk_o, v_o, st_o, sm_o)


def qkv_second_kernel(sp, a1, w0, w1, w2, w3, cos, sin, om, pq_o, pk_o, v_o, st_o, sm_o, w_o):
    i = pl.program_id(0)

    @pl.when(i == 0)
    def _():
        n = w_o.shape[1] // 4
        for k in range(3):
            put_quarters(sp, [w.at[pl.ds(k * n, n), :] for w in (w0, w1, w2, w3)], w_o.at[k])

    project(sp, i, a1[...], lambda k: w_o[k], cos, sin, om, pq_o, pk_o, v_o, st_o, sm_o)


def expand_states(sp, states, extra, out, scratch):
    own = own_lanes(64 * SEGS)
    at = pl.ds(pl.multiple_of(sp[S_DOC] * 64, 64), 64)
    for g in range(states.shape[0]):
        scratch[...] = states[g]
        scratch[at, :] += extra[g]
        out[g] = expand(scratch[...], own)


def attend_kernel(
    sp, x, g2, pq_l, pq_r, st_l, st_r, ex_l, ex_r, wo_l, w0, w1, w2, w3,
    at_l, at_r, x2_o, a2_o, wo_o, wide_l, wide_r, scratch,
):
    i = pl.program_id(0)

    @pl.when(i == 0)
    def _():
        expand_states(sp, st_l, ex_l, wide_l, scratch)
        expand_states(sp, st_r, ex_r, wide_r, scratch)
        put_quarters(sp, (w0, w1, w2, w3), wo_o)

    mask = doc_mask(sp, i).astype(BF16)
    x2 = x[...].astype(F32)
    for pq, wide, wo, at in ((pq_l, wide_l, wo_l, at_l), (pq_r, wide_r, wo_o, at_r)):
        parts = []
        for g in range(wide.shape[0]):
            nd = mm(spread(lanes(pq, g), mask), wide[g])
            parts.append((lanes(nd, 0) / lanes(nd, 1)).astype(BF16))
        attn = jnp.concatenate(parts, axis=1)
        at[...] = attn
        x2 = x2 + mm(attn, wo[...])
    x2_o[...] = x2
    xhat, _ = norm_parts(x2)
    a2_o[...] = (xhat * g2[...]).astype(BF16)


GC = 0.7978845608028654
CHUNK = 512


def mlp_kernel(
    sp, a2, dy, wu, wd, w0, w1, w2, w3, out_in, *rest, last,
):
    if last:
        da_in, *rest = rest
    out_o, da_o, keep, send, wu_s, wd_s, hact, dhp, acc, perm = rest
    j = pl.program_id(0)
    nj = pl.num_programs(0)
    rows, width = a2.shape

    @pl.when(j == 0)
    def _():
        acc[...] = out_in[...]
        if last:
            da_o[...] = da_in[...]
        else:
            da_o[...] = jnp.zeros_like(da_o)
        wu_s[...] = wu[...]
        wd_s[...] = wd[...]

    @pl.when(j == 1)
    def _():
        n = w0.shape[0] // 2
        put_quarters(sp, [w.at[pl.ds(0, n), :] for w in (w0, w1, w2, w3)], wu_s)
        put_quarters(sp, [w.at[pl.ds(n, n), :] for w in (w0, w1, w2, w3)], wd_s)

    for r in range(rows // CHUNK):
        rs = pl.ds(r * CHUNK, CHUNK)
        h = mm(a2[rs, :], wu_s[...])
        d = mm_t(dy[rs, :], wd_s[...])
        sq = h * h
        t = jnp.tanh(h * (GC + (GC * 0.044715) * sq))
        half1 = 0.5 + 0.5 * t
        act = (h * half1).astype(BF16)
        slope = half1 + (0.5 * h) * (1.0 - t * t) * (GC + (3 * GC * 0.044715) * sq)
        back = (d * slope).astype(BF16)
        hact[rs, :] = act
        dhp[rs, :] = back
        acc[rs, :] += mm(act, wd_s[...])
        da_o[rs, :] += mm_t(back, wu_s[...])

    store_pieces(t_mm(a2[...], dhp[...]), perm, keep.at[0], send.at[0], sp)
    store_pieces(t_mm(dy[...], hact[...]), perm, keep.at[1], send.at[1], sp)

    @pl.when(j == nj - 1)
    def _():
        out_o[...] = acc[...].astype(out_o.dtype)


def back_one_kernel(
    sp, x2, da2, dy, g2, cos, sin, om, pq_l, pq_r, st_l, st_r, ex_l, ex_r, wo_l, wo_r,
    dx2_o, db_o, gain_o, dq_l, dq_r, dst_l, dst_r, dsm_l, dsm_r, wide_l, wide_r, scratch,
):
    i = pl.program_id(0)

    @pl.when(i == 0)
    def _():
        expand_states(sp, st_l, ex_l, wide_l, scratch)
        expand_states(sp, st_r, ex_r, wide_r, scratch)
        gain_o[...] = jnp.zeros_like(gain_o)
        dst_l[...] = jnp.zeros_like(dst_l)
        dst_r[...] = jnp.zeros_like(dst_r)

    xhat, rstd = norm_parts(x2[...])
    da = da2[...]
    gain_o[...] += row_sums(da * xhat)
    dx2 = dy[...].astype(F32) + norm_back(da, xhat, rstd, g2[...])
    dx2_o[...] = dx2
    datt = dx2.astype(BF16)
    db_o[...] = datt
    mask = doc_mask(sp, i)
    mask_b = mask.astype(BF16)
    own = own_lanes(64 * SEGS)
    back = omega_back(om[...])
    c, s = cos[...], sin[...]
    for pq, wide, wo, dq, dst in (
        (pq_l, wide_l, wo_l, dq_l, dst_l),
        (pq_r, wide_r, wo_r, dq_r, dst_r),
    ):
        dattn = mm_t(datt, wo[...])
        for g in range(wide.shape[0]):
            feat = lanes(pq, g)
            sprd = spread(feat, mask_b)
            nd = mm(sprd, wide[g])
            inv = 1.0 / lanes(nd, 1)
            attn = lanes(nd, 0) * inv
            dnum = lanes(dattn, g) * inv
            both = jnp.concatenate([dnum, -dnum * attn], axis=1).astype(BF16)
            dpq = collect(mm_t(both, wide[g]), mask)
            dwide = t_mm(sprd, both)
            dst[g] += lanes(dwide, 0) * own + pltpu.roll(lanes(dwide, 1) * own, 64, 1)
            dz = (dpq * gate(feat.astype(F32))).astype(BF16)
            dr = mm_t(dz, back)
            dq[:, 128 * g : 128 * (g + 1)] = (dr * c + swap_halves(dr * s)).astype(BF16)

    @pl.when(i == pl.num_programs(0) - 1)
    def _():
        at = pl.ds(pl.multiple_of(sp[S_DOC] * 64, 64), 64)
        for g in range(dst_l.shape[0]):
            dsm_l[g] = dst_l[g, at, :]
            dsm_r[g] = dst_r[g, at, :]


def back_two_kernel(
    sp, cos, sin, om, pk_l, pk_r, v_l, v_r, dst_l, dst_r, ex_l, ex_r,
    dk_l, dv_l, dk_r, dv_r, wide_l, wide_r, scratch,
):
    i = pl.program_id(0)

    @pl.when(i == 0)
    def _():
        expand_states(sp, dst_l, ex_l, wide_l, scratch)
        expand_states(sp, dst_r, ex_r, wide_r, scratch)

    mask = doc_mask(sp, i)
    mask_b = mask.astype(BF16)
    back = omega_back(om[...])
    c, s = cos[...], sin[...]
    ones = jnp.ones((BR, 128), BF16)
    for pk, v, wide, dk, dv in (
        (pk_l, v_l, wide_l, dk_l, dv_l),
        (pk_r, v_r, wide_r, dk_r, dv_r),
    ):
        for g in range(wide.shape[0]):
            feat = lanes(pk, g)
            dpk = collect(mm_t(jnp.concatenate([lanes(v, g), ones], axis=1), wide[g]), mask)
            dv[:, 128 * g : 128 * (g + 1)] = mm(spread(feat, mask_b), wide[g, :, :128]).astype(BF16)
            dz = (dpk * gate(feat.astype(F32))).astype(BF16)
            dr = mm_t(dz, back)
            dk[:, 128 * g : 128 * (g + 1)] = (dr * c + swap_halves(dr * s)).astype(BF16)


def outer_kernel(sp, left0, l0, r0, left1, l1, r1, keep, send, perm):
    for t, (left, sides) in enumerate(((left0, (l0, r0)), (left1, (l1, r1)))):
        for k, right in enumerate(sides):
            store_pieces(t_mm(left[...], right[...]), perm, keep.at[t, k], send.at[t, k], sp)


def input_kernel(x, g1, dx2, dq_l, dk_l, dv_l, dq_r, dk_r, dv_r, w_l, w_r, dx_o, gain_o):
    i = pl.program_id(0)

    @pl.when(i == 0)
    def _():
        gain_o[...] = jnp.zeros_like(gain_o)

    da = None
    for w, parts in ((w_l, (dq_l, dk_l, dv_l)), (w_r, (dq_r, dk_r, dv_r))):
        for k, part in enumerate(parts):
            term = mm_t(part[...], w[k])
            da = term if da is None else da + term
    xhat, rstd = norm_parts(x[...].astype(F32))
    gain_o[...] += row_sums(da * xhat)
    dx_o[...] = dx2[...] + norm_back(da, xhat, rstd, g1[...])


def whole(a, once=True):
    shape = tuple(a.shape)
    zeros = (0,) * len(shape)
    mode = dict(pipeline_mode=pl.Buffered(1)) if once else {}
    return pl.BlockSpec(shape, lambda i, *_: zeros, **mode)


def by_rows(a, br=BR):
    return pl.BlockSpec((br, a.shape[1]), lambda i, *_: (i, 0))


def call(kernel, grid, scalars, ins, outs, scratch, flops, vmem, into=None):
    args = [a for a, _ in ins]
    moved = sum(a.size * a.dtype.itemsize for a in args)
    moved += sum(s.size * s.dtype.itemsize for s, _ in outs)
    n_in = len(args) + 1
    extra = [] if into is None else [into]
    n_dep = len(extra)

    def body(*refs):
        return kernel(*refs[:n_in], *refs[n_in + n_dep :])

    return pl.pallas_call(
        body,
        out_shape=[s if isinstance(s, jax.ShapeDtypeStruct) else pltpu.HBM(s.shape, s.dtype) for s, _ in outs],
        grid_spec=pltpu.PrefetchScalarGridSpec(
            num_scalar_prefetch=1,
            grid=grid,
            in_specs=[s for _, s in ins] + [pl.BlockSpec(memory_space=pl.ANY)] * n_dep,
            out_specs=[s for _, s in outs],
            scratch_shapes=scratch,
        ),
        compiler_params=pltpu.CompilerParams(
            dimension_semantics=("arbitrary",) * len(grid), vmem_limit_bytes=vmem * MIB
        ),
        cost_estimate=pl.CostEstimate(flops=flops, bytes_accessed=moved, transcendentals=0),
            input_output_aliases={n_in: 0} if extra else {},
    )(scalars, *args, *extra)


def struct(shape, dtype):
    return jax.ShapeDtypeStruct(tuple(shape), dtype)


class Far:
    def __init__(self, shape, dtype):
        self.shape, self.dtype = tuple(shape), jnp.dtype(dtype)
        self.size = int(np.prod(shape))


def far(a):
    return pltpu.with_memory_space_constraint(a, pltpu.HBM)


class Links:
    def __init__(self, n_dp, n_mp):
        self.n_dp, self.n_mp = n_dp, n_mp
        self.fine = n_dp // PIECES

    def dp_xor(self, v, bits):
        return lax.ppermute(v, "dp", [(d, d ^ bits) for d in range(self.n_dp)])

    def mp_swap(self, v):
        return lax.ppermute(v, "mp", [(m, m ^ 1) for m in range(self.n_mp)])

    def both_swap(self, v, bits):
        n = self.n_mp
        pairs = [(d * n + m, (d ^ bits) * n + (m ^ 1)) for d in range(self.n_dp) for m in range(n)]
        return lax.ppermute(v, ("dp", "mp"), pairs)


def total(parts, dtype=BF16):
    return sum(v.astype(F32) for v in parts).astype(dtype)


def after(v, *deps):
    return lax.optimization_barrier((v,) + deps)[0]


class Sum:
    def __init__(self, links, keep, send, direct=False):
        self.links, self.stage, self.direct = links, 0, direct
        self.keep, self.leave = (keep,), (send,)
        self.rider, self.riders = None, []

    def launch(self):
        links, fine = self.links, self.links.fine

        def along(bits):
            return lambda v: links.dp_xor(v, bits * fine)

        last = [[along(8), along(4), along(12)]] if self.direct else [[along(4)], [along(8)]]
        ways = [[along(1)], [along(2), links.mp_swap], [links.mp_swap, along(2)], *last][self.stage]
        if self.stage == 3 and self.rider is not None:
            self.leave = tuple(jnp.concatenate([v, self.rider], axis=0) for v in self.leave)
        self.flight = [way(v) for way, v in zip(ways, self.leave)]

    def land(self):
        stage, got = self.stage, self.flight
        self.stage, self.flight = stage + 1, []
        if stage == 0:
            (keep,), (got,) = self.keep, got
            half = keep.shape[2] // 2
            self.keep = (total((keep[0, :, :half], got[0, :, :half])), total((keep[1, 0], got[1, 0])))
            self.leave = (total((keep[0, :, half:], got[0, :, half:])), total((keep[1, 1], got[1, 1])))
        elif stage == 1:
            (a, b), (ga, gb) = self.keep, got
            half = b.shape[0] // 2
            self.keep = (total((a[0], ga[0])), total((b[:half], gb[:half])))
            self.leave = (total((a[1], ga[1])), total((b[half:], gb[half:])))
        elif stage == 2:
            (a, b), (ga, gb) = self.keep, got
            n = a.shape[0] // (4 if self.direct else 2)
            cuts = [slice(r, r + n) for r in range(0, a.shape[0], n)]
            parts = [jnp.concatenate([total((a[c], ga[c])), total((b[c], gb[c]))], axis=0) for c in cuts]
            self.keep, self.leave = (parts[0],), tuple(parts[1:])
        elif stage == 3 and not self.direct:
            (a,), (ga,) = self.keep, got
            a, ga = [v.reshape((2, -1) + v.shape[1:]) for v in (a, ga)]
            half = a.shape[1] // 2
            both = [total((a[:, c], ga[:, c])) for c in (slice(0, half), slice(half, 2 * half))]
            self.keep, self.leave = (both[0].reshape((-1,) + a.shape[2:]),), (both[1].reshape((-1,) + a.shape[2:]),)
        else:
            (a,) = self.keep
            self.riders = [g[a.shape[0] :] for g in got]
            self.keep, self.leave = (total([a] + [g[: a.shape[0]] for g in got], F32),), ()
        return self.keep + self.leave

    def result(self):
        (sums,) = self.keep
        sums, bit = sums.reshape((2, -1) + sums.shape[1:]), self.links.fine // 2
        me = lax.axis_index("dp")
        while bit:
            half = sums.shape[1] // 2
            upper = (me // bit) % 2
            out = lax.dynamic_slice_in_dim(sums, (1 - upper) * half, half, 1)
            stay = lax.dynamic_slice_in_dim(sums, upper * half, half, 1)
            sums = stay + self.links.dp_xor(out, bit)
            bit //= 2
        return sums


class Gains:
    def __init__(self, links, v):
        self.links, self.value = links, v

    def launch(self):
        links = self.links
        x = links.dp_xor(self.value, 2 * links.fine)
        self.flight = [x, links.mp_swap(self.value), links.both_swap(self.value, 2 * links.fine)]

    def land(self):
        self.value = self.value + self.flight[0] + self.flight[1] + self.flight[2]
        self.flight = []
        return (self.value,)

    def parts(self, n):
        hi = self.value.astype(BF16)
        lo = (self.value - hi.astype(F32)).astype(BF16)
        return jnp.concatenate([hi, lo], axis=0).reshape(-1, n)

    def take(self, riders):
        shape = (2,) + self.value.shape
        for r in riders:
            self.value = self.value + r.reshape(shape).astype(F32).sum(0)

    def result(self):
        bits = [self.links.fine] + [1 << b for b in range(self.links.fine.bit_length() - 1)]
        for bit in bits:
            self.value = self.value + self.links.dp_xor(self.value, bit)
        return self.value


def settle(done, *chains):
    flat = list(done) + [v for c in chains for v in c.flight]
    flat = list(lax.optimization_barrier(tuple(flat)))
    done, flat = flat[: len(done)], flat[len(done) :]
    sums = []
    for c in chains:
        c.flight, flat = flat[: len(c.flight)], flat[len(c.flight) :]
        sums.extend(c.land())
    return done, sums


def launch(*chains):
    for c in chains:
        c.launch()


def rotary_tables(total, head_size):
    places = np.arange(total, dtype=np.float32)
    steps = np.arange(head_size // 2, dtype=np.float32) * np.float32(2.0) / np.float32(head_size)
    rates = np.power(np.float32(10000.0), -steps).astype(np.float32)
    angles = (places[:, None] * rates[None, :]).astype(np.float64)
    cos, sin = np.cos(angles).astype(np.float32), np.sin(angles).astype(np.float32)
    return np.concatenate([cos] * 4, 1), np.concatenate([-sin, sin, -sin, sin], 1)


def on_device(
    n_dp, n_mp, inputs, seg_ids, omega, norm1_gain, qkv_weight, out_weight, norm2_gain, up_weight, down_weight, out_grad
):
    links = Links(n_dp, n_mp)
    x, dy = inputs[0], out_grad[0]
    rows, width = x.shape
    nb = rows // BR
    dp, mp = lax.axis_index("dp"), lax.axis_index("mp")
    quarter = dp % 4
    half = out_weight.shape[0]
    hd = omega.shape[0]
    groups = half // (2 * hd)
    ff = up_weight.shape[1]
    n_mlp = ff // BF
    scale = hd ** (-0.25)

    seg_all = seg_ids[0]
    starts = jnp.sum((seg_all[None, :] < jnp.arange(SEGS + 1)[:, None]).astype(jnp.int32), axis=1) - mp * rows
    scalars = jnp.concatenate(
        [starts, jnp.stack([seg_all[rows], quarter, dp // links.fine, mp])]
    ).astype(jnp.int32)
    wq_mine = jnp.transpose(qkv_weight, (1, 0, 2))

    def quarter_of(w, axis=0):
        n = w.shape[axis] // 4
        return lax.dynamic_slice_in_dim(w, quarter * n, n, axis)

    wq_quarter = quarter_of(wq_mine, 1).reshape(-1, half)

    cos_np, sin_np = rotary_tables(seg_all.shape[0], hd)
    table = pl.BlockSpec((BR, 128), lambda i, sp: (sp[S_MP] * nb + i, 0))
    tables = [(far(jnp.asarray(cos_np)), table), (far(jnp.asarray(sin_np)), table)]
    om = (omega * scale, whole(omega))
    g1, g2 = norm1_gain.reshape(1, -1), norm2_gain.reshape(1, -1)

    def rowed(n, dtype, kind=Far):
        s = kind((rows, n), dtype)
        return (s, by_rows(s))

    def kept(shape, dtype, kind=Far):
        s = kind(shape, dtype)
        return (s, whole(s))

    def ws(a):
        return (far(a), whole(a))

    def rs(a):
        return (far(a), by_rows(a))

    def near(pair):
        a, spec = pair
        return (struct(a.shape, a.dtype), spec) if isinstance(a, Far) else (a, spec)

    def near_rows(a):
        return (a, by_rows(a))

    def near_whole(a):
        return (a, whole(a))

    state_out = kept((groups, 64 * SEGS, 128), F32)
    small_out = near(kept((groups, 64, 128), F32))
    one_flops = 2 * rows * width * 3 * half
    wq_y = links.mp_swap(wq_quarter)
    a1, pq_l, pk_l, v_l, st_l, sm_l = call(
        qkv_first_kernel, (nb,), scalars,
        [rs(x), near_whole(g1), ws(wq_mine)] + tables + [om],
        [rowed(width, BF16), rowed(half, BF16), rowed(half, BF16), rowed(half, BF16), state_out, small_out],
        [], one_flops, 16,
    )
    wq_y, a1, sm_l, *weights = lax.optimization_barrier((wq_y, a1, sm_l, out_weight, up_weight, down_weight))
    wq_x, wq_c = links.dp_xor(wq_y, 2), links.dp_xor(wq_y, 1)
    ex_r = links.mp_swap(sm_l)
    wo_y = links.mp_swap(quarter_of(weights[0]))
    mlp_quarters = []
    for k in range(n_mlp):
        cols = slice(k * BF, (k + 1) * BF)
        mlp_quarters.append(jnp.concatenate([quarter_of(weights[1][:, cols]), quarter_of(weights[2][cols])], axis=0))
    mlp_y = links.mp_swap(mlp_quarters[0])
    wq_x, wq_c, wo_y, ex_r, a1, *mlp_quarters = lax.optimization_barrier((wq_x, wq_c, wo_y, ex_r, a1, *mlp_quarters))
    wq_pieces = (wq_y, wq_c, wq_x, links.dp_xor(wq_x, 1))
    wo_x, wo_c = links.dp_xor(wo_y, 2), links.dp_xor(wo_y, 1)
    pq_r, pk_r, v_r, st_r, sm_r, wq_other = call(
        qkv_second_kernel, (nb,), scalars,
        [rs(a1)] + [near_whole(p) for p in wq_pieces] + tables + [om],
        [rowed(half, BF16), rowed(half, BF16), rowed(half, BF16), state_out, small_out, kept(wq_mine.shape, BF16)],
        [], one_flops, 16,
    )
    wo_x, wo_c, mlp_y, sm_r, mlp_quarters[1] = lax.optimization_barrier((wo_x, wo_c, mlp_y, sm_r, mlp_quarters[1]))
    ex_l = links.mp_swap(sm_r)
    wo_pieces = (wo_y, wo_c, wo_x, links.dp_xor(wo_x, 1))
    mlp_x, mlp_c = links.dp_xor(mlp_y, 2), links.dp_xor(mlp_y, 1)
    ex_l, mlp_quarters[1] = lax.optimization_barrier((ex_l, mlp_quarters[1]))
    next_y = links.mp_swap(mlp_quarters[1])
    wide_scratch = pltpu.VMEM((groups, 64 * SEGS, 256), BF16)
    state_scratch = pltpu.VMEM((64 * SEGS, 128), F32)
    at_l, at_r, x2, a2, wo_other = call(
        attend_kernel, (nb,), scalars,
        [rs(x), near_whole(g2), rs(pq_l), rs(pq_r), ws(st_l), ws(st_r), near_whole(ex_l), near_whole(ex_r), ws(out_weight)]
        + [near_whole(p) for p in wo_pieces],
        [rowed(half, BF16), rowed(half, BF16), rowed(width, F32), rowed(width, BF16), kept(out_weight.shape, BF16)],
        [wide_scratch, wide_scratch, state_scratch], 2 * rows * width * 2 * half, 20,
    )
    mlp_x, mlp_c, next_y, a2 = lax.optimization_barrier((mlp_x, mlp_c, next_y, a2))
    mlp_pieces = [(mlp_y, mlp_c, mlp_x, links.dp_xor(mlp_x, 1))]
    next_x, next_c = links.dp_xor(next_y, 2), links.dp_xor(next_y, 1)

    grad_scratch = pltpu.VMEM((width, BF), BF16)

    def mlp(k, out_in, da_in):
        last = da_in is not None
        grad = Far((2, 2, width // 2, BF), BF16)
        grad_out = (grad, pl.BlockSpec((2, None, width // 2, BF), lambda j, *_: (0, j, 0, 0)))
        mine_u = pl.BlockSpec((width, BF), lambda j, *_: (0, k), pipeline_mode=pl.Buffered(1))
        mine_d = pl.BlockSpec((BF, width), lambda j, *_: (k, 0), pipeline_mode=pl.Buffered(1))
        return call(
            functools.partial(mlp_kernel, last=last), (2,), scalars,
            [ws(a2), ws(dy), (far(up_weight), mine_u), (far(down_weight), mine_d)] + [near_whole(p) for p in mlp_pieces[k]]
            + [ws(out_in)] + ([ws(da_in)] if last else []),
            [kept((rows, width), BF16 if last else F32), (near if last else tuple)(kept((rows, width), F32))] + [grad_out] * 2,
            [grad_scratch, pltpu.VMEM((BF, width), BF16), pltpu.VMEM((rows, BF), BF16), pltpu.VMEM((rows, BF), BF16),
             pltpu.VMEM((rows, width), F32), grad_scratch],
            2 * 6 * 2 * rows * width * BF, 46,
        )

    part_out, part_da, *grads = mlp(0, x2, None)
    next_x, next_c, part_da = lax.optimization_barrier((next_x, next_c, part_da))
    mlp_pieces.append((next_y, next_c, next_x, links.dp_xor(next_x, 1)))
    sum_a = Sum(links, *grads)
    launch(sum_a)
    output, da2, *grads = mlp(1, part_out, part_da)
    sum_b = Sum(links, *grads)
    launch(sum_b)
    (da2,), sums = settle((da2,), sum_a, sum_b)
    da2 = after(da2, *sums)
    launch(sum_a, sum_b)

    gain8 = near(kept((8, width), F32))
    dx2, db, gain2, dq_l, dq_r, dst_l, dst_r, dsm_l, dsm_r = call(
        back_one_kernel, (nb,), scalars,
        [near_rows(x2), near_rows(da2), near_rows(dy), near_whole(g2)] + tables
        + [om, rs(pq_l), rs(pq_r), ws(st_l), ws(st_r), near_whole(ex_l), near_whole(ex_r), near_whole(out_weight), near_whole(wo_other)],
        [rowed(width, F32), near(rowed(width, BF16)), gain8, near(rowed(half, BF16)), near(rowed(half, BF16)),
         state_out, state_out, small_out, small_out],
        [wide_scratch, wide_scratch, state_scratch], 2 * rows * width * 2 * half, 32,
    )
    (db, dsm_l, dsm_r), sums = settle((db, dsm_l, dsm_r), sum_a)
    db = after(db, *sums)
    dex_r, dex_l = links.mp_swap(dsm_l), links.mp_swap(dsm_r)
    launch(sum_a)

    def outer(first, second):
        n = first[1].shape[1]
        out = near(kept((2, 2, width // 2, n), BF16))
        return call(
            outer_kernel, (1,), scalars, [near_whole(a) for a in first + second], [out, out],
            [pltpu.VMEM((width, n), BF16)], 4 * 2 * rows * width * n, 12,
        )

    grads = outer((db, at_l, at_r), (a1, dq_l, dq_r))
    (keep, send, dex_l, dex_r), sums = settle((*grads, dex_l, dex_r), sum_a)
    sum_c = Sum(links, keep, send)
    dex_l = after(dex_l, *sums)
    launch(sum_a, sum_c)
    dk_l, dv_l, dk_r, dv_r = call(
        back_two_kernel, (nb,), scalars,
        tables + [om, rs(pk_l), rs(pk_r), rs(v_l), rs(v_r), ws(dst_l), ws(dst_r), near_whole(dex_l), near_whole(dex_r)],
        [near(rowed(half, BF16))] * 4, [wide_scratch, wide_scratch, state_scratch], 2 * rows * width * half, 18,
    )
    (dk_l, dk_r, dv_l, dv_r), sums = settle((dk_l, dk_r, dv_l, dv_r), sum_a, sum_b, sum_c)
    dk_l = after(dk_l, *sums)
    launch(sum_a, sum_b)
    grads = outer((a1, dk_l, dk_r), (a1, dv_l, dv_r))
    (keep, send), sums = settle(grads, sum_a, sum_b)
    sum_d = Sum(links, keep, send, direct=True)
    dx2 = after(dx2, keep, *sums)
    launch(sum_d, sum_c, sum_b)

    def inward(part, dx2, so_far):
        n = nb // 2
        first = part * n

        def at(a):
            return (a, pl.BlockSpec((BR, a.shape[1]), lambda i, *_: (first + i, 0)))

        def body(sp, *refs):
            input_kernel(*refs)

        s = Far((rows, width), F32)
        return call(
            body, (n,), scalars,
            [at(x), near_whole(g1), at(dx2), at(dq_l), at(dk_l), at(dv_l), at(dq_r), at(dk_r), at(dv_r), near_whole(wq_mine), near_whole(wq_other)],
            [(s, at(s)[1]), gain8], [], one_flops, 18, into=so_far,
        )

    input_grad, gain1a = inward(0, dx2, None)
    (input_grad, gain1a), sums = settle((input_grad, gain1a), sum_d, sum_c, sum_b)
    dx2 = after(dx2, *sums)
    launch(sum_d, sum_c, sum_b)
    input_grad, gain1b = inward(1, dx2, input_grad)
    (gain1b,), sums = settle((gain1b,), sum_d, sum_c, sum_b)
    gains = Gains(links, jnp.stack([(gain1a + gain1b).sum(0), gain2.sum(0)]))
    launch(sum_d, sum_c, gains)
    settle((), gains)
    settle((), sum_d, sum_c)
    sum_d.rider = gains.parts(half)
    launch(sum_d, sum_c)
    settle((), sum_d, sum_c)
    gains.take(sum_d.riders)
    mlp_sums = [sum_a.result(), sum_b.result()]
    out_sum, q_sum = sum_c.result()
    k_sum, v_sum = sum_d.result()
    up_sum = jnp.concatenate([m[0] for m in mlp_sums], axis=1)
    down_sum = jnp.transpose(jnp.concatenate([m[1] for m in mlp_sums], axis=1))
    out_sum = jnp.transpose(out_sum)
    share = width // (n_dp * n_mp)
    gains = lax.dynamic_slice_in_dim(gains.result(), (dp * n_mp + mp) * share, share, 1)
    qkv_sum = jnp.stack([q_sum, k_sum, v_sum], axis=1)
    return (output[None], input_grad[None], gains[0], qkv_sum, out_sum, gains[1], up_sum, down_sum)


def solution(mesh):
    n_dp, n_mp = mesh.shape["dp"], mesh.shape["mp"]
    return jax.shard_map(
        functools.partial(on_device, n_dp, n_mp),
        mesh=mesh,
        in_specs=(
            P("dp", "mp", None),
            P("dp", None),
            P(),
            P(),
            P(None, None, "mp"),
            P("mp", None),
            P(),
            P(None, "mp"),
            P("mp", None),
            P("dp", "mp", None),
        ),
        out_specs=(
            P("dp", "mp", None),
            P("dp", "mp", None),
            P(("dp", "mp")),
            P("dp", None, "mp"),
            P("mp", "dp"),
            P(("dp", "mp")),
            P("dp", "mp"),
            P("mp", "dp"),
        ),
        check_vma=False,
    )
```

```python
import functools

import jax
import jax.numpy as jnp
import numpy as np
from jax import lax
from jax.experimental import pallas as pl
from jax.experimental.pallas import tpu as pltpu
from jax.sharding import PartitionSpec as P

SEGS = 8
BR = 512
BF = 768
PIECES = 16
F32 = jnp.float32
BF16 = jnp.bfloat16
MIB = 1 << 20
ORDER = [int(format(p, "04b")[::-1], 2) for p in range(PIECES)]

S_QUARTER, S_COARSE, S_MP = 9, 10, 11


def mm(a, b):
    return lax.dot_general(a, b, (((1,), (0,)), ((), ())), preferred_element_type=F32)


def mm_t(a, b):
    return lax.dot_general(a, b, (((1,), (1,)), ((), ())), preferred_element_type=F32)


def t_mm(a, b):
    return lax.dot_general(a, b, (((0,), (0,)), ((), ())), preferred_element_type=F32)


def norm_parts(v):
    mean = jnp.mean(v, axis=-1, keepdims=True)
    centred = v - mean
    var = jnp.mean(centred * centred, axis=-1, keepdims=True)
    rstd = lax.rsqrt(var + 1e-5)
    return centred * rstd, rstd


def norm_back(da, xhat, rstd, gain):
    dxhat = da * gain
    m1 = jnp.mean(dxhat, axis=-1, keepdims=True)
    m2 = jnp.mean(dxhat * xhat, axis=-1, keepdims=True)
    return rstd * (dxhat - m1 - xhat * m2)


def row_sums(v):
    r, n = v.shape
    return jnp.sum(v.reshape(r // 8, 8, n), axis=0)


def lanes(v, g):
    return v[:, 128 * g : 128 * (g + 1)]


def swap_halves(u):
    lane = lax.broadcasted_iota(jnp.int32, u.shape, 1)
    return jnp.where((lane & 63) < 32, pltpu.roll(u, 96, 1), pltpu.roll(u, 32, 1))


def softplus(z):
    e = jnp.exp(-jnp.abs(z))
    series = e * (1.0 + e * (e * (1.0 / 3.0) - 0.5))
    return jnp.maximum(z, 0.0) + jnp.where(e < 0.01, series, jnp.log(1.0 + e))


def gate(p):
    return jnp.where(p < 0.01, p * (1.0 + p * (p * (1.0 / 6.0) - 0.5)), 1.0 - jnp.exp(-p))


def omega_pair(om):
    om = om * om.shape[1] ** (-0.25)
    rows = jnp.concatenate([om, om], axis=0)
    wide = jnp.concatenate([rows, rows], axis=1)
    r = lax.broadcasted_iota(jnp.int32, wide.shape, 0) // 32
    c = lax.broadcasted_iota(jnp.int32, wide.shape, 1) // 64
    return jnp.where(r == c, wide, 0.0)


def omega_split(om):
    pair = omega_pair(om)
    hi = pair.astype(BF16)
    lo = (pair - hi.astype(F32)).astype(BF16)
    top = jnp.concatenate([hi, hi], axis=1)
    bottom = jnp.concatenate([lo, jnp.zeros_like(lo)], axis=1)
    return jnp.concatenate([top, top, bottom, bottom], axis=0)


def omega_back(om):
    pair = omega_pair(om).astype(BF16)
    return jnp.concatenate([pair, jnp.zeros_like(pair)], axis=0)


def shared_doc(sp):
    middle = (1 - sp[S_MP]) * pl.num_programs(0) * BR
    doc = sum((sp[s] <= middle).astype(jnp.int32) for s in range(1, SEGS))
    return pl.ds(pl.multiple_of(doc * 64, 64), 64)


def doc_mask(sp, i):
    parts = []
    for t in range(SEGS // 2):
        lane = lax.broadcasted_iota(jnp.int32, (BR, 128), 1) < 64
        row = lax.broadcasted_iota(jnp.int32, (BR, 128), 0) + i * BR
        low = jnp.where(lane, sp[2 * t], sp[2 * t + 1])
        high = jnp.where(lane, sp[2 * t + 1], sp[2 * t + 2])
        parts.append(jnp.where((row >= low) & (row < high), 1.0, 0.0).astype(F32))
    return jnp.concatenate(parts, axis=1)


def spread(feat, mask):
    return jnp.concatenate([feat] * (SEGS // 2), axis=1) * mask


def collect(wide, mask):
    masked = wide * mask
    total = sum(lanes(masked, t) for t in range(SEGS // 2))
    return total + pltpu.roll(total, 64, 1)


def own_lanes(n):
    row = lax.broadcasted_iota(jnp.int32, (n, 128), 0) // 32
    lane = lax.broadcasted_iota(jnp.int32, (n, 128), 1) // 64
    return jnp.where((row & 1) == lane, 1.0, 0.0).astype(F32)


def expand(state, own):
    return jnp.concatenate([state * own, pltpu.roll(state, 64, 1) * own], axis=1).astype(BF16)


def store_pieces(value, scratch, keep_ref, send_ref, sp):
    d = value.shape[0]
    step = d // PIECES
    scratch[...] = value.astype(BF16)
    for p in range(PIECES):
        at = pl.multiple_of((ORDER[p] ^ sp[S_COARSE]) * step, 16)
        ref = keep_ref if p < PIECES // 2 else send_ref
        q = p % (PIECES // 2)
        ref[q * step : (q + 1) * step, :] = scratch[pl.ds(at, step), :]


def put_pieces(sp, pieces, out):
    n = pieces[0].shape[0]
    own = sp[S_QUARTER] & (len(pieces) - 1)
    for k, piece in enumerate(pieces):
        out[pl.ds(pl.multiple_of((own ^ k) * n, 16), n), :] = piece[...]


def feature(u, cos, sin, split):
    turned = u * cos + swap_halves(u) * sin
    hi = turned.astype(BF16)
    lo = (turned - hi.astype(F32)).astype(BF16)
    z = mm_t(jnp.concatenate([hi, lo], axis=1), split)
    return softplus(lanes(z, 0) + lanes(z, 1)).astype(BF16)


def features(a1, w, cos, sin, om, out):
    split = omega_split(om[...])
    u, c, s = mm(a1, w), cos[...], sin[...]
    for g in range(u.shape[1] // 128):
        out[:, 128 * g : 128 * (g + 1)] = feature(lanes(u, g), c, s, split)


def keys_values(sp, a1, wk, wv, cos, sin, om, pk_o, v_o, st_o, sm_o):
    i = pl.program_id(0)
    mask = doc_mask(sp, i).astype(BF16)
    ones = jnp.ones((BR, 128), BF16)

    @pl.when(i == 0)
    def _():
        st_o[...] = jnp.zeros_like(st_o)

    v = mm(a1, wv).astype(BF16)
    v_o[...] = v
    features(a1, wk, cos, sin, om, pk_o)
    own = own_lanes(64 * SEGS)
    for g in range(st_o.shape[0]):
        wide = t_mm(spread(lanes(pk_o, g), mask), jnp.concatenate([lanes(v, g), ones], axis=1))
        st_o[g] += lanes(wide, 0) * own + lanes(wide, 1) * (1.0 - own)

    @pl.when(i == pl.num_programs(0) - 1)
    def _():
        at = shared_doc(sp)
        for g in range(st_o.shape[0]):
            sm_o[g] = st_o[g, at, :]


def keys_first_kernel(sp, x, gains, wk, wv, cos, sin, om, a1_o, pk_o, v_o, st_o, sm_o):
    xhat, _ = norm_parts(x[...].astype(F32))
    a1 = (xhat * gains[0:1, :]).astype(BF16)
    a1_o[...] = a1
    keys_values(sp, a1, wk[...], wv[...], cos, sin, om, pk_o, v_o, st_o, sm_o)


def keys_second_kernel(sp, a1, *refs):
    *pieces, cos, sin, om, pk_o, v_o, st_o, sm_o, w_o = refs

    @pl.when(pl.program_id(0) == 0)
    def _():
        n = w_o.shape[1] // len(pieces)
        for k in range(3):
            put_pieces(sp, [w.at[pl.ds(k * n, n), :] for w in pieces], w_o.at[k])

    keys_values(sp, a1[...], w_o[1], w_o[2], cos, sin, om, pk_o, v_o, st_o, sm_o)


def queries_kernel(sp, a1, w, cos, sin, om, pq_o):
    features(a1[...], w[...], cos, sin, om, pq_o)


def expand_states(sp, states, extra, out, scratch):
    own = own_lanes(64 * SEGS)
    at = shared_doc(sp)
    for g in range(states.shape[0]):
        scratch[...] = states[g]
        scratch[at, :] += extra[g]
        out[g] = expand(scratch[...], own)


def attend_kernel(
    sp, x, gains, pq_l, pq_r, st_l, st_r, ex_l, ex_r, wo_l, w0, w1,
    at_l, at_r, x2_o, a2_o, wo_o, wide_l, wide_r, scratch,
):
    i = pl.program_id(0)

    @pl.when(i == 0)
    def _():
        expand_states(sp, st_l, ex_l, wide_l, scratch)
        expand_states(sp, st_r, ex_r, wide_r, scratch)
        put_pieces(sp, (w0, w1), wo_o)

    mask = doc_mask(sp, i).astype(BF16)
    x2 = x[...].astype(F32)
    for pq, wide, wo, at in ((pq_l, wide_l, wo_l, at_l), (pq_r, wide_r, wo_o, at_r)):
        parts = []
        for g in range(wide.shape[0]):
            nd = mm(spread(lanes(pq, g), mask), wide[g])
            parts.append((lanes(nd, 0) / lanes(nd, 1)).astype(BF16))
        attn = jnp.concatenate(parts, axis=1)
        at[...] = attn
        x2 = x2 + mm(attn, wo[...])
    x2_o[...] = x2
    xhat, _ = norm_parts(x2)
    a2_o[...] = (xhat * gains[1:2, :]).astype(BF16)


GC = 0.7978845608028654
CHUNK = 512


def mlp_kernel(
    sp, a2, dy, wu, wd, *rest, last, count,
):
    pieces, (out_in, *rest) = rest[:count], rest[count:]
    if last:
        da_in, *rest = rest
    out_o, da_o, keep, send, wu_s, wd_s, hact, dhp, acc, perm = rest
    j = pl.program_id(0)
    nj = pl.num_programs(0)
    rows, width = a2.shape

    @pl.when(j == 0)
    def _():
        acc[...] = out_in[...]
        if last:
            da_o[...] = da_in[...]
        else:
            da_o[...] = jnp.zeros_like(da_o)
        wu_s[...] = wu[...]
        wd_s[...] = wd[...]

    @pl.when(j == 1)
    def _():
        n = pieces[0].shape[0] // 2
        put_pieces(sp, [w.at[pl.ds(0, n), :] for w in pieces], wu_s)
        put_pieces(sp, [w.at[pl.ds(n, n), :] for w in pieces], wd_s)

    for r in range(rows // CHUNK):
        rs = pl.ds(r * CHUNK, CHUNK)
        h = mm(a2[rs, :], wu_s[...])
        d = mm_t(dy[rs, :], wd_s[...])
        sq = h * h
        t = jnp.tanh(h * (GC + (GC * 0.044715) * sq))
        half1 = 0.5 + 0.5 * t
        act = (h * half1).astype(BF16)
        slope = half1 + (0.5 * h) * (1.0 - t * t) * (GC + (3 * GC * 0.044715) * sq)
        back = (d * slope).astype(BF16)
        hact[rs, :] = act
        dhp[rs, :] = back
        acc[rs, :] += mm(act, wd_s[...])
        da_o[rs, :] += mm_t(back, wu_s[...])

    store_pieces(t_mm(a2[...], dhp[...]), perm, keep.at[0], send.at[0], sp)
    store_pieces(t_mm(dy[...], hact[...]), perm, keep.at[1], send.at[1], sp)

    @pl.when(j == nj - 1)
    def _():
        out_o[...] = acc[...].astype(out_o.dtype)


def back_one_kernel(
    sp, x2, da2, dy, gains, cos, sin, om, pq_l, pq_r, st_l, st_r, ex_l, ex_r, wo_l, wo_r,
    dx2_o, db_o, gain_o, dq_l, dq_r, dst_l, dst_r, dsm_o, wide_l, wide_r, scratch,
):
    i = pl.program_id(0)

    @pl.when(i == 0)
    def _():
        expand_states(sp, st_l, ex_l, wide_l, scratch)
        expand_states(sp, st_r, ex_r, wide_r, scratch)
        gain_o[...] = jnp.zeros_like(gain_o)
        dst_l[...] = jnp.zeros_like(dst_l)
        dst_r[...] = jnp.zeros_like(dst_r)

    xhat, rstd = norm_parts(x2[...])
    da = da2[...]
    gain_o[...] += row_sums(da * xhat)
    dx2 = dy[...].astype(F32) + norm_back(da, xhat, rstd, gains[1:2, :])
    dx2_o[...] = dx2
    datt = dx2.astype(BF16)
    db_o[...] = datt
    mask = doc_mask(sp, i)
    mask_b = mask.astype(BF16)
    own = own_lanes(64 * SEGS)
    back = omega_back(om[...])
    c, s = cos[...], sin[...]
    for pq, wide, wo, dq, dst in (
        (pq_l, wide_l, wo_l, dq_l, dst_l),
        (pq_r, wide_r, wo_r, dq_r, dst_r),
    ):
        dattn = mm_t(datt, wo[...])
        for g in range(wide.shape[0]):
            feat = lanes(pq, g)
            sprd = spread(feat, mask_b)
            nd = mm(sprd, wide[g])
            inv = 1.0 / lanes(nd, 1)
            attn = lanes(nd, 0) * inv
            dnum = lanes(dattn, g) * inv
            both = jnp.concatenate([dnum, -dnum * attn], axis=1).astype(BF16)
            dpq = collect(mm_t(both, wide[g]), mask)
            dwide = t_mm(sprd, both)
            dst[g] += lanes(dwide, 0) * own + pltpu.roll(lanes(dwide, 1) * own, 64, 1)
            dz = (dpq * gate(feat.astype(F32))).astype(BF16)
            dr = mm(dz, back)
            dq[:, 128 * g : 128 * (g + 1)] = (dr * c + swap_halves(dr * s)).astype(BF16)

    @pl.when(i == pl.num_programs(0) - 1)
    def _():
        at = shared_doc(sp)
        for g in range(dst_l.shape[0]):
            dsm_o[1, g] = dst_l[g, at, :]
            dsm_o[0, g] = dst_r[g, at, :]


def back_two_kernel(
    sp, cos, sin, om, pk_l, pk_r, v_l, v_r, dst_l, dst_r, ex,
    dk_l, dv_l, dk_r, dv_r, wide_l, wide_r, scratch,
):
    i = pl.program_id(0)

    @pl.when(i == 0)
    def _():
        expand_states(sp, dst_l, ex.at[0], wide_l, scratch)
        expand_states(sp, dst_r, ex.at[1], wide_r, scratch)

    mask = doc_mask(sp, i)
    mask_b = mask.astype(BF16)
    back = omega_back(om[...])
    c, s = cos[...], sin[...]
    ones = jnp.ones((BR, 128), BF16)
    for pk, v, wide, dk, dv in (
        (pk_l, v_l, wide_l, dk_l, dv_l),
        (pk_r, v_r, wide_r, dk_r, dv_r),
    ):
        for g in range(wide.shape[0]):
            feat = lanes(pk, g)
            dpk = collect(mm_t(jnp.concatenate([lanes(v, g), ones], axis=1), wide[g]), mask)
            dv[:, 128 * g : 128 * (g + 1)] = mm(spread(feat, mask_b), wide[g, :, :128]).astype(BF16)
            dz = (dpk * gate(feat.astype(F32))).astype(BF16)
            dr = mm(dz, back)
            dk[:, 128 * g : 128 * (g + 1)] = (dr * c + swap_halves(dr * s)).astype(BF16)


def outer_kernel(sp, left0, l0, r0, left1, l1, r1, keep, send, perm):
    for t, (left, sides) in enumerate(((left0, (l0, r0)), (left1, (l1, r1)))):
        for k, right in enumerate(sides):
            store_pieces(t_mm(left[...], right[...]), perm, keep.at[t, k], send.at[t, k], sp)


def input_kernel(x, gains, dx2, dq_l, dk_l, dv_l, dq_r, dk_r, dv_r, w_l, w_r, dx_o, gain_o):
    i = pl.program_id(0)

    @pl.when(i == 0)
    def _():
        gain_o[...] = jnp.zeros_like(gain_o)

    da = None
    for w, parts in ((w_l, (dq_l, dk_l, dv_l)), (w_r, (dq_r, dk_r, dv_r))):
        for k, part in enumerate(parts):
            term = mm_t(part[...], w[k])
            da = term if da is None else da + term
    xhat, rstd = norm_parts(x[...].astype(F32))
    gain_o[...] += row_sums(da * xhat)
    dx_o[...] = dx2[...] + norm_back(da, xhat, rstd, gains[0:1, :])


def whole(a, once=True):
    shape = tuple(a.shape)
    zeros = (0,) * len(shape)
    mode = dict(pipeline_mode=pl.Buffered(1)) if once else {}
    return pl.BlockSpec(shape, lambda i, *_: zeros, **mode)


def by_rows(a, br=BR):
    return pl.BlockSpec((br, a.shape[1]), lambda i, *_: (i, 0))


def call(kernel, grid, scalars, ins, outs, scratch, flops, vmem, into=None):
    args = [a for a, _ in ins]
    moved = sum(a.size * a.dtype.itemsize for a in args)
    moved += sum(s.size * s.dtype.itemsize for s, _ in outs)
    n_in = len(args) + 1
    extra = [] if into is None else [into]
    n_dep = len(extra)

    def body(*refs):
        return kernel(*refs[:n_in], *refs[n_in + n_dep :])

    return pl.pallas_call(
        body,
        out_shape=[s if isinstance(s, jax.ShapeDtypeStruct) else pltpu.HBM(s.shape, s.dtype) for s, _ in outs],
        grid_spec=pltpu.PrefetchScalarGridSpec(
            num_scalar_prefetch=1,
            grid=grid,
            in_specs=[s for _, s in ins] + [pl.BlockSpec(memory_space=pl.ANY)] * n_dep,
            out_specs=[s for _, s in outs],
            scratch_shapes=scratch,
        ),
        compiler_params=pltpu.CompilerParams(
            dimension_semantics=("arbitrary",) * len(grid), vmem_limit_bytes=vmem * MIB
        ),
        cost_estimate=pl.CostEstimate(flops=flops, bytes_accessed=moved, transcendentals=0),
            input_output_aliases={n_in: 0} if extra else {},
    )(scalars, *args, *extra)


def struct(shape, dtype):
    return jax.ShapeDtypeStruct(tuple(shape), dtype)


class Far:
    def __init__(self, shape, dtype):
        self.shape, self.dtype = tuple(shape), jnp.dtype(dtype)
        self.size = int(np.prod(shape))


def far(a):
    return pltpu.with_memory_space_constraint(a, pltpu.HBM)


class Links:
    def __init__(self, n_dp, n_mp):
        self.n_dp, self.n_mp = n_dp, n_mp
        self.fine = n_dp // PIECES

    def dp_xor(self, v, bits):
        return lax.ppermute(v, "dp", [(d, d ^ bits) for d in range(self.n_dp)])

    def mp_swap(self, v):
        return lax.ppermute(v, "mp", [(m, m ^ 1) for m in range(self.n_mp)])

    def both_swap(self, v, bits):
        n = self.n_mp
        pairs = [(d * n + m, (d ^ bits) * n + (m ^ 1)) for d in range(self.n_dp) for m in range(n)]
        return lax.ppermute(v, ("dp", "mp"), pairs)


def total(parts, dtype=BF16):
    return sum(v.astype(F32) for v in parts).astype(dtype)


def after(v, *deps):
    return lax.optimization_barrier((v,) + deps)[0]


class Sum:
    def __init__(self, links, keep, send):
        self.links, self.stage = links, 0
        self.keep, self.leave = (keep,), (send,)

    def launch(self):
        links = self.links

        def along_x(v):
            return links.dp_xor(v, 2 * links.fine)

        core = [lambda v: links.dp_xor(v, links.fine)]
        ways = [core, [along_x, links.mp_swap], [links.mp_swap, along_x]][self.stage]
        self.flight = [way(v) for way, v in zip(ways, self.leave)]

    def land(self):
        stage, got = self.stage, self.flight
        self.stage, self.flight = stage + 1, []
        if stage == 0:
            (keep,), (got,) = self.keep, got
            half = keep.shape[2] // 2
            self.keep = (total((keep[0, :, :half], got[0, :, :half])), total((keep[1, 0], got[1, 0])))
            self.leave = (total((keep[0, :, half:], got[0, :, half:])), total((keep[1, 1], got[1, 1])))
        elif stage == 1:
            (a, b), (ga, gb) = self.keep, got
            half = b.shape[0] // 2
            self.keep = (total((a[0], ga[0])), total((b[:half], gb[:half])))
            self.leave = (total((a[1], ga[1])), total((b[half:], gb[half:])))
        else:
            self.pairs = list(zip(self.keep, got))
            return tuple(got)
        return self.keep + self.leave


class LastSum:
    def __init__(self, links, sums, direct=False, rider=None):
        self.links, self.direct, self.stage = links, direct, 0
        pairs = [p for s in sums for p in s.pairs]
        self.count = len(pairs)
        n = pairs[0][0].shape[0] // (4 if direct else 2)
        cuts = [slice(r * n, (r + 1) * n) for r in range(4 if direct else 2)]
        extra = [] if rider is None else [rider]
        self.keep = jnp.concatenate([total([v[cuts[0]] for v in p]) for p in pairs], axis=0)
        self.leave = [
            jnp.concatenate([total([v[c] for v in p]) for p in pairs] + extra, axis=0) for c in cuts[1:]
        ]

    def launch(self):
        fine = self.links.fine
        ways = (8, 4, 12) if self.direct else (4, 8)[self.stage : self.stage + 1]
        self.flight = [self.links.dp_xor(v, bits * fine) for v, bits in zip(self.leave, ways)]

    def land(self):
        got, keep = self.flight, self.keep
        self.flight, self.stage = [], self.stage + 1
        rows = keep.shape[0]
        if self.direct or self.stage == 2:
            self.riders = [g[rows:] for g in got]
            self.keep, self.leave = total([keep] + [g[:rows] for g in got], F32), []
            return (self.keep,)
        a, g = [v.reshape((self.count, -1) + v.shape[1:]) for v in (keep, got[0])]
        half = a.shape[1] // 2
        near, far_ = [
            total((a[:, c], g[:, c])).reshape((-1,) + a.shape[2:]) for c in (slice(0, half), slice(half, 2 * half))
        ]
        self.keep, self.leave = near, [far_]
        return near, far_

    def result(self):
        sums, bit = self.keep.reshape((self.count, -1) + self.keep.shape[1:]), self.links.fine // 2
        me = lax.axis_index("dp")
        while bit:
            half = sums.shape[1] // 2
            upper = (me // bit) % 2
            out = lax.dynamic_slice_in_dim(sums, (1 - upper) * half, half, 1)
            stay = lax.dynamic_slice_in_dim(sums, upper * half, half, 1)
            sums = stay + self.links.dp_xor(out, bit)
            bit //= 2
        return sums


class Gains:
    def __init__(self, links, v):
        self.links, self.value = links, v

    def launch(self):
        links = self.links
        x = links.dp_xor(self.value, 2 * links.fine)
        self.flight = [x, links.mp_swap(self.value), links.both_swap(self.value, 2 * links.fine)]

    def land(self):
        self.value = self.value + self.flight[0] + self.flight[1] + self.flight[2]
        self.flight = []
        return (self.value,)

    def parts(self, n):
        hi = self.value.astype(BF16)
        lo = (self.value - hi.astype(F32)).astype(BF16)
        return jnp.concatenate([hi, lo], axis=0).reshape(-1, n)

    def take(self, riders):
        shape = (2,) + self.value.shape
        for r in riders:
            self.value = self.value + r.reshape(shape).astype(F32).sum(0)

    def result(self):
        bits = [self.links.fine] + [1 << b for b in range(self.links.fine.bit_length() - 1)]
        for bit in bits:
            self.value = self.value + self.links.dp_xor(self.value, bit)
        return self.value


def settle(done, *chains):
    sums = []
    for c in chains:
        c.flight = list(lax.optimization_barrier((*c.flight, *done[:1])))[: len(c.flight)]
        sums.extend(c.land())
    return done, sums


def launch(*chains):
    for c in chains:
        c.launch()


def rotary_tables(total, head_size):
    places = np.arange(total, dtype=np.float32)
    steps = np.arange(head_size // 2, dtype=np.float32) * np.float32(2.0) / np.float32(head_size)
    rates = np.power(np.float32(10000.0), -steps).astype(np.float32)
    angles = (places[:, None] * rates[None, :]).astype(np.float64)
    cos, sin = np.cos(angles).astype(np.float32), np.sin(angles).astype(np.float32)
    return np.concatenate([cos] * 4, 1), np.concatenate([-sin, sin, -sin, sin], 1)


def on_device(
    n_dp, n_mp, inputs, seg_ids, omega, norm1_gain, qkv_weight, out_weight, norm2_gain, up_weight, down_weight, out_grad
):
    links = Links(n_dp, n_mp)
    x, dy = inputs[0], out_grad[0]
    rows, width = x.shape
    nb = rows // BR
    dp, mp = lax.axis_index("dp"), lax.axis_index("mp")
    quarter = dp % 4
    half = out_weight.shape[0]
    hd = omega.shape[0]
    groups = half // (2 * hd)
    ff = up_weight.shape[1]
    n_mlp = ff // BF

    starts = jnp.sum((seg_ids < jnp.arange(SEGS + 1)[:, None]).astype(jnp.int32), axis=1) - mp * rows
    scalars = jnp.concatenate([starts, jnp.stack([quarter, dp // links.fine, mp])]).astype(jnp.int32)
    wq_mine = jnp.transpose(qkv_weight, (1, 0, 2))

    def piece_of(w, axis=0, count=4):
        n = w.shape[axis] // count
        return lax.dynamic_slice_in_dim(w, (dp % count) * n, n, axis)

    wq_quarter = piece_of(wq_mine, 1).reshape(-1, half)

    cos_np, sin_np = rotary_tables(seg_ids.shape[1], hd)
    table = pl.BlockSpec((BR, 128), lambda i, sp: (sp[S_MP] * nb + i, 0))
    tables = [(far(jnp.asarray(cos_np)), table), (far(jnp.asarray(sin_np)), table)]
    om_t = jnp.transpose(omega)
    om = (om_t, whole(om_t))
    both_gains = jnp.stack([norm1_gain, norm2_gain])
    gains_in = (both_gains, whole(both_gains))

    def rowed(n, dtype, kind=Far):
        s = kind((rows, n), dtype)
        return (s, by_rows(s))

    def kept(shape, dtype, kind=Far):
        s = kind(shape, dtype)
        return (s, whole(s))

    def ws(a):
        return (far(a), whole(a))

    def rs(a):
        return (far(a), by_rows(a))

    def near(pair):
        a, spec = pair
        return (struct(a.shape, a.dtype), spec) if isinstance(a, Far) else (a, spec)

    def near_rows(a):
        return (a, by_rows(a))

    def near_whole(a):
        return (a, whole(a))

    state_out = kept((groups, 64 * SEGS, 128), F32)
    small_out = near(kept((groups, 64, 128), F32))
    one_flops = 2 * rows * width * 3 * half
    def wq_of(w, k):
        return (far(w), pl.BlockSpec((None, width, half), lambda i, *_: (k, 0, 0), pipeline_mode=pl.Buffered(1)))

    rows_out, rows_near = rowed(half, BF16), near(rowed(half, BF16))
    third = one_flops // 3
    wq_y = links.mp_swap(wq_quarter)
    a1, pk_l, v_l, st_l, sm_l = call(
        keys_first_kernel, (nb,), scalars,
        [rs(x), gains_in, wq_of(wq_mine, 1), wq_of(wq_mine, 2)] + tables + [om],
        [near(rowed(width, BF16)), rows_out, rows_out, state_out, small_out], [], 2 * third, 16,
    )
    wq_y, a1, sm_l, *weights = lax.optimization_barrier((wq_y, a1, sm_l, out_weight, up_weight, down_weight))
    wq_x, wq_c = links.dp_xor(wq_y, 2), links.dp_xor(wq_y, 1)
    ex_r = links.mp_swap(sm_l)
    wo_y = links.mp_swap(piece_of(weights[0], 0, 2))
    mlp_parts = []
    for k in range(n_mlp):
        cols = slice(k * BF, (k + 1) * BF)
        mlp_parts.append(jnp.concatenate([piece_of(weights[1][:, cols]), piece_of(weights[2][cols])], axis=0))
    mlp_y = links.mp_swap(mlp_parts[0])

    def queries(a1, w):
        return call(
            queries_kernel, (nb,), scalars, [near_rows(a1), w] + tables + [om], [rows_out], [], third, 14,
        )[0]

    pq_l = queries(a1, wq_of(wq_mine, 0))
    wq_x, wq_c, ex_r, a1, pq_l, mlp_parts[1] = lax.optimization_barrier((wq_x, wq_c, ex_r, a1, pq_l, mlp_parts[1]))
    wq_pieces = (wq_y, wq_c, wq_x, links.dp_xor(wq_x, 1))
    pk_r, v_r, st_r, sm_r, wq_other = call(
        keys_second_kernel, (nb,), scalars,
        [near_rows(a1)] + [near_whole(p) for p in wq_pieces] + tables + [om],
        [rows_out, rows_out, state_out, small_out, kept(wq_mine.shape, BF16)], [], 2 * third, 18,
    )
    wo_y, mlp_y, sm_r, a1 = lax.optimization_barrier((wo_y, mlp_y, sm_r, a1))
    ex_l = links.mp_swap(sm_r)
    wo_pieces = (wo_y, links.dp_xor(wo_y, 1))
    mlp_x, mlp_c = links.dp_xor(mlp_y, 2), links.dp_xor(mlp_y, 1)
    pq_r = queries(a1, wq_of(wq_other, 0))
    ex_l, pq_r, *wo_pieces, mlp_parts[1] = lax.optimization_barrier((ex_l, pq_r, *wo_pieces, mlp_parts[1]))
    next_y = links.mp_swap(mlp_parts[1])
    wide_scratch = pltpu.VMEM((groups, 64 * SEGS, 256), BF16)
    state_scratch = pltpu.VMEM((64 * SEGS, 128), F32)
    at_l, at_r, x2, a2, wo_other = call(
        attend_kernel, (nb,), scalars,
        [rs(x), gains_in, rs(pq_l), rs(pq_r), ws(st_l), ws(st_r), near_whole(ex_l), near_whole(ex_r), ws(out_weight)]
        + [near_whole(p) for p in wo_pieces],
        [rows_out, rows_out, near(rowed(width, F32)), near(rowed(width, BF16)), kept(out_weight.shape, BF16)],
        [wide_scratch, wide_scratch, state_scratch], 2 * rows * width * 2 * half, 20,
    )
    mlp_x, mlp_c, next_y, a2 = lax.optimization_barrier((mlp_x, mlp_c, next_y, a2))
    mlp_pieces = [(mlp_y, mlp_c, mlp_x, links.dp_xor(mlp_x, 1))]
    next_x, next_c = links.dp_xor(next_y, 2), links.dp_xor(next_y, 1)

    grad_scratch = pltpu.VMEM((width, BF), BF16)

    def mlp(k, out_in, da_in):
        last = da_in is not None
        grad = Far((2, 2, width // 2, BF), BF16)
        grad_out = (grad, pl.BlockSpec((2, None, width // 2, BF), lambda j, *_: (0, j, 0, 0)))
        mine_u = pl.BlockSpec((width, BF), lambda j, *_: (0, k), pipeline_mode=pl.Buffered(1))
        mine_d = pl.BlockSpec((BF, width), lambda j, *_: (k, 0), pipeline_mode=pl.Buffered(1))
        return call(
            functools.partial(mlp_kernel, last=last, count=len(mlp_pieces[k])), (2,), scalars,
            [near_whole(a2), near_whole(dy), (far(up_weight), mine_u), (far(down_weight), mine_d)] + [near_whole(p) for p in mlp_pieces[k]]
            + [near_whole(out_in)] + ([near_whole(da_in)] if last else []),
            [(tuple if last else near)(kept((rows, width), BF16 if last else F32)), near(kept((rows, width), F32))] + [grad_out] * 2,
            [grad_scratch, pltpu.VMEM((BF, width), BF16), pltpu.VMEM((rows, BF), BF16), pltpu.VMEM((rows, BF), BF16),
             pltpu.VMEM((rows, width), F32), grad_scratch],
            2 * 6 * 2 * rows * width * BF, 38,
        )

    part_out, part_da, *grads = mlp(0, x2, None)
    next_x, next_c, part_da = lax.optimization_barrier((next_x, next_c, part_da))
    mlp_pieces.append((next_y, next_c, next_x, links.dp_xor(next_x, 1)))
    sum_a = Sum(links, *grads)
    launch(sum_a)
    output, da2, *grads = mlp(1, part_out, part_da)
    sum_b = Sum(links, *grads)
    launch(sum_b)
    (da2,), sums = settle((da2,), sum_a, sum_b)
    da2 = after(da2, *sums)
    launch(sum_a)

    gain8 = near(kept((8, width), F32))
    dx2, db, gain2, dq_l, dq_r, dst_l, dst_r, dsm = call(
        back_one_kernel, (nb,), scalars,
        [near_rows(x2), near_rows(da2), near_rows(dy), gains_in] + tables
        + [om, rs(pq_l), rs(pq_r), ws(st_l), ws(st_r), near_whole(ex_l), near_whole(ex_r), near_whole(out_weight), near_whole(wo_other)],
        [rowed(width, F32), near(rowed(width, BF16)), gain8, near(rowed(half, BF16)), near(rowed(half, BF16)),
         state_out, state_out, near(kept((2, groups, 64, 128), F32))],
        [wide_scratch, wide_scratch, state_scratch], 2 * rows * width * 2 * half, 32,
    )
    (db, dsm), sums = settle((db, dsm), sum_a)
    db = after(db, *sums)
    dex = links.mp_swap(dsm)
    launch(sum_a)

    def outer(first, second):
        n = first[1].shape[1]
        out = near(kept((2, 2, width // 2, n), BF16))
        return call(
            outer_kernel, (1,), scalars, [near_whole(a) for a in first + second], [out, out],
            [pltpu.VMEM((width, n), BF16)], 4 * 2 * rows * width * n, 12,
        )

    grads = outer((db, at_l, at_r), (a1, dq_l, dq_r))
    (keep, send), sums = settle(grads, sum_a)
    sum_b.leave = [after(v, keep) for v in sum_b.leave]
    last_a = LastSum(links, [sum_a])
    dex = after(dex, last_a.keep, *last_a.leave, *sum_b.leave)
    sum_c = Sum(links, keep, send)
    launch(sum_b, sum_c, last_a)
    dk_l, dv_l, dk_r, dv_r = call(
        back_two_kernel, (nb,), scalars,
        tables + [om, rs(pk_l), rs(pk_r), rs(v_l), rs(v_r), ws(dst_l), ws(dst_r), near_whole(dex)],
        [near(rowed(half, BF16))] * 4, [wide_scratch, wide_scratch, state_scratch], 2 * rows * width * half, 18,
    )
    (dk_l, dk_r, dv_l, dv_r), sums = settle((dk_l, dk_r, dv_l, dv_r), sum_b, sum_c, last_a)
    dk_l = after(dk_l, *sums)
    launch(sum_b, sum_c, last_a)
    grads = outer((a1, dk_l, dk_r), (a1, dv_l, dv_r))
    (keep, send), sums = settle(grads, sum_b, last_a)
    sum_d = Sum(links, keep, send)
    last_b = LastSum(links, [sum_b])
    dx2 = after(dx2, keep, last_b.keep, *last_b.leave)
    launch(sum_d, last_b)

    def inward(part, dx2, so_far):
        n = nb // 2
        first = part * n

        def at(a):
            return (a, pl.BlockSpec((BR, a.shape[1]), lambda i, *_: (first + i, 0)))

        def body(sp, *refs):
            input_kernel(*refs)

        s = Far((rows, width), F32)
        return call(
            body, (n,), scalars,
            [at(x), gains_in, at(dx2), at(dq_l), at(dk_l), at(dv_l), at(dq_r), at(dk_r), at(dv_r), near_whole(wq_mine), near_whole(wq_other)],
            [(s, at(s)[1]), gain8], [], one_flops, 18, into=so_far,
        )

    input_grad, gain1a = inward(0, dx2, None)
    (input_grad, gain1a), sums = settle((input_grad, gain1a), sum_d, sum_c, last_b)
    dx2 = after(dx2, *sums)
    launch(sum_d, sum_c, last_b)
    input_grad, gain1b = inward(1, dx2, input_grad)
    (gain1b,), sums = settle((gain1b,), sum_d, sum_c, last_b)
    gains = Gains(links, jnp.stack([(gain1a + gain1b).sum(0), gain2.sum(0)]))
    launch(sum_d, gains)
    settle((), sum_d, gains)
    sum_cd = LastSum(links, [sum_c, sum_d], True, gains.parts(half))
    launch(sum_cd)
    settle((), sum_cd)
    gains.take(sum_cd.riders)
    (up_a, down_a), (up_b, down_b) = last_a.result(), last_b.result()
    out_sum, q_sum, k_sum, v_sum = sum_cd.result()
    up_sum = jnp.concatenate([up_a, up_b], axis=1)
    down_sum = jnp.transpose(jnp.concatenate([down_a, down_b], axis=1))
    out_sum = jnp.transpose(out_sum)
    share = width // (n_dp * n_mp)
    gains = lax.dynamic_slice_in_dim(gains.result(), (dp * n_mp + mp) * share, share, 1)
    qkv_sum = jnp.stack([q_sum, k_sum, v_sum], axis=1)
    return (output[None], input_grad[None], gains[0], qkv_sum, out_sum, gains[1], up_sum, down_sum)


def solution(mesh):
    n_dp, n_mp = mesh.shape["dp"], mesh.shape["mp"]
    return jax.shard_map(
        functools.partial(on_device, n_dp, n_mp),
        mesh=mesh,
        in_specs=(
            P("dp", "mp", None),
            P("dp", None),
            P(),
            P(),
            P(None, None, "mp"),
            P("mp", None),
            P(),
            P(None, "mp"),
            P("mp", None),
            P("dp", "mp", None),
        ),
        out_specs=(
            P("dp", "mp", None),
            P("dp", "mp", None),
            P(("dp", "mp")),
            P("dp", None, "mp"),
            P("mp", "dp"),
            P(("dp", "mp")),
            P("dp", "mp"),
            P("mp", "dp"),
        ),
        check_vma=False,
    )
```

```python
import functools

import jax
import jax.numpy as jnp
import numpy as np
from jax import lax
from jax.experimental import pallas as pl
from jax.experimental.pallas import tpu as pltpu
from jax.sharding import PartitionSpec as P

SEGS = 8
BR = 512
BF = 768
PIECES = 16
F32 = jnp.float32
BF16 = jnp.bfloat16
MIB = 1 << 20
ORDER = [int(format(p, "04b")[::-1], 2) for p in range(PIECES)]

S_QUARTER, S_COARSE, S_MP = 9, 10, 11


def mm(a, b):
    return lax.dot_general(a, b, (((1,), (0,)), ((), ())), preferred_element_type=F32)


def mm_t(a, b):
    return lax.dot_general(a, b, (((1,), (1,)), ((), ())), preferred_element_type=F32)


def t_mm(a, b):
    return lax.dot_general(a, b, (((0,), (0,)), ((), ())), preferred_element_type=F32)


def norm_parts(v):
    mean = jnp.mean(v, axis=-1, keepdims=True)
    centred = v - mean
    var = jnp.mean(centred * centred, axis=-1, keepdims=True)
    rstd = lax.rsqrt(var + 1e-5)
    return centred * rstd, rstd


def norm_back(da, xhat, rstd, gain):
    dxhat = da * gain
    m1 = jnp.mean(dxhat, axis=-1, keepdims=True)
    m2 = jnp.mean(dxhat * xhat, axis=-1, keepdims=True)
    return rstd * (dxhat - m1 - xhat * m2)


def row_sums(v):
    r, n = v.shape
    return jnp.sum(v.reshape(r // 8, 8, n), axis=0)


def lanes(v, g):
    return v[:, 128 * g : 128 * (g + 1)]


def swap_halves(u):
    lane = lax.broadcasted_iota(jnp.int32, u.shape, 1)
    return jnp.where((lane & 63) < 32, pltpu.roll(u, 96, 1), pltpu.roll(u, 32, 1))


def softplus(z):
    e = jnp.exp(-jnp.abs(z))
    series = e * (1.0 + e * (e * (1.0 / 3.0) - 0.5))
    return jnp.maximum(z, 0.0) + jnp.where(e < 0.01, series, jnp.log(1.0 + e))


def gate(p):
    return jnp.where(p < 0.01, p * (1.0 + p * (p * (1.0 / 6.0) - 0.5)), 1.0 - jnp.exp(-p))


def omega_pair(om):
    om = om * om.shape[1] ** (-0.25)
    rows = jnp.concatenate([om, om], axis=0)
    wide = jnp.concatenate([rows, rows], axis=1)
    r = lax.broadcasted_iota(jnp.int32, wide.shape, 0) // 32
    c = lax.broadcasted_iota(jnp.int32, wide.shape, 1) // 64
    return jnp.where(r == c, wide, 0.0)


def omega_split(om):
    pair = omega_pair(om)
    hi = pair.astype(BF16)
    lo = (pair - hi.astype(F32)).astype(BF16)
    top = jnp.concatenate([hi, hi], axis=1)
    bottom = jnp.concatenate([lo, jnp.zeros_like(lo)], axis=1)
    return jnp.concatenate([top, top, bottom, bottom], axis=0)


def omega_back(om):
    pair = omega_pair(om).astype(BF16)
    return jnp.concatenate([pair, jnp.zeros_like(pair)], axis=0)


def shared_doc(sp):
    middle = (1 - sp[S_MP]) * pl.num_programs(0) * BR
    doc = sum((sp[s] <= middle).astype(jnp.int32) for s in range(1, SEGS))
    return pl.ds(pl.multiple_of(doc * 64, 64), 64)


def doc_mask(sp, i):
    parts = []
    for t in range(SEGS // 2):
        lane = lax.broadcasted_iota(jnp.int32, (BR, 128), 1) < 64
        row = lax.broadcasted_iota(jnp.int32, (BR, 128), 0) + i * BR
        low = jnp.where(lane, sp[2 * t], sp[2 * t + 1])
        high = jnp.where(lane, sp[2 * t + 1], sp[2 * t + 2])
        parts.append(jnp.where((row >= low) & (row < high), 1.0, 0.0).astype(F32))
    return jnp.concatenate(parts, axis=1)


def spread(feat, mask):
    return jnp.concatenate([feat] * (SEGS // 2), axis=1) * mask


def collect(wide, mask):
    masked = wide * mask
    total = sum(lanes(masked, t) for t in range(SEGS // 2))
    return total + pltpu.roll(total, 64, 1)


def own_lanes(n):
    row = lax.broadcasted_iota(jnp.int32, (n, 128), 0) // 32
    lane = lax.broadcasted_iota(jnp.int32, (n, 128), 1) // 64
    return jnp.where((row & 1) == lane, 1.0, 0.0).astype(F32)


def expand(state, own):
    return jnp.concatenate([state * own, pltpu.roll(state, 64, 1) * own], axis=1).astype(BF16)


def store_pieces(value, scratch, keep_ref, send_ref, sp):
    d = value.shape[0]
    step = d // PIECES
    scratch[...] = value.astype(BF16)
    for p in range(PIECES):
        at = pl.multiple_of((ORDER[p] ^ sp[S_COARSE]) * step, 16)
        ref = keep_ref if p < PIECES // 2 else send_ref
        q = p % (PIECES // 2)
        ref[q * step : (q + 1) * step, :] = scratch[pl.ds(at, step), :]


def put_pieces(sp, pieces, out):
    n = pieces[0].shape[0]
    own = sp[S_QUARTER] & (len(pieces) - 1)
    for k, piece in enumerate(pieces):
        out[pl.ds(pl.multiple_of((own ^ k) * n, 16), n), :] = piece[...]


def feature(u, cos, sin, split):
    turned = u * cos + swap_halves(u) * sin
    hi = turned.astype(BF16)
    lo = (turned - hi.astype(F32)).astype(BF16)
    z = mm_t(jnp.concatenate([hi, lo], axis=1), split)
    return softplus(lanes(z, 0) + lanes(z, 1)).astype(BF16)


def features(a1, w, cos, sin, om, out):
    split = omega_split(om[...])
    u, c, s = mm(a1, w), cos[...], sin[...]
    for g in range(u.shape[1] // 128):
        out[:, 128 * g : 128 * (g + 1)] = feature(lanes(u, g), c, s, split)


def keys_values(sp, a1, wk, wv, cos, sin, om, pk_o, v_o, st_o, sm_o):
    i = pl.program_id(0)
    mask = doc_mask(sp, i).astype(BF16)
    ones = jnp.ones((BR, 128), BF16)

    @pl.when(i == 0)
    def _():
        st_o[...] = jnp.zeros_like(st_o)

    v = mm(a1, wv).astype(BF16)
    v_o[...] = v
    features(a1, wk, cos, sin, om, pk_o)
    own = own_lanes(64 * SEGS)
    for g in range(st_o.shape[0]):
        wide = t_mm(spread(lanes(pk_o, g), mask), jnp.concatenate([lanes(v, g), ones], axis=1))
        st_o[g] += lanes(wide, 0) * own + lanes(wide, 1) * (1.0 - own)

    @pl.when(i == pl.num_programs(0) - 1)
    def _():
        at = shared_doc(sp)
        for g in range(st_o.shape[0]):
            sm_o[g] = st_o[g, at, :].astype(BF16)


def keys_first_kernel(sp, x, gain, wk, wv, cos, sin, om, a1_o, pk_o, v_o, st_o, sm_o):
    xhat, _ = norm_parts(x[...].astype(F32))
    a1 = (xhat * gain[...]).astype(BF16)
    a1_o[...] = a1
    keys_values(sp, a1, wk[...], wv[...], cos, sin, om, pk_o, v_o, st_o, sm_o)


def keys_second_kernel(sp, a1, *refs):
    *pieces, cos, sin, om, pk_o, v_o, st_o, sm_o, w_o = refs

    @pl.when(pl.program_id(0) == 0)
    def _():
        n = w_o.shape[1] // len(pieces)
        for k in range(3):
            put_pieces(sp, [w.at[pl.ds(k * n, n), :] for w in pieces], w_o.at[k])

    keys_values(sp, a1[...], w_o[1], w_o[2], cos, sin, om, pk_o, v_o, st_o, sm_o)


def queries_kernel(sp, a1, w, cos, sin, om, pq_o):
    features(a1[...], w[...], cos, sin, om, pq_o)


def expand_states(sp, states, extra, out, scratch):
    own = own_lanes(64 * SEGS)
    at = shared_doc(sp)
    for g in range(states.shape[0]):
        scratch[...] = states[g]
        scratch[at, :] += extra[g].astype(F32)
        out[g] = expand(scratch[...], own)


def attend_kernel(
    sp, x, gain, pq_l, pq_r, st_l, st_r, ex_l, ex_r, wo_l, w0, w1,
    at_l, at_r, x2_o, a2_o, wo_o, wide_l, wide_r, scratch,
):
    i = pl.program_id(0)

    @pl.when(i == 0)
    def _():
        expand_states(sp, st_l, ex_l, wide_l, scratch)
        expand_states(sp, st_r, ex_r, wide_r, scratch)
        put_pieces(sp, (w0, w1), wo_o)

    mask = doc_mask(sp, i).astype(BF16)
    x2 = x[...].astype(F32)
    for pq, wide, wo, at in ((pq_l, wide_l, wo_l, at_l), (pq_r, wide_r, wo_o, at_r)):
        parts = []
        for g in range(wide.shape[0]):
            nd = mm(spread(lanes(pq, g), mask), wide[g])
            parts.append((lanes(nd, 0) / lanes(nd, 1)).astype(BF16))
        attn = jnp.concatenate(parts, axis=1)
        at[...] = attn
        x2 = x2 + mm(attn, wo[...])
    x2_o[...] = x2
    xhat, _ = norm_parts(x2)
    a2_o[...] = (xhat * gain[...]).astype(BF16)


GC = 0.7978845608028654
CHUNK = 512


def mlp_kernel(
    sp, a2, dy, wu, wd, *rest, last, count,
):
    pieces, (out_in, *rest) = rest[:count], rest[count:]
    if last:
        da_in, *rest = rest
    out_o, da_o, keep, send, wu_s, wd_s, hact, dhp, acc, perm = rest
    j = pl.program_id(0)
    nj = pl.num_programs(0)
    rows, width = a2.shape

    @pl.when(j == 0)
    def _():
        acc[...] = out_in[...]
        if last:
            da_o[...] = da_in[...]
        else:
            da_o[...] = jnp.zeros_like(da_o)
        wu_s[...] = wu[...]
        wd_s[...] = wd[...]

    @pl.when(j == 1)
    def _():
        n = pieces[0].shape[0] // 2
        put_pieces(sp, [w.at[pl.ds(0, n), :] for w in pieces], wu_s)
        put_pieces(sp, [w.at[pl.ds(n, n), :] for w in pieces], wd_s)

    for r in range(rows // CHUNK):
        rs = pl.ds(r * CHUNK, CHUNK)
        h = mm(a2[rs, :], wu_s[...])
        d = mm_t(dy[rs, :], wd_s[...])
        sq = h * h
        t = jnp.tanh(h * (GC + (GC * 0.044715) * sq))
        half1 = 0.5 + 0.5 * t
        act = (h * half1).astype(BF16)
        slope = half1 + (0.5 * h) * (1.0 - t * t) * (GC + (3 * GC * 0.044715) * sq)
        back = (d * slope).astype(BF16)
        hact[rs, :] = act
        dhp[rs, :] = back
        acc[rs, :] += mm(act, wd_s[...])
        da_o[rs, :] += mm_t(back, wu_s[...])

    store_pieces(t_mm(a2[...], dhp[...]), perm, keep.at[0], send.at[0], sp)
    store_pieces(t_mm(dy[...], hact[...]), perm, keep.at[1], send.at[1], sp)

    @pl.when(j == nj - 1)
    def _():
        out_o[...] = acc[...].astype(out_o.dtype)


def back_one_kernel(
    sp, x2, da2, dy, gain, cos, sin, om, pq_l, pq_r, st_l, st_r, ex_l, ex_r, wo_l, wo_r,
    dx2_o, db_o, gain_o, dq_l, dq_r, dst_l, dst_r, dsm_o, wide_l, wide_r, scratch,
):
    i = pl.program_id(0)

    @pl.when(i == 0)
    def _():
        expand_states(sp, st_l, ex_l, wide_l, scratch)
        expand_states(sp, st_r, ex_r, wide_r, scratch)
        gain_o[...] = jnp.zeros_like(gain_o)
        dst_l[...] = jnp.zeros_like(dst_l)
        dst_r[...] = jnp.zeros_like(dst_r)

    xhat, rstd = norm_parts(x2[...])
    da = da2[...]
    gain_o[...] += row_sums(da * xhat)
    dx2 = dy[...].astype(F32) + norm_back(da, xhat, rstd, gain[...])
    dx2_o[...] = dx2
    datt = dx2.astype(BF16)
    db_o[...] = datt
    mask = doc_mask(sp, i)
    mask_b = mask.astype(BF16)
    own = own_lanes(64 * SEGS)
    back = omega_back(om[...])
    c, s = cos[...], sin[...]
    for pq, wide, wo, dq, dst in (
        (pq_l, wide_l, wo_l, dq_l, dst_l),
        (pq_r, wide_r, wo_r, dq_r, dst_r),
    ):
        dattn = mm_t(datt, wo[...])
        for g in range(wide.shape[0]):
            feat = lanes(pq, g)
            sprd = spread(feat, mask_b)
            nd = mm(sprd, wide[g])
            inv = 1.0 / lanes(nd, 1)
            attn = lanes(nd, 0) * inv
            dnum = lanes(dattn, g) * inv
            both = jnp.concatenate([dnum, -dnum * attn], axis=1).astype(BF16)
            dpq = collect(mm_t(both, wide[g]), mask)
            dwide = t_mm(sprd, both)
            dst[g] += lanes(dwide, 0) * own + pltpu.roll(lanes(dwide, 1) * own, 64, 1)
            dz = (dpq * gate(feat.astype(F32))).astype(BF16)
            dr = mm(dz, back)
            dq[:, 128 * g : 128 * (g + 1)] = (dr * c + swap_halves(dr * s)).astype(BF16)

    @pl.when(i == pl.num_programs(0) - 1)
    def _():
        at = shared_doc(sp)
        for g in range(dst_l.shape[0]):
            dsm_o[1, g] = dst_l[g, at, :].astype(BF16)
            dsm_o[0, g] = dst_r[g, at, :].astype(BF16)


def back_two_kernel(
    sp, cos, sin, om, pk_l, pk_r, v_l, v_r, dst_l, dst_r, ex,
    dk_l, dv_l, dk_r, dv_r, wide_l, wide_r, scratch,
):
    i = pl.program_id(0)

    @pl.when(i == 0)
    def _():
        expand_states(sp, dst_l, ex.at[0], wide_l, scratch)
        expand_states(sp, dst_r, ex.at[1], wide_r, scratch)

    mask = doc_mask(sp, i)
    mask_b = mask.astype(BF16)
    back = omega_back(om[...])
    c, s = cos[...], sin[...]
    ones = jnp.ones((BR, 128), BF16)
    for pk, v, wide, dk, dv in (
        (pk_l, v_l, wide_l, dk_l, dv_l),
        (pk_r, v_r, wide_r, dk_r, dv_r),
    ):
        for g in range(wide.shape[0]):
            feat = lanes(pk, g)
            dpk = collect(mm_t(jnp.concatenate([lanes(v, g), ones], axis=1), wide[g]), mask)
            dv[:, 128 * g : 128 * (g + 1)] = mm(spread(feat, mask_b), wide[g, :, :128]).astype(BF16)
            dz = (dpk * gate(feat.astype(F32))).astype(BF16)
            dr = mm(dz, back)
            dk[:, 128 * g : 128 * (g + 1)] = (dr * c + swap_halves(dr * s)).astype(BF16)


def outer_kernel(sp, left0, l0, r0, left1, l1, r1, keep, send, perm):
    for t, (left, sides) in enumerate(((left0, (l0, r0)), (left1, (l1, r1)))):
        for k, right in enumerate(sides):
            store_pieces(t_mm(left[...], right[...]), perm, keep.at[t, k], send.at[t, k], sp)


def input_kernel(x, gain, dx2, dq_l, dk_l, dv_l, dq_r, dk_r, dv_r, w_l, w_r, dx_o, gain_o):
    i = pl.program_id(0)

    @pl.when(i == 0)
    def _():
        gain_o[...] = jnp.zeros_like(gain_o)

    da = None
    for w, parts in ((w_l, (dq_l, dk_l, dv_l)), (w_r, (dq_r, dk_r, dv_r))):
        for k, part in enumerate(parts):
            term = mm_t(part[...], w[k])
            da = term if da is None else da + term
    xhat, rstd = norm_parts(x[...].astype(F32))
    gain_o[...] += row_sums(da * xhat)
    dx_o[...] = dx2[...] + norm_back(da, xhat, rstd, gain[...])


def whole(a, once=True):
    shape = tuple(a.shape)
    zeros = (0,) * len(shape)
    mode = dict(pipeline_mode=pl.Buffered(1)) if once else {}
    return pl.BlockSpec(shape, lambda i, *_: zeros, **mode)


def by_rows(a, br=BR):
    return pl.BlockSpec((br, a.shape[1]), lambda i, *_: (i, 0))


def call(kernel, grid, scalars, ins, outs, scratch, flops, vmem, into=None):
    args = [a for a, _ in ins]
    moved = sum(a.size * a.dtype.itemsize for a in args)
    moved += sum(s.size * s.dtype.itemsize for s, _ in outs)
    n_in = len(args) + 1
    extra = [] if into is None else [into]
    n_dep = len(extra)

    def body(*refs):
        return kernel(*refs[:n_in], *refs[n_in + n_dep :])

    return pl.pallas_call(
        body,
        out_shape=[s if isinstance(s, jax.ShapeDtypeStruct) else pltpu.HBM(s.shape, s.dtype) for s, _ in outs],
        grid_spec=pltpu.PrefetchScalarGridSpec(
            num_scalar_prefetch=1,
            grid=grid,
            in_specs=[s for _, s in ins] + [pl.BlockSpec(memory_space=pl.ANY)] * n_dep,
            out_specs=[s for _, s in outs],
            scratch_shapes=scratch,
        ),
        compiler_params=pltpu.CompilerParams(
            dimension_semantics=("arbitrary",) * len(grid), vmem_limit_bytes=vmem * MIB
        ),
        cost_estimate=pl.CostEstimate(flops=flops, bytes_accessed=moved, transcendentals=0),
            input_output_aliases={n_in: 0} if extra else {},
    )(scalars, *args, *extra)


def struct(shape, dtype):
    return jax.ShapeDtypeStruct(tuple(shape), dtype)


class Far:
    def __init__(self, shape, dtype):
        self.shape, self.dtype = tuple(shape), jnp.dtype(dtype)
        self.size = int(np.prod(shape))


def far(a):
    return pltpu.with_memory_space_constraint(a, pltpu.HBM)


class Links:
    def __init__(self, n_dp, n_mp):
        self.n_dp, self.n_mp = n_dp, n_mp
        self.fine = n_dp // PIECES

    def dp_xor(self, v, bits):
        return lax.ppermute(v, "dp", [(d, d ^ bits) for d in range(self.n_dp)])

    def mp_swap(self, v):
        return lax.ppermute(v, "mp", [(m, m ^ 1) for m in range(self.n_mp)])

    def both_swap(self, v, bits):
        n = self.n_mp
        pairs = [(d * n + m, (d ^ bits) * n + (m ^ 1)) for d in range(self.n_dp) for m in range(n)]
        return lax.ppermute(v, ("dp", "mp"), pairs)


def total(parts, dtype=BF16):
    return sum(v.astype(F32) for v in parts).astype(dtype)


def after(v, *deps):
    return lax.optimization_barrier((v,) + deps)[0]


class Sum:
    def __init__(self, links, keep, send):
        self.links, self.stage = links, 0
        self.keep, self.leave = (keep,), (send,)

    def launch(self):
        links = self.links

        def along_x(v):
            return links.dp_xor(v, 2 * links.fine)

        core = [lambda v: links.dp_xor(v, links.fine)]
        ways = [core, [along_x, links.mp_swap], [links.mp_swap, along_x]][self.stage]
        self.flight = [way(v) for way, v in zip(ways, self.leave)]

    def land(self):
        stage, got = self.stage, self.flight
        self.stage, self.flight = stage + 1, []
        if stage == 0:
            (keep,), (got,) = self.keep, got
            half = keep.shape[2] // 2
            self.keep = (total((keep[0, :, :half], got[0, :, :half])), total((keep[1, 0], got[1, 0])))
            self.leave = (total((keep[0, :, half:], got[0, :, half:])), total((keep[1, 1], got[1, 1])))
        elif stage == 1:
            (a, b), (ga, gb) = self.keep, got
            half = b.shape[0] // 2
            self.keep = (total((a[0], ga[0])), total((b[:half], gb[:half])))
            self.leave = (total((a[1], ga[1])), total((b[half:], gb[half:])))
        else:
            self.pairs = list(zip(self.keep, got))
            return tuple(got)
        return self.keep + self.leave


class LastSum:
    def __init__(self, links, sums, direct=False, rider=None):
        self.links, self.direct, self.stage = links, direct, 0
        pairs = [p for s in sums for p in s.pairs]
        self.count = len(pairs)
        n = pairs[0][0].shape[0] // (4 if direct else 2)
        cuts = [slice(r * n, (r + 1) * n) for r in range(4 if direct else 2)]
        extra = [] if rider is None else [rider]
        self.keep = jnp.concatenate([total([v[cuts[0]] for v in p]) for p in pairs], axis=0)
        self.leave = [
            jnp.concatenate([total([v[c] for v in p]) for p in pairs] + extra, axis=0) for c in cuts[1:]
        ]

    def launch(self):
        fine = self.links.fine
        ways = (8, 4, 12) if self.direct else (4, 8)[self.stage : self.stage + 1]
        self.flight = [self.links.dp_xor(v, bits * fine) for v, bits in zip(self.leave, ways)]

    def land(self):
        got, keep = self.flight, self.keep
        self.flight, self.stage = [], self.stage + 1
        rows = keep.shape[0]
        if self.direct or self.stage == 2:
            self.riders = [g[rows:] for g in got]
            self.keep, self.leave = total([keep] + [g[:rows] for g in got], F32), []
            return (self.keep,)
        a, g = [v.reshape((self.count, -1) + v.shape[1:]) for v in (keep, got[0])]
        half = a.shape[1] // 2
        near, far_ = [
            total((a[:, c], g[:, c])).reshape((-1,) + a.shape[2:]) for c in (slice(0, half), slice(half, 2 * half))
        ]
        self.keep, self.leave = near, [far_]
        return near, far_

    def result(self):
        sums, bit = self.keep.reshape((self.count, -1) + self.keep.shape[1:]), self.links.fine // 2
        me = lax.axis_index("dp")
        while bit:
            half = sums.shape[1] // 2
            upper = (me // bit) % 2
            out = lax.dynamic_slice_in_dim(sums, (1 - upper) * half, half, 1)
            stay = lax.dynamic_slice_in_dim(sums, upper * half, half, 1)
            sums = stay + self.links.dp_xor(out, bit)
            bit //= 2
        return sums


class Gains:
    def __init__(self, links, v):
        self.links, self.value = links, v

    def launch(self):
        links = self.links
        x = links.dp_xor(self.value, 2 * links.fine)
        self.flight = [x, links.mp_swap(self.value), links.both_swap(self.value, 2 * links.fine)]

    def land(self):
        self.value = self.value + self.flight[0] + self.flight[1] + self.flight[2]
        self.flight = []
        return (self.value,)

    def parts(self, n):
        hi = self.value.astype(BF16)
        lo = (self.value - hi.astype(F32)).astype(BF16)
        return jnp.concatenate([hi, lo], axis=0).reshape(-1, n)

    def take(self, riders):
        shape = (2,) + self.value.shape
        for r in riders:
            self.value = self.value + r.reshape(shape).astype(F32).sum(0)

    def result(self):
        bits = [self.links.fine] + [1 << b for b in range(self.links.fine.bit_length() - 1)]
        for bit in bits:
            self.value = self.value + self.links.dp_xor(self.value, bit)
        return self.value


def settle(done, *chains, first=None):
    sums = []
    if first is not None:
        flat = list(lax.optimization_barrier((*first.flight, *done)))
        first.flight, done = flat[: len(first.flight)], flat[len(first.flight) :]
        sums.extend(first.land())
    for c in chains:
        c.flight = list(lax.optimization_barrier((*c.flight, *done[:1])))[: len(c.flight)]
        sums.extend(c.land())
    return done, sums


def launch(*chains):
    for c in chains:
        c.launch()


def rotary_tables(total, head_size):
    places = np.arange(total, dtype=np.float32)
    steps = np.arange(head_size // 2, dtype=np.float32) * np.float32(2.0) / np.float32(head_size)
    rates = np.power(np.float32(10000.0), -steps).astype(np.float32)
    angles = (places[:, None] * rates[None, :]).astype(np.float64)
    cos, sin = np.cos(angles).astype(np.float32), np.sin(angles).astype(np.float32)
    return np.concatenate([cos] * 4, 1), np.concatenate([-sin, sin, -sin, sin], 1)


def on_device(
    n_dp, n_mp, inputs, seg_ids, omega, norm1_gain, qkv_weight, out_weight, norm2_gain, up_weight, down_weight, out_grad
):
    links = Links(n_dp, n_mp)
    x, dy = inputs[0], out_grad[0]
    rows, width = x.shape
    nb = rows // BR
    dp, mp = lax.axis_index("dp"), lax.axis_index("mp")
    quarter = dp % 4
    half = out_weight.shape[0]
    hd = omega.shape[0]
    groups = half // (2 * hd)
    ff = up_weight.shape[1]
    n_mlp = ff // BF

    starts = jnp.sum((seg_ids < jnp.arange(SEGS + 1)[:, None]).astype(jnp.int32), axis=1) - mp * rows
    scalars = jnp.concatenate([starts, jnp.stack([quarter, dp // links.fine, mp])]).astype(jnp.int32)
    wq_mine = jnp.transpose(qkv_weight, (1, 0, 2))

    def piece_of(w, axis=0, count=4):
        n = w.shape[axis] // count
        return lax.dynamic_slice_in_dim(w, (dp % count) * n, n, axis)

    wq_quarter = piece_of(wq_mine, 1).reshape(-1, half)

    cos_np, sin_np = rotary_tables(seg_ids.shape[1], hd)
    table = pl.BlockSpec((BR, 128), lambda i, sp: (sp[S_MP] * nb + i, 0))
    tables = [(far(jnp.asarray(cos_np)), table), (far(jnp.asarray(sin_np)), table)]
    om_t = jnp.transpose(omega)
    om = (om_t, whole(om_t))
    gain_rows = [g.reshape(1, -1) for g in (norm1_gain, norm2_gain)]
    gain_1, gain_2 = [(g, whole(g)) for g in gain_rows]

    def rowed(n, dtype, kind=Far):
        s = kind((rows, n), dtype)
        return (s, by_rows(s))

    def kept(shape, dtype, kind=Far):
        s = kind(shape, dtype)
        return (s, whole(s))

    def ws(a):
        return (far(a), whole(a))

    def rs(a):
        return (far(a), by_rows(a))

    def near(pair):
        a, spec = pair
        return (struct(a.shape, a.dtype), spec) if isinstance(a, Far) else (a, spec)

    def near_rows(a):
        return (a, by_rows(a))

    def near_whole(a):
        return (a, whole(a))

    state_out = kept((groups, 64 * SEGS, 128), F32)
    small_out = near(kept((groups, 64, 128), BF16))
    one_flops = 2 * rows * width * 3 * half
    def wq_of(w, k):
        return (far(w), pl.BlockSpec((None, width, half), lambda i, *_: (k, 0, 0), pipeline_mode=pl.Buffered(1)))

    rows_out, rows_near = rowed(half, BF16), near(rowed(half, BF16))
    third = one_flops // 3
    wq_y = links.mp_swap(wq_quarter)
    a1, pk_l, v_l, st_l, sm_l = call(
        keys_first_kernel, (nb,), scalars,
        [rs(x), gain_1, wq_of(wq_mine, 1), wq_of(wq_mine, 2)] + tables + [om],
        [near(rowed(width, BF16)), rows_out, rows_out, state_out, small_out], [], 2 * third, 16,
    )
    wq_y, a1, sm_l, *weights = lax.optimization_barrier((wq_y, a1, sm_l, out_weight, up_weight, down_weight))
    wq_x, wq_c = links.dp_xor(wq_y, 2), links.dp_xor(wq_y, 1)
    ex_r = links.mp_swap(sm_l)
    wo_y = links.mp_swap(piece_of(weights[0], 0, 2))
    mlp_parts = []
    for k in range(n_mlp):
        cols = slice(k * BF, (k + 1) * BF)
        mlp_parts.append(jnp.concatenate([piece_of(weights[1][:, cols]), piece_of(weights[2][cols])], axis=0))
    mlp_y = links.mp_swap(mlp_parts[0])

    def queries(a1, w):
        return call(
            queries_kernel, (nb,), scalars, [near_rows(a1), w] + tables + [om], [rows_out], [], third, 14,
        )[0]

    pq_l = queries(a1, wq_of(wq_mine, 0))
    wq_x, wq_c, ex_r, a1, pq_l, mlp_parts[1] = lax.optimization_barrier((wq_x, wq_c, ex_r, a1, pq_l, mlp_parts[1]))
    wq_pieces = (wq_y, wq_c, wq_x, links.dp_xor(wq_x, 1))
    pk_r, v_r, st_r, sm_r, wq_other = call(
        keys_second_kernel, (nb,), scalars,
        [near_rows(a1)] + [near_whole(p) for p in wq_pieces] + tables + [om],
        [rows_out, rows_out, state_out, small_out, kept(wq_mine.shape, BF16)], [], 2 * third, 18,
    )
    wo_y, mlp_y, sm_r, a1 = lax.optimization_barrier((wo_y, mlp_y, sm_r, a1))
    ex_l = links.mp_swap(sm_r)
    wo_pieces = (wo_y, links.dp_xor(wo_y, 1))
    mlp_x, mlp_c = links.dp_xor(mlp_y, 2), links.dp_xor(mlp_y, 1)
    pq_r = queries(a1, wq_of(wq_other, 0))
    ex_l, pq_r, *wo_pieces, mlp_parts[1] = lax.optimization_barrier((ex_l, pq_r, *wo_pieces, mlp_parts[1]))
    next_y = links.mp_swap(mlp_parts[1])
    wide_scratch = pltpu.VMEM((groups, 64 * SEGS, 256), BF16)
    state_scratch = pltpu.VMEM((64 * SEGS, 128), F32)
    at_l, at_r, x2, a2, wo_other = call(
        attend_kernel, (nb,), scalars,
        [rs(x), gain_2, rs(pq_l), rs(pq_r), ws(st_l), ws(st_r), near_whole(ex_l), near_whole(ex_r), ws(out_weight)]
        + [near_whole(p) for p in wo_pieces],
        [rows_out, rows_out, near(rowed(width, F32)), near(rowed(width, BF16)), kept(out_weight.shape, BF16)],
        [wide_scratch, wide_scratch, state_scratch], 2 * rows * width * 2 * half, 20,
    )
    mlp_x, mlp_c, next_y, a2 = lax.optimization_barrier((mlp_x, mlp_c, next_y, a2))
    mlp_pieces = [(mlp_y, mlp_c, mlp_x, links.dp_xor(mlp_x, 1))]
    next_x, next_c = links.dp_xor(next_y, 2), links.dp_xor(next_y, 1)

    grad_scratch = pltpu.VMEM((width, BF), BF16)

    def mlp(k, out_in, da_in):
        last = da_in is not None
        grad = Far((2, 2, width // 2, BF), BF16)
        grad_out = (grad, pl.BlockSpec((2, None, width // 2, BF), lambda j, *_: (0, j, 0, 0)))
        mine_u = pl.BlockSpec((width, BF), lambda j, *_: (0, k), pipeline_mode=pl.Buffered(1))
        mine_d = pl.BlockSpec((BF, width), lambda j, *_: (k, 0), pipeline_mode=pl.Buffered(1))
        return call(
            functools.partial(mlp_kernel, last=last, count=len(mlp_pieces[k])), (2,), scalars,
            [near_whole(a2), near_whole(dy), (far(up_weight), mine_u), (far(down_weight), mine_d)] + [near_whole(p) for p in mlp_pieces[k]]
            + [near_whole(out_in)] + ([near_whole(da_in)] if last else []),
            [(tuple if last else near)(kept((rows, width), BF16 if last else F32)), near(kept((rows, width), F32))] + [grad_out] * 2,
            [grad_scratch, pltpu.VMEM((BF, width), BF16), pltpu.VMEM((rows, BF), BF16), pltpu.VMEM((rows, BF), BF16),
             pltpu.VMEM((rows, width), F32), grad_scratch],
            2 * 6 * 2 * rows * width * BF, 38,
        )

    part_out, part_da, *grads = mlp(0, x2, None)
    next_x, next_c, part_da = lax.optimization_barrier((next_x, next_c, part_da))
    mlp_pieces.append((next_y, next_c, next_x, links.dp_xor(next_x, 1)))
    sum_a = Sum(links, *grads)
    launch(sum_a)
    output, da2, *grads = mlp(1, part_out, part_da)
    sum_b = Sum(links, *grads)
    launch(sum_b)
    (da2,), sums = settle((da2,), sum_a, sum_b)
    da2 = after(da2, *sums)
    launch(sum_a)

    gain8 = near(kept((8, width), F32))
    dx2, db, gain2, dq_l, dq_r, dst_l, dst_r, dsm = call(
        back_one_kernel, (nb,), scalars,
        [near_rows(x2), near_rows(da2), near_rows(dy), gain_2] + tables
        + [om, rs(pq_l), rs(pq_r), ws(st_l), ws(st_r), near_whole(ex_l), near_whole(ex_r), near_whole(out_weight), near_whole(wo_other)],
        [rowed(width, F32), near(rowed(width, BF16)), gain8, near(rowed(half, BF16)), near(rowed(half, BF16)),
         state_out, state_out, near(kept((2, groups, 64, 128), BF16))],
        [wide_scratch, wide_scratch, state_scratch], 2 * rows * width * 2 * half, 32,
    )
    (db, dsm), sums = settle((db, dsm), sum_a)
    db = after(db, *sums)
    dex = links.mp_swap(dsm)
    launch(sum_a)

    def outer(first, second):
        n = first[1].shape[1]
        out = near(kept((2, 2, width // 2, n), BF16))
        return call(
            outer_kernel, (1,), scalars, [near_whole(a) for a in first + second], [out, out],
            [pltpu.VMEM((width, n), BF16)], 4 * 2 * rows * width * n, 12,
        )

    grads = outer((db, at_l, at_r), (a1, dq_l, dq_r))
    (keep, send), sums = settle(grads, sum_a)
    sum_b.leave = [after(v, keep) for v in sum_b.leave]
    last_a = LastSum(links, [sum_a])
    dex = after(dex, last_a.keep, *last_a.leave, *sum_b.leave)
    sum_c = Sum(links, keep, send)
    launch(sum_b, sum_c, last_a)
    dk_l, dv_l, dk_r, dv_r = call(
        back_two_kernel, (nb,), scalars,
        tables + [om, rs(pk_l), rs(pk_r), rs(v_l), rs(v_r), ws(dst_l), ws(dst_r), near_whole(dex)],
        [near(rowed(half, BF16))] * 4, [wide_scratch, wide_scratch, state_scratch], 2 * rows * width * half, 18,
    )
    (dk_l, dk_r, dv_l, dv_r), sums = settle((dk_l, dk_r, dv_l, dv_r), sum_b, sum_c, last_a)
    dk_l = after(dk_l, *sums)
    launch(sum_b, sum_c, last_a)
    grads = outer((a1, dk_l, dk_r), (a1, dv_l, dv_r))
    (keep, send), sums = settle(grads, sum_b, last_a)
    sum_d = Sum(links, keep, send)
    last_b = LastSum(links, [sum_b])
    dx2 = after(dx2, keep, last_b.keep, *last_b.leave)
    launch(sum_d, last_b)

    def inward(part, dx2, so_far):
        n = nb // 2
        first = part * n

        def at(a):
            return (a, pl.BlockSpec((BR, a.shape[1]), lambda i, *_: (first + i, 0)))

        def body(sp, *refs):
            input_kernel(*refs)

        s = Far((rows, width), F32)
        return call(
            body, (n,), scalars,
            [at(x), gain_1, at(dx2), at(dq_l), at(dk_l), at(dv_l), at(dq_r), at(dk_r), at(dv_r), near_whole(wq_mine), near_whole(wq_other)],
            [(s, at(s)[1]), gain8], [], one_flops, 18, into=so_far,
        )

    input_grad, gain1a = inward(0, dx2, None)
    (input_grad, gain1a), sums = settle((input_grad, gain1a), sum_d, sum_c, last_b)
    dx2 = after(dx2, *sums)
    launch(sum_d, sum_c, last_b)
    input_grad, gain1b = inward(1, dx2, input_grad)
    (gain1b,), sums = settle((gain1b,), sum_c, last_b, first=sum_d)
    gains = Gains(links, jnp.stack([(gain1a + gain1b).sum(0), gain2.sum(0)]))
    launch(sum_d, gains)
    settle((), sum_d, gains)
    sum_cd = LastSum(links, [sum_c, sum_d], True, gains.parts(half))
    launch(sum_cd)
    settle((), sum_cd)
    gains.take(sum_cd.riders)
    (up_a, down_a), (up_b, down_b) = last_a.result(), last_b.result()
    out_sum, q_sum, k_sum, v_sum = sum_cd.result()
    up_sum = jnp.concatenate([up_a, up_b], axis=1)
    down_sum = jnp.transpose(jnp.concatenate([down_a, down_b], axis=1))
    out_sum = jnp.transpose(out_sum)
    share = width // (n_dp * n_mp)
    gains = lax.dynamic_slice_in_dim(gains.result(), (dp * n_mp + mp) * share, share, 1)
    qkv_sum = jnp.stack([q_sum, k_sum, v_sum], axis=1)
    return (output[None], input_grad[None], gains[0], qkv_sum, out_sum, gains[1], up_sum, down_sum)


def solution(mesh):
    n_dp, n_mp = mesh.shape["dp"], mesh.shape["mp"]
    return jax.shard_map(
        functools.partial(on_device, n_dp, n_mp),
        mesh=mesh,
        in_specs=(
            P("dp", "mp", None),
            P("dp", None),
            P(),
            P(),
            P(None, None, "mp"),
            P("mp", None),
            P(),
            P(None, "mp"),
            P("mp", None),
            P("dp", "mp", None),
        ),
        out_specs=(
            P("dp", "mp", None),
            P("dp", "mp", None),
            P(("dp", "mp")),
            P("dp", None, "mp"),
            P("mp", "dp"),
            P(("dp", "mp")),
            P("dp", "mp"),
            P("mp", "dp"),
        ),
        check_vma=False,
    )
```

```python
import functools

import jax
import jax.numpy as jnp
import numpy as np
from jax import lax
from jax.experimental import pallas as pl
from jax.experimental.pallas import tpu as pltpu
from jax.sharding import PartitionSpec as P

SEGS = 8
BR = 512
BF = 768
PIECES = 16
F32 = jnp.float32
BF16 = jnp.bfloat16
MIB = 1 << 20
ORDER = [int(format(p, "04b")[::-1], 2) for p in range(PIECES)]

S_QUARTER, S_COARSE, S_MP = 9, 10, 11


def mm(a, b):
    return lax.dot_general(a, b, (((1,), (0,)), ((), ())), preferred_element_type=F32)


def mm_t(a, b):
    return lax.dot_general(a, b, (((1,), (1,)), ((), ())), preferred_element_type=F32)


def t_mm(a, b):
    return lax.dot_general(a, b, (((0,), (0,)), ((), ())), preferred_element_type=F32)


def norm_parts(v):
    mean = jnp.mean(v, axis=-1, keepdims=True)
    centred = v - mean
    var = jnp.mean(centred * centred, axis=-1, keepdims=True)
    rstd = lax.rsqrt(var + 1e-5)
    return centred * rstd, rstd


def norm_back(da, xhat, rstd, gain):
    dxhat = da * gain
    m1 = jnp.mean(dxhat, axis=-1, keepdims=True)
    m2 = jnp.mean(dxhat * xhat, axis=-1, keepdims=True)
    return rstd * (dxhat - m1 - xhat * m2)


def row_sums(v):
    r, n = v.shape
    return jnp.sum(v.reshape(r // 8, 8, n), axis=0)


def lanes(v, g):
    return v[:, 128 * g : 128 * (g + 1)]


def swap_halves(u):
    lane = lax.broadcasted_iota(jnp.int32, u.shape, 1)
    return jnp.where((lane & 63) < 32, pltpu.roll(u, 96, 1), pltpu.roll(u, 32, 1))


def softplus(z):
    e = jnp.exp(-jnp.abs(z))
    series = e * (1.0 + e * (e * (1.0 / 3.0) - 0.5))
    return jnp.maximum(z, 0.0) + jnp.where(e < 0.01, series, jnp.log(1.0 + e))


def gate(p):
    return jnp.where(p < 0.01, p * (1.0 + p * (p * (1.0 / 6.0) - 0.5)), 1.0 - jnp.exp(-p))


def omega_pair(om):
    om = om * om.shape[1] ** (-0.25)
    rows = jnp.concatenate([om, om], axis=0)
    wide = jnp.concatenate([rows, rows], axis=1)
    r = lax.broadcasted_iota(jnp.int32, wide.shape, 0) // 32
    c = lax.broadcasted_iota(jnp.int32, wide.shape, 1) // 64
    return jnp.where(r == c, wide, 0.0)


def omega_split(om):
    pair = omega_pair(om)
    hi = pair.astype(BF16)
    lo = (pair - hi.astype(F32)).astype(BF16)
    top = jnp.concatenate([hi, hi], axis=1)
    bottom = jnp.concatenate([lo, jnp.zeros_like(lo)], axis=1)
    return jnp.concatenate([top, top, bottom, bottom], axis=0)


def omega_back(om):
    pair = omega_pair(om).astype(BF16)
    return jnp.concatenate([pair, jnp.zeros_like(pair)], axis=0)


def shared_doc(sp):
    middle = (1 - sp[S_MP]) * pl.num_programs(0) * BR
    doc = sum((sp[s] <= middle).astype(jnp.int32) for s in range(1, SEGS))
    return pl.ds(pl.multiple_of(doc * 64, 64), 64)


def doc_mask(sp, i):
    parts = []
    for t in range(SEGS // 2):
        lane = lax.broadcasted_iota(jnp.int32, (BR, 128), 1) < 64
        row = lax.broadcasted_iota(jnp.int32, (BR, 128), 0) + i * BR
        low = jnp.where(lane, sp[2 * t], sp[2 * t + 1])
        high = jnp.where(lane, sp[2 * t + 1], sp[2 * t + 2])
        parts.append(jnp.where((row >= low) & (row < high), 1.0, 0.0).astype(F32))
    return jnp.concatenate(parts, axis=1)


def spread(feat, mask):
    return jnp.concatenate([feat] * (SEGS // 2), axis=1) * mask


def collect(wide, mask):
    masked = wide * mask
    total = sum(lanes(masked, t) for t in range(SEGS // 2))
    return total + pltpu.roll(total, 64, 1)


def own_lanes(n):
    row = lax.broadcasted_iota(jnp.int32, (n, 128), 0) // 32
    lane = lax.broadcasted_iota(jnp.int32, (n, 128), 1) // 64
    return jnp.where((row & 1) == lane, 1.0, 0.0).astype(F32)


def expand(state, own):
    return jnp.concatenate([state * own, pltpu.roll(state, 64, 1) * own], axis=1).astype(BF16)


def store_pieces(value, scratch, keep_ref, send_ref, sp):
    d = value.shape[0]
    step = d // PIECES
    scratch[...] = value.astype(BF16)
    for p in range(PIECES):
        at = pl.multiple_of((ORDER[p] ^ sp[S_COARSE]) * step, 16)
        ref = keep_ref if p < PIECES // 2 else send_ref
        q = p % (PIECES // 2)
        ref[q * step : (q + 1) * step, :] = scratch[pl.ds(at, step), :]


def put_pieces(sp, pieces, out):
    n = pieces[0].shape[0]
    own = sp[S_QUARTER] & (len(pieces) - 1)
    for k, piece in enumerate(pieces):
        out[pl.ds(pl.multiple_of((own ^ k) * n, 16), n), :] = piece[...]


def feature(u, cos, sin, split):
    turned = u * cos + swap_halves(u) * sin
    hi = turned.astype(BF16)
    lo = (turned - hi.astype(F32)).astype(BF16)
    z = mm_t(jnp.concatenate([hi, lo], axis=1), split)
    return softplus(lanes(z, 0) + lanes(z, 1)).astype(BF16)


def features(a1, w, cos, sin, om, out):
    split = omega_split(om[...])
    u, c, s = mm(a1, w), cos[...], sin[...]
    for g in range(u.shape[1] // 128):
        out[:, 128 * g : 128 * (g + 1)] = feature(lanes(u, g), c, s, split)


def keys_values(sp, a1, wk, wv, cos, sin, om, pk_o, v_o, st_o, sm_o):
    i = pl.program_id(0)
    mask = doc_mask(sp, i).astype(BF16)
    ones = jnp.ones((BR, 128), BF16)

    @pl.when(i == 0)
    def _():
        st_o[...] = jnp.zeros_like(st_o)

    v = mm(a1, wv).astype(BF16)
    v_o[...] = v
    features(a1, wk, cos, sin, om, pk_o)
    own = own_lanes(64 * SEGS)
    for g in range(st_o.shape[0]):
        wide = t_mm(spread(lanes(pk_o, g), mask), jnp.concatenate([lanes(v, g), ones], axis=1))
        st_o[g] += lanes(wide, 0) * own + lanes(wide, 1) * (1.0 - own)

    @pl.when(i == pl.num_programs(0) - 1)
    def _():
        at = shared_doc(sp)
        for g in range(st_o.shape[0]):
            sm_o[g] = st_o[g, at, :].astype(BF16)


def queries_first_kernel(sp, x, gain, w, cos, sin, om, a1_o, pq_o):
    xhat, _ = norm_parts(x[...].astype(F32))
    a1 = (xhat * gain[...]).astype(BF16)
    a1_o[...] = a1
    features(a1, w[...], cos, sin, om, pq_o)


def keys_first_kernel(sp, a1, wk, wv, cos, sin, om, pk_o, v_o, st_o, sm_o):
    keys_values(sp, a1[...], wk[...], wv[...], cos, sin, om, pk_o, v_o, st_o, sm_o)


def keys_second_kernel(sp, a1, *refs):
    *pieces, cos, sin, om, pk_o, v_o, st_o, sm_o, w_o = refs

    @pl.when(pl.program_id(0) == 0)
    def _():
        n = w_o.shape[1] // len(pieces)
        for k in range(3):
            put_pieces(sp, [w.at[pl.ds(k * n, n), :] for w in pieces], w_o.at[k])

    keys_values(sp, a1[...], w_o[1], w_o[2], cos, sin, om, pk_o, v_o, st_o, sm_o)


def queries_kernel(sp, a1, w, cos, sin, om, pq_o):
    features(a1[...], w[...], cos, sin, om, pq_o)


def expand_states(sp, states, extra, out, scratch):
    own = own_lanes(64 * SEGS)
    at = shared_doc(sp)
    for g in range(states.shape[0]):
        scratch[...] = states[g]
        scratch[at, :] += extra[g].astype(F32)
        out[g] = expand(scratch[...], own)


def attend_kernel(
    sp, x, gain, pq_l, pq_r, st_l, st_r, ex_l, ex_r, wo_l, w0, w1,
    at_l, at_r, x2_o, a2_o, wo_o, wide_l, wide_r, scratch,
):
    i = pl.program_id(0)

    @pl.when(i == 0)
    def _():
        expand_states(sp, st_l, ex_l, wide_l, scratch)
        expand_states(sp, st_r, ex_r, wide_r, scratch)
        put_pieces(sp, (w0, w1), wo_o)

    mask = doc_mask(sp, i).astype(BF16)
    x2 = x[...].astype(F32)
    for pq, wide, wo, at in ((pq_l, wide_l, wo_l, at_l), (pq_r, wide_r, wo_o, at_r)):
        parts = []
        for g in range(wide.shape[0]):
            nd = mm(spread(lanes(pq, g), mask), wide[g])
            parts.append((lanes(nd, 0) / lanes(nd, 1)).astype(BF16))
        attn = jnp.concatenate(parts, axis=1)
        at[...] = attn
        x2 = x2 + mm(attn, wo[...])
    x2_o[...] = x2
    xhat, _ = norm_parts(x2)
    a2_o[...] = (xhat * gain[...]).astype(BF16)


GC = 0.7978845608028654
CHUNK = 512


def mlp_kernel(
    sp, a2, dy, wu, wd, *rest, last, count,
):
    pieces, (out_in, *rest) = rest[:count], rest[count:]
    if last:
        da_in, *rest = rest
    out_o, da_o, keep, send, wu_s, wd_s, hact, dhp, acc, perm = rest
    j = pl.program_id(0)
    nj = pl.num_programs(0)
    rows, width = a2.shape

    @pl.when(j == 0)
    def _():
        acc[...] = out_in[...]
        if last:
            da_o[...] = da_in[...]
        else:
            da_o[...] = jnp.zeros_like(da_o)
        wu_s[...] = wu[...]
        wd_s[...] = wd[...]

    @pl.when(j == 1)
    def _():
        n = pieces[0].shape[0] // 2
        put_pieces(sp, [w.at[pl.ds(0, n), :] for w in pieces], wu_s)
        put_pieces(sp, [w.at[pl.ds(n, n), :] for w in pieces], wd_s)

    for r in range(rows // CHUNK):
        rs = pl.ds(r * CHUNK, CHUNK)
        h = mm(a2[rs, :], wu_s[...])
        d = mm_t(dy[rs, :], wd_s[...])
        sq = h * h
        t = jnp.tanh(h * (GC + (GC * 0.044715) * sq))
        half1 = 0.5 + 0.5 * t
        act = (h * half1).astype(BF16)
        slope = half1 + (0.5 * h) * (1.0 - t * t) * (GC + (3 * GC * 0.044715) * sq)
        back = (d * slope).astype(BF16)
        hact[rs, :] = act
        dhp[rs, :] = back
        acc[rs, :] += mm(act, wd_s[...])
        da_o[rs, :] += mm_t(back, wu_s[...])

    store_pieces(t_mm(a2[...], dhp[...]), perm, keep.at[0], send.at[0], sp)
    store_pieces(t_mm(dy[...], hact[...]), perm, keep.at[1], send.at[1], sp)

    @pl.when(j == nj - 1)
    def _():
        out_o[...] = acc[...].astype(out_o.dtype)


def back_one_kernel(
    sp, x2, da2, dy, gain, cos, sin, om, pq_l, pq_r, st_l, st_r, ex_l, ex_r, wo_l, wo_r,
    dx2_o, db_o, gain_o, dq_l, dq_r, dst_l, dst_r, dsm_o, wide_l, wide_r, scratch,
):
    i = pl.program_id(0)

    @pl.when(i == 0)
    def _():
        expand_states(sp, st_l, ex_l, wide_l, scratch)
        expand_states(sp, st_r, ex_r, wide_r, scratch)
        gain_o[...] = jnp.zeros_like(gain_o)
        dst_l[...] = jnp.zeros_like(dst_l)
        dst_r[...] = jnp.zeros_like(dst_r)

    xhat, rstd = norm_parts(x2[...])
    da = da2[...]
    gain_o[...] += row_sums(da * xhat)
    dx2 = dy[...].astype(F32) + norm_back(da, xhat, rstd, gain[...])
    dx2_o[...] = dx2
    datt = dx2.astype(BF16)
    db_o[...] = datt
    mask = doc_mask(sp, i)
    mask_b = mask.astype(BF16)
    own = own_lanes(64 * SEGS)
    back = omega_back(om[...])
    c, s = cos[...], sin[...]
    for pq, wide, wo, dq, dst in (
        (pq_l, wide_l, wo_l, dq_l, dst_l),
        (pq_r, wide_r, wo_r, dq_r, dst_r),
    ):
        dattn = mm_t(datt, wo[...])
        for g in range(wide.shape[0]):
            feat = lanes(pq, g)
            sprd = spread(feat, mask_b)
            nd = mm(sprd, wide[g])
            inv = 1.0 / lanes(nd, 1)
            attn = lanes(nd, 0) * inv
            dnum = lanes(dattn, g) * inv
            both = jnp.concatenate([dnum, -dnum * attn], axis=1).astype(BF16)
            dpq = collect(mm_t(both, wide[g]), mask)
            dwide = t_mm(sprd, both)
            dst[g] += lanes(dwide, 0) * own + pltpu.roll(lanes(dwide, 1) * own, 64, 1)
            dz = (dpq * gate(feat.astype(F32))).astype(BF16)
            dr = mm(dz, back)
            dq[:, 128 * g : 128 * (g + 1)] = (dr * c + swap_halves(dr * s)).astype(BF16)

    @pl.when(i == pl.num_programs(0) - 1)
    def _():
        at = shared_doc(sp)
        for g in range(dst_l.shape[0]):
            dsm_o[1, g] = dst_l[g, at, :].astype(BF16)
            dsm_o[0, g] = dst_r[g, at, :].astype(BF16)


def back_two_kernel(
    sp, cos, sin, om, pk_l, pk_r, v_l, v_r, dst_l, dst_r, ex,
    dk_l, dv_l, dk_r, dv_r, wide_l, wide_r, scratch,
):
    i = pl.program_id(0)

    @pl.when(i == 0)
    def _():
        expand_states(sp, dst_l, ex.at[0], wide_l, scratch)
        expand_states(sp, dst_r, ex.at[1], wide_r, scratch)

    mask = doc_mask(sp, i)
    mask_b = mask.astype(BF16)
    back = omega_back(om[...])
    c, s = cos[...], sin[...]
    ones = jnp.ones((BR, 128), BF16)
    for pk, v, wide, dk, dv in (
        (pk_l, v_l, wide_l, dk_l, dv_l),
        (pk_r, v_r, wide_r, dk_r, dv_r),
    ):
        for g in range(wide.shape[0]):
            feat = lanes(pk, g)
            dpk = collect(mm_t(jnp.concatenate([lanes(v, g), ones], axis=1), wide[g]), mask)
            dv[:, 128 * g : 128 * (g + 1)] = mm(spread(feat, mask_b), wide[g, :, :128]).astype(BF16)
            dz = (dpk * gate(feat.astype(F32))).astype(BF16)
            dr = mm(dz, back)
            dk[:, 128 * g : 128 * (g + 1)] = (dr * c + swap_halves(dr * s)).astype(BF16)


def outer_kernel(sp, left0, l0, r0, left1, l1, r1, keep, send, perm):
    for t, (left, sides) in enumerate(((left0, (l0, r0)), (left1, (l1, r1)))):
        for k, right in enumerate(sides):
            store_pieces(t_mm(left[...], right[...]), perm, keep.at[t, k], send.at[t, k], sp)


def input_kernel(x, gain, dx2, dq_l, dk_l, dv_l, dq_r, dk_r, dv_r, w_l, w_r, dx_o, gain_o):
    i = pl.program_id(0)

    @pl.when(i == 0)
    def _():
        gain_o[...] = jnp.zeros_like(gain_o)

    da = None
    for w, parts in ((w_l, (dq_l, dk_l, dv_l)), (w_r, (dq_r, dk_r, dv_r))):
        for k, part in enumerate(parts):
            term = mm_t(part[...], w[k])
            da = term if da is None else da + term
    xhat, rstd = norm_parts(x[...].astype(F32))
    gain_o[...] += row_sums(da * xhat)
    dx_o[...] = dx2[...] + norm_back(da, xhat, rstd, gain[...])


def whole(a, once=True):
    shape = tuple(a.shape)
    zeros = (0,) * len(shape)
    mode = dict(pipeline_mode=pl.Buffered(1)) if once else {}
    return pl.BlockSpec(shape, lambda i, *_: zeros, **mode)


def by_rows(a, br=BR):
    return pl.BlockSpec((br, a.shape[1]), lambda i, *_: (i, 0))


def call(kernel, grid, scalars, ins, outs, scratch, flops, vmem, into=None):
    args = [a for a, _ in ins]
    moved = sum(a.size * a.dtype.itemsize for a in args)
    moved += sum(s.size * s.dtype.itemsize for s, _ in outs)
    n_in = len(args) + 1
    extra = [] if into is None else [into]
    n_dep = len(extra)

    def body(*refs):
        return kernel(*refs[:n_in], *refs[n_in + n_dep :])

    return pl.pallas_call(
        body,
        out_shape=[s if isinstance(s, jax.ShapeDtypeStruct) else pltpu.HBM(s.shape, s.dtype) for s, _ in outs],
        grid_spec=pltpu.PrefetchScalarGridSpec(
            num_scalar_prefetch=1,
            grid=grid,
            in_specs=[s for _, s in ins] + [pl.BlockSpec(memory_space=pl.ANY)] * n_dep,
            out_specs=[s for _, s in outs],
            scratch_shapes=scratch,
        ),
        compiler_params=pltpu.CompilerParams(
            dimension_semantics=("arbitrary",) * len(grid), vmem_limit_bytes=vmem * MIB
        ),
        cost_estimate=pl.CostEstimate(flops=flops, bytes_accessed=moved, transcendentals=0),
            input_output_aliases={n_in: 0} if extra else {},
    )(scalars, *args, *extra)


def struct(shape, dtype):
    return jax.ShapeDtypeStruct(tuple(shape), dtype)


class Far:
    def __init__(self, shape, dtype):
        self.shape, self.dtype = tuple(shape), jnp.dtype(dtype)
        self.size = int(np.prod(shape))


def far(a):
    return pltpu.with_memory_space_constraint(a, pltpu.HBM)


class Links:
    def __init__(self, n_dp, n_mp):
        self.n_dp, self.n_mp = n_dp, n_mp
        self.fine = n_dp // PIECES

    def dp_xor(self, v, bits):
        return lax.ppermute(v, "dp", [(d, d ^ bits) for d in range(self.n_dp)])

    def mp_swap(self, v):
        return lax.ppermute(v, "mp", [(m, m ^ 1) for m in range(self.n_mp)])

    def both_swap(self, v, bits):
        n = self.n_mp
        pairs = [(d * n + m, (d ^ bits) * n + (m ^ 1)) for d in range(self.n_dp) for m in range(n)]
        return lax.ppermute(v, ("dp", "mp"), pairs)


def total(parts, dtype=BF16):
    return sum(v.astype(F32) for v in parts).astype(dtype)


def after(v, *deps):
    return lax.optimization_barrier((v,) + deps)[0]


class Sum:
    def __init__(self, links, keep, send):
        self.links, self.stage = links, 0
        self.keep, self.leave = (keep,), (send,)

    def launch(self):
        links = self.links

        def along_x(v):
            return links.dp_xor(v, 2 * links.fine)

        core = [lambda v: links.dp_xor(v, links.fine)]
        ways = [core, [along_x, links.mp_swap], [links.mp_swap, along_x]][self.stage]
        self.flight = [way(v) for way, v in zip(ways, self.leave)]

    def land(self):
        stage, got = self.stage, self.flight
        self.stage, self.flight = stage + 1, []
        if stage == 0:
            (keep,), (got,) = self.keep, got
            half = keep.shape[2] // 2
            self.keep = (total((keep[0, :, :half], got[0, :, :half])), total((keep[1, 0], got[1, 0])))
            self.leave = (total((keep[0, :, half:], got[0, :, half:])), total((keep[1, 1], got[1, 1])))
        elif stage == 1:
            (a, b), (ga, gb) = self.keep, got
            half = b.shape[0] // 2
            self.keep = (total((a[0], ga[0])), total((b[:half], gb[:half])))
            self.leave = (total((a[1], ga[1])), total((b[half:], gb[half:])))
        else:
            self.pairs = list(zip(self.keep, got))
            return tuple(got)
        return self.keep + self.leave


class LastSum:
    def __init__(self, links, sums, direct=False, rider=None):
        self.links, self.direct, self.stage = links, direct, 0
        pairs = [p for s in sums for p in s.pairs]
        self.count = len(pairs)
        n = pairs[0][0].shape[0] // (4 if direct else 2)
        cuts = [slice(r * n, (r + 1) * n) for r in range(4 if direct else 2)]
        extra = [] if rider is None else [rider]
        self.keep = jnp.concatenate([total([v[cuts[0]] for v in p]) for p in pairs], axis=0)
        self.leave = [
            jnp.concatenate([total([v[c] for v in p]) for p in pairs] + extra, axis=0) for c in cuts[1:]
        ]

    def launch(self):
        fine = self.links.fine
        ways = (8, 4, 12) if self.direct else (4, 8)[self.stage : self.stage + 1]
        self.flight = [self.links.dp_xor(v, bits * fine) for v, bits in zip(self.leave, ways)]

    def land(self):
        got, keep = self.flight, self.keep
        self.flight, self.stage = [], self.stage + 1
        rows = keep.shape[0]
        if self.direct or self.stage == 2:
            self.riders = [g[rows:] for g in got]
            self.keep, self.leave = total([keep] + [g[:rows] for g in got], F32), []
            return (self.keep,)
        a, g = [v.reshape((self.count, -1) + v.shape[1:]) for v in (keep, got[0])]
        half = a.shape[1] // 2
        near, far_ = [
            total((a[:, c], g[:, c])).reshape((-1,) + a.shape[2:]) for c in (slice(0, half), slice(half, 2 * half))
        ]
        self.keep, self.leave = near, [far_]
        return near, far_

    def result(self):
        sums, bit = self.keep.reshape((self.count, -1) + self.keep.shape[1:]), self.links.fine // 2
        me = lax.axis_index("dp")
        while bit:
            half = sums.shape[1] // 2
            upper = (me // bit) % 2
            out = lax.dynamic_slice_in_dim(sums, (1 - upper) * half, half, 1)
            stay = lax.dynamic_slice_in_dim(sums, upper * half, half, 1)
            sums = stay + self.links.dp_xor(out, bit)
            bit //= 2
        return sums


class Gains:
    def __init__(self, links, v):
        self.links, self.value = links, v

    def launch(self):
        links = self.links
        x = links.dp_xor(self.value, 2 * links.fine)
        self.flight = [x, links.mp_swap(self.value), links.both_swap(self.value, 2 * links.fine)]

    def land(self):
        self.value = self.value + self.flight[0] + self.flight[1] + self.flight[2]
        self.flight = []
        return (self.value,)

    def parts(self, n):
        hi = self.value.astype(BF16)
        lo = (self.value - hi.astype(F32)).astype(BF16)
        return jnp.concatenate([hi, lo], axis=0).reshape(-1, n)

    def take(self, riders):
        shape = (2,) + self.value.shape
        for r in riders:
            self.value = self.value + r.reshape(shape).astype(F32).sum(0)

    def result(self):
        bits = [self.links.fine] + [1 << b for b in range(self.links.fine.bit_length() - 1)]
        for bit in bits:
            self.value = self.value + self.links.dp_xor(self.value, bit)
        return self.value


def settle(done, *chains, first=None):
    sums = []
    if first is not None:
        flat = list(lax.optimization_barrier((*first.flight, *done)))
        first.flight, done = flat[: len(first.flight)], flat[len(first.flight) :]
        sums.extend(first.land())
    for c in chains:
        c.flight = list(lax.optimization_barrier((*c.flight, *done[:1])))[: len(c.flight)]
        sums.extend(c.land())
    return done, sums


def launch(*chains):
    for c in chains:
        c.launch()


def rotary_tables(total, head_size):
    places = np.arange(total, dtype=np.float32)
    steps = np.arange(head_size // 2, dtype=np.float32) * np.float32(2.0) / np.float32(head_size)
    rates = np.power(np.float32(10000.0), -steps).astype(np.float32)
    angles = (places[:, None] * rates[None, :]).astype(np.float64)
    cos, sin = np.cos(angles).astype(np.float32), np.sin(angles).astype(np.float32)
    return np.concatenate([cos] * 4, 1), np.concatenate([-sin, sin, -sin, sin], 1)


def on_device(
    n_dp, n_mp, inputs, seg_ids, omega, norm1_gain, qkv_weight, out_weight, norm2_gain, up_weight, down_weight, out_grad
):
    links = Links(n_dp, n_mp)
    x, dy = inputs[0], out_grad[0]
    rows, width = x.shape
    nb = rows // BR
    dp, mp = lax.axis_index("dp"), lax.axis_index("mp")
    quarter = dp % 4
    half = out_weight.shape[0]
    hd = omega.shape[0]
    groups = half // (2 * hd)
    ff = up_weight.shape[1]
    n_mlp = ff // BF

    starts = jnp.sum((seg_ids < jnp.arange(SEGS + 1)[:, None]).astype(jnp.int32), axis=1) - mp * rows
    scalars = jnp.concatenate([starts, jnp.stack([quarter, dp // links.fine, mp])]).astype(jnp.int32)
    wq_mine = jnp.transpose(qkv_weight, (1, 0, 2))

    def piece_of(w, axis=0, count=4):
        n = w.shape[axis] // count
        return lax.dynamic_slice_in_dim(w, (dp % count) * n, n, axis)

    wq_quarter = piece_of(wq_mine, 1).reshape(-1, half)

    cos_np, sin_np = rotary_tables(seg_ids.shape[1], hd)
    table = pl.BlockSpec((BR, 128), lambda i, sp: (sp[S_MP] * nb + i, 0))
    tables = [(far(jnp.asarray(cos_np)), table), (far(jnp.asarray(sin_np)), table)]
    om_t = jnp.transpose(omega)
    om = (om_t, whole(om_t))
    gain_rows = [g.reshape(1, -1) for g in (norm1_gain, norm2_gain)]
    gain_1, gain_2 = [(g, whole(g)) for g in gain_rows]

    def rowed(n, dtype, kind=Far):
        s = kind((rows, n), dtype)
        return (s, by_rows(s))

    def kept(shape, dtype, kind=Far):
        s = kind(shape, dtype)
        return (s, whole(s))

    def ws(a):
        return (far(a), whole(a))

    def rs(a):
        return (far(a), by_rows(a))

    def near(pair):
        a, spec = pair
        return (struct(a.shape, a.dtype), spec) if isinstance(a, Far) else (a, spec)

    def near_rows(a):
        return (a, by_rows(a))

    def near_whole(a):
        return (a, whole(a))

    state_out = kept((groups, 64 * SEGS, 128), F32)
    small_out = near(kept((groups, 64, 128), BF16))
    one_flops = 2 * rows * width * 3 * half
    def wq_of(w, k):
        return (far(w), pl.BlockSpec((None, width, half), lambda i, *_: (k, 0, 0), pipeline_mode=pl.Buffered(1)))

    rows_out, rows_near = rowed(half, BF16), near(rowed(half, BF16))
    third = one_flops // 3
    wq_y = links.mp_swap(wq_quarter)
    a1, pq_l = call(
        queries_first_kernel, (nb,), scalars, [rs(x), gain_1, wq_of(wq_mine, 0)] + tables + [om],
        [near(rowed(width, BF16)), rows_out], [], third, 14,
    )
    wq_y, a1, *weights = lax.optimization_barrier((wq_y, a1, out_weight, up_weight, down_weight))
    wq_x, wq_c = links.dp_xor(wq_y, 2), links.dp_xor(wq_y, 1)
    wo_y = links.mp_swap(piece_of(weights[0], 0, 2))
    mlp_parts = []
    for k in range(n_mlp):
        cols = slice(k * BF, (k + 1) * BF)
        mlp_parts.append(jnp.concatenate([piece_of(weights[1][:, cols]), piece_of(weights[2][cols])], axis=0))
    mlp_y = links.mp_swap(mlp_parts[0])
    pk_l, v_l, st_l, sm_l = call(
        keys_first_kernel, (nb,), scalars,
        [near_rows(a1), wq_of(wq_mine, 1), wq_of(wq_mine, 2)] + tables + [om],
        [rows_out, rows_out, state_out, small_out], [], 2 * third, 16,
    )

    def queries(a1, w):
        return call(
            queries_kernel, (nb,), scalars, [near_rows(a1), w] + tables + [om], [rows_out], [], third, 14,
        )[0]

    wq_x, wq_c, a1, sm_l, mlp_parts[1] = lax.optimization_barrier((wq_x, wq_c, a1, sm_l, mlp_parts[1]))
    ex_r = links.mp_swap(sm_l)
    wq_pieces = (wq_y, wq_c, wq_x, links.dp_xor(wq_x, 1))
    pk_r, v_r, st_r, sm_r, wq_other = call(
        keys_second_kernel, (nb,), scalars,
        [near_rows(a1)] + [near_whole(p) for p in wq_pieces] + tables + [om],
        [rows_out, rows_out, state_out, small_out, kept(wq_mine.shape, BF16)], [], 2 * third, 18,
    )
    wo_y, mlp_y, sm_r, a1 = lax.optimization_barrier((wo_y, mlp_y, sm_r, a1))
    ex_l = links.mp_swap(sm_r)
    wo_pieces = (wo_y, links.dp_xor(wo_y, 1))
    mlp_x, mlp_c = links.dp_xor(mlp_y, 2), links.dp_xor(mlp_y, 1)
    ex_l, ex_r, a1, mlp_parts[1] = lax.optimization_barrier((ex_l, ex_r, a1, mlp_parts[1]))
    next_y = links.mp_swap(mlp_parts[1])
    pq_r = queries(a1, wq_of(wq_other, 0))
    pq_r, *wo_pieces = lax.optimization_barrier((pq_r, *wo_pieces))
    wide_scratch = pltpu.VMEM((groups, 64 * SEGS, 256), BF16)
    state_scratch = pltpu.VMEM((64 * SEGS, 128), F32)
    at_l, at_r, x2, a2, wo_other = call(
        attend_kernel, (nb,), scalars,
        [rs(x), gain_2, rs(pq_l), rs(pq_r), ws(st_l), ws(st_r), near_whole(ex_l), near_whole(ex_r), ws(out_weight)]
        + [near_whole(p) for p in wo_pieces],
        [rows_out, rows_out, near(rowed(width, F32)), near(rowed(width, BF16)), kept(out_weight.shape, BF16)],
        [wide_scratch, wide_scratch, state_scratch], 2 * rows * width * 2 * half, 20,
    )
    mlp_x, mlp_c, next_y, a2 = lax.optimization_barrier((mlp_x, mlp_c, next_y, a2))
    mlp_pieces = [(mlp_y, mlp_c, mlp_x, links.dp_xor(mlp_x, 1))]
    next_x, next_c = links.dp_xor(next_y, 2), links.dp_xor(next_y, 1)

    grad_scratch = pltpu.VMEM((width, BF), BF16)

    def mlp(k, out_in, da_in):
        last = da_in is not None
        grad = Far((2, 2, width // 2, BF), BF16)
        grad_out = (grad, pl.BlockSpec((2, None, width // 2, BF), lambda j, *_: (0, j, 0, 0)))
        mine_u = pl.BlockSpec((width, BF), lambda j, *_: (0, k), pipeline_mode=pl.Buffered(1))
        mine_d = pl.BlockSpec((BF, width), lambda j, *_: (k, 0), pipeline_mode=pl.Buffered(1))
        return call(
            functools.partial(mlp_kernel, last=last, count=len(mlp_pieces[k])), (2,), scalars,
            [near_whole(a2), near_whole(dy), (far(up_weight), mine_u), (far(down_weight), mine_d)] + [near_whole(p) for p in mlp_pieces[k]]
            + [near_whole(out_in)] + ([near_whole(da_in)] if last else []),
            [(tuple if last else near)(kept((rows, width), BF16 if last else F32)), near(kept((rows, width), F32))] + [grad_out] * 2,
            [grad_scratch, pltpu.VMEM((BF, width), BF16), pltpu.VMEM((rows, BF), BF16), pltpu.VMEM((rows, BF), BF16),
             pltpu.VMEM((rows, width), F32), grad_scratch],
            2 * 6 * 2 * rows * width * BF, 38,
        )

    part_out, part_da, *grads = mlp(0, x2, None)
    next_x, next_c, part_da = lax.optimization_barrier((next_x, next_c, part_da))
    mlp_pieces.append((next_y, next_c, next_x, links.dp_xor(next_x, 1)))
    sum_a = Sum(links, *grads)
    launch(sum_a)
    output, da2, *grads = mlp(1, part_out, part_da)
    sum_b = Sum(links, *grads)
    launch(sum_b)
    (da2,), sums = settle((da2,), sum_a, sum_b)
    da2 = after(da2, *sums)
    launch(sum_a)

    gain8 = near(kept((8, width), F32))
    dx2, db, gain2, dq_l, dq_r, dst_l, dst_r, dsm = call(
        back_one_kernel, (nb,), scalars,
        [near_rows(x2), near_rows(da2), near_rows(dy), gain_2] + tables
        + [om, rs(pq_l), rs(pq_r), ws(st_l), ws(st_r), near_whole(ex_l), near_whole(ex_r), near_whole(out_weight), near_whole(wo_other)],
        [rowed(width, F32), rowed(width, BF16), gain8, near(rowed(half, BF16)), near(rowed(half, BF16)),
         state_out, state_out, near(kept((2, groups, 64, 128), BF16))],
        [wide_scratch, wide_scratch, state_scratch], 2 * rows * width * 2 * half, 32,
    )
    (db, dsm), sums = settle((db, dsm), sum_a)
    db = after(db, *sums)
    dex = links.mp_swap(dsm)
    launch(sum_a)

    def outer(first, second):
        n = first[1].shape[1]
        out = near(kept((2, 2, width // 2, n), BF16))
        return call(
            outer_kernel, (1,), scalars, [near_whole(a) for a in first + second], [out, out],
            [pltpu.VMEM((width, n), BF16)], 4 * 2 * rows * width * n, 12,
        )

    grads = outer((far(db), far(at_l), far(at_r)), (a1, dq_l, dq_r))
    (keep, send), sums = settle(grads, sum_a)
    sum_b.leave = [after(v, keep) for v in sum_b.leave]
    last_a = LastSum(links, [sum_a])
    dex = after(dex, last_a.keep, *last_a.leave, *sum_b.leave)
    sum_c = Sum(links, keep, send)
    launch(sum_b, sum_c, last_a)
    dk_l, dv_l, dk_r, dv_r = call(
        back_two_kernel, (nb,), scalars,
        tables + [om, rs(pk_l), rs(pk_r), rs(v_l), rs(v_r), ws(dst_l), ws(dst_r), near_whole(dex)],
        [near(rowed(half, BF16))] * 4, [wide_scratch, wide_scratch, state_scratch], 2 * rows * width * half, 18,
    )
    (dk_l, dk_r, dv_l, dv_r), sums = settle((dk_l, dk_r, dv_l, dv_r), sum_b, sum_c, last_a)
    dk_l = after(dk_l, *sums)
    launch(sum_b, sum_c, last_a)
    grads = outer((a1, dk_l, dk_r), (a1, dv_l, dv_r))
    (keep, send), sums = settle(grads, sum_b, last_a)
    sum_d = Sum(links, keep, send)
    last_b = LastSum(links, [sum_b])
    dx2 = after(dx2, keep, last_b.keep, *last_b.leave)
    launch(sum_d, last_b)

    def inward(part, dx2, so_far):
        n = nb // 2
        first = part * n

        def at(a):
            return (a, pl.BlockSpec((BR, a.shape[1]), lambda i, *_: (first + i, 0)))

        def body(sp, *refs):
            input_kernel(*refs)

        s = Far((rows, width), F32)
        return call(
            body, (n,), scalars,
            [at(x), gain_1, at(dx2), at(dq_l), at(dk_l), at(dv_l), at(dq_r), at(dk_r), at(dv_r), near_whole(wq_mine), near_whole(wq_other)],
            [(s, at(s)[1]), gain8], [], one_flops, 18, into=so_far,
        )

    input_grad, gain1a = inward(0, dx2, None)
    (input_grad, gain1a), sums = settle((input_grad, gain1a), sum_d, sum_c, last_b)
    dx2 = after(dx2, *sums)
    launch(sum_d, sum_c, last_b)
    input_grad, gain1b = inward(1, dx2, input_grad)
    (gain1b,), sums = settle((gain1b,), sum_c, last_b, first=sum_d)
    gains = Gains(links, jnp.stack([(gain1a + gain1b).sum(0), gain2.sum(0)]))
    launch(sum_d, gains)
    settle((), sum_d, gains)
    sum_cd = LastSum(links, [sum_c, sum_d], True, gains.parts(half))
    launch(sum_cd)
    settle((), sum_cd)
    gains.take(sum_cd.riders)
    (up_a, down_a), (up_b, down_b) = last_a.result(), last_b.result()
    out_sum, q_sum, k_sum, v_sum = sum_cd.result()
    up_sum = jnp.concatenate([up_a, up_b], axis=1)
    down_sum = jnp.transpose(jnp.concatenate([down_a, down_b], axis=1))
    out_sum = jnp.transpose(out_sum)
    share = width // (n_dp * n_mp)
    gains = lax.dynamic_slice_in_dim(gains.result(), (dp * n_mp + mp) * share, share, 1)
    qkv_sum = jnp.stack([q_sum, k_sum, v_sum], axis=1)
    return (output[None], input_grad[None], gains[0], qkv_sum, out_sum, gains[1], up_sum, down_sum)


def solution(mesh):
    n_dp, n_mp = mesh.shape["dp"], mesh.shape["mp"]
    return jax.shard_map(
        functools.partial(on_device, n_dp, n_mp),
        mesh=mesh,
        in_specs=(
            P("dp", "mp", None),
            P("dp", None),
            P(),
            P(),
            P(None, None, "mp"),
            P("mp", None),
            P(),
            P(None, "mp"),
            P("mp", None),
            P("dp", "mp", None),
        ),
        out_specs=(
            P("dp", "mp", None),
            P("dp", "mp", None),
            P(("dp", "mp")),
            P("dp", None, "mp"),
            P("mp", "dp"),
            P(("dp", "mp")),
            P("dp", "mp"),
            P("mp", "dp"),
        ),
        check_vma=False,
    )
```

```python
import functools

import jax
import jax.numpy as jnp
import numpy as np
from jax import lax
from jax.experimental import pallas as pl
from jax.experimental.pallas import tpu as pltpu
from jax.sharding import PartitionSpec as P

SEGS = 8
BR = 512
BF = 768
PIECES = 16
F32 = jnp.float32
BF16 = jnp.bfloat16
MIB = 1 << 20
ORDER = [int(format(p, "04b")[::-1], 2) for p in range(PIECES)]

S_QUARTER, S_COARSE, S_MP = 9, 10, 11


def mm(a, b):
    return lax.dot_general(a, b, (((1,), (0,)), ((), ())), preferred_element_type=F32)


def mm_t(a, b):
    return lax.dot_general(a, b, (((1,), (1,)), ((), ())), preferred_element_type=F32)


def t_mm(a, b):
    return lax.dot_general(a, b, (((0,), (0,)), ((), ())), preferred_element_type=F32)


def norm_parts(v):
    mean = jnp.mean(v, axis=-1, keepdims=True)
    centred = v - mean
    var = jnp.mean(centred * centred, axis=-1, keepdims=True)
    rstd = lax.rsqrt(var + 1e-5)
    return centred * rstd, rstd


def norm_back(da, xhat, rstd, gain):
    dxhat = da * gain
    m1 = jnp.mean(dxhat, axis=-1, keepdims=True)
    m2 = jnp.mean(dxhat * xhat, axis=-1, keepdims=True)
    return rstd * (dxhat - m1 - xhat * m2)


def row_sums(v):
    r, n = v.shape
    return jnp.sum(v.reshape(r // 8, 8, n), axis=0)


def lanes(v, g):
    return v[:, 128 * g : 128 * (g + 1)]


def swap_halves(u):
    lane = lax.broadcasted_iota(jnp.int32, u.shape, 1)
    return jnp.where((lane & 63) < 32, pltpu.roll(u, 96, 1), pltpu.roll(u, 32, 1))


def softplus(z):
    e = jnp.exp(-jnp.abs(z))
    series = e * (1.0 + e * (e * (1.0 / 3.0) - 0.5))
    return jnp.maximum(z, 0.0) + jnp.where(e < 0.01, series, jnp.log(1.0 + e))


def gate(p):
    return jnp.where(p < 0.01, p * (1.0 + p * (p * (1.0 / 6.0) - 0.5)), 1.0 - jnp.exp(-p))


def omega_pair(om):
    om = om * om.shape[1] ** (-0.25)
    rows = jnp.concatenate([om, om], axis=0)
    wide = jnp.concatenate([rows, rows], axis=1)
    r = lax.broadcasted_iota(jnp.int32, wide.shape, 0) // 32
    c = lax.broadcasted_iota(jnp.int32, wide.shape, 1) // 64
    return jnp.where(r == c, wide, 0.0)


def omega_split(om):
    pair = omega_pair(om)
    hi = pair.astype(BF16)
    lo = (pair - hi.astype(F32)).astype(BF16)
    top = jnp.concatenate([hi, hi], axis=1)
    bottom = jnp.concatenate([lo, jnp.zeros_like(lo)], axis=1)
    return jnp.concatenate([top, top, bottom, bottom], axis=0)


def omega_back(om):
    pair = omega_pair(om).astype(BF16)
    return jnp.concatenate([pair, jnp.zeros_like(pair)], axis=0)


def shared_doc(sp):
    middle = (1 - sp[S_MP]) * pl.num_programs(0) * BR
    doc = sum((sp[s] <= middle).astype(jnp.int32) for s in range(1, SEGS))
    return pl.ds(pl.multiple_of(doc * 64, 64), 64)


def doc_mask(sp, i):
    parts = []
    for t in range(SEGS // 2):
        lane = lax.broadcasted_iota(jnp.int32, (BR, 128), 1) < 64
        row = lax.broadcasted_iota(jnp.int32, (BR, 128), 0) + i * BR
        low = jnp.where(lane, sp[2 * t], sp[2 * t + 1])
        high = jnp.where(lane, sp[2 * t + 1], sp[2 * t + 2])
        parts.append(jnp.where((row >= low) & (row < high), 1.0, 0.0).astype(F32))
    return jnp.concatenate(parts, axis=1)


def spread(feat, mask):
    return jnp.concatenate([feat] * (SEGS // 2), axis=1) * mask


def collect(wide, mask):
    masked = wide * mask
    total = sum(lanes(masked, t) for t in range(SEGS // 2))
    return total + pltpu.roll(total, 64, 1)


def own_lanes(n):
    row = lax.broadcasted_iota(jnp.int32, (n, 128), 0) // 32
    lane = lax.broadcasted_iota(jnp.int32, (n, 128), 1) // 64
    return jnp.where((row & 1) == lane, 1.0, 0.0).astype(F32)


def expand(state, own):
    return jnp.concatenate([state * own, pltpu.roll(state, 64, 1) * own], axis=1).astype(BF16)


def store_pieces(value, scratch, keep_ref, send_ref, sp):
    d = value.shape[0]
    step = d // PIECES
    scratch[...] = value.astype(BF16)
    for p in range(PIECES):
        at = pl.multiple_of((ORDER[p] ^ sp[S_COARSE]) * step, 16)
        ref = keep_ref if p < PIECES // 2 else send_ref
        q = p % (PIECES // 2)
        ref[q * step : (q + 1) * step, :] = scratch[pl.ds(at, step), :]


def put_pieces(sp, pieces, out):
    n = pieces[0].shape[0]
    own = sp[S_QUARTER] & (len(pieces) - 1)
    for k, piece in enumerate(pieces):
        out[pl.ds(pl.multiple_of((own ^ k) * n, 16), n), :] = piece[...]


def feature(u, cos, sin, split):
    turned = u * cos + swap_halves(u) * sin
    hi = turned.astype(BF16)
    lo = (turned - hi.astype(F32)).astype(BF16)
    z = mm_t(jnp.concatenate([hi, lo], axis=1), split)
    return softplus(lanes(z, 0) + lanes(z, 1)).astype(BF16)


def features(a1, w, cos, sin, om, out):
    split = omega_split(om[...])
    u, c, s = mm(a1, w), cos[...], sin[...]
    for g in range(u.shape[1] // 128):
        out[:, 128 * g : 128 * (g + 1)] = feature(lanes(u, g), c, s, split)


def keys_values(sp, a1, wk, wv, cos, sin, om, pk_o, v_o, st_o, sm_o):
    i = pl.program_id(0)
    mask = doc_mask(sp, i).astype(BF16)
    ones = jnp.ones((BR, 128), BF16)

    @pl.when(i == 0)
    def _():
        st_o[...] = jnp.zeros_like(st_o)

    v = mm(a1, wv).astype(BF16)
    v_o[...] = v
    features(a1, wk, cos, sin, om, pk_o)
    own = own_lanes(64 * SEGS)
    for g in range(st_o.shape[0]):
        wide = t_mm(spread(lanes(pk_o, g), mask), jnp.concatenate([lanes(v, g), ones], axis=1))
        st_o[g] += lanes(wide, 0) * own + lanes(wide, 1) * (1.0 - own)

    @pl.when(i == pl.num_programs(0) - 1)
    def _():
        at = shared_doc(sp)
        for g in range(st_o.shape[0]):
            sm_o[g] = st_o[g, at, :].astype(BF16)


def queries_first_kernel(sp, x, gain, w, cos, sin, om, a1_o, pq_o):
    xhat, _ = norm_parts(x[...].astype(F32))
    a1 = (xhat * gain[...]).astype(BF16)
    a1_o[...] = a1
    features(a1, w[...], cos, sin, om, pq_o)


def keys_first_kernel(sp, a1, wk, wv, cos, sin, om, pk_o, v_o, st_o, sm_o):
    keys_values(sp, a1[...], wk[...], wv[...], cos, sin, om, pk_o, v_o, st_o, sm_o)


def keys_second_kernel(sp, a1, *refs):
    *pieces, cos, sin, om, pk_o, v_o, st_o, sm_o, w_o = refs

    @pl.when(pl.program_id(0) == 0)
    def _():
        n = w_o.shape[1] // len(pieces)
        for k in range(3):
            put_pieces(sp, [w.at[pl.ds(k * n, n), :] for w in pieces], w_o.at[k])

    keys_values(sp, a1[...], w_o[1], w_o[2], cos, sin, om, pk_o, v_o, st_o, sm_o)


def queries_kernel(sp, a1, w, cos, sin, om, pq_o):
    features(a1[...], w[...], cos, sin, om, pq_o)


def expand_states(sp, states, extra, out, scratch):
    own = own_lanes(64 * SEGS)
    at = shared_doc(sp)
    for g in range(states.shape[0]):
        scratch[...] = states[g]
        scratch[at, :] += extra[g].astype(F32)
        out[g] = expand(scratch[...], own)


def attend_kernel(
    sp, x, gain, pq_l, pq_r, st_l, st_r, ex_l, ex_r, wo_l, w0, w1,
    at_l, at_r, x2_o, a2_o, wo_o, wide_l, wide_r, scratch,
):
    i = pl.program_id(0)

    @pl.when(i == 0)
    def _():
        expand_states(sp, st_l, ex_l, wide_l, scratch)
        expand_states(sp, st_r, ex_r, wide_r, scratch)
        put_pieces(sp, (w0, w1), wo_o)

    mask = doc_mask(sp, i).astype(BF16)
    x2 = x[...].astype(F32)
    for pq, wide, wo, at in ((pq_l, wide_l, wo_l, at_l), (pq_r, wide_r, wo_o, at_r)):
        parts = []
        for g in range(wide.shape[0]):
            nd = mm(spread(lanes(pq, g), mask), wide[g])
            parts.append((lanes(nd, 0) / lanes(nd, 1)).astype(BF16))
        attn = jnp.concatenate(parts, axis=1)
        at[...] = attn
        x2 = x2 + mm(attn, wo[...])
    x2_o[...] = x2
    xhat, _ = norm_parts(x2)
    a2_o[...] = (xhat * gain[...]).astype(BF16)


GC = 0.7978845608028654
CHUNK = 512


def mlp_kernel(
    sp, a2, dy, wu, wd, *rest, last, count,
):
    pieces, (out_in, *rest) = rest[:count], rest[count:]
    if last:
        da_in, *rest = rest
    out_o, da_o, keep, send, wu_s, wd_s, hact, dhp, acc, perm = rest
    j = pl.program_id(0)
    nj = pl.num_programs(0)
    rows, width = a2.shape

    @pl.when(j == 0)
    def _():
        acc[...] = out_in[...]
        if last:
            da_o[...] = da_in[...]
        else:
            da_o[...] = jnp.zeros_like(da_o)
        wu_s[...] = wu[...]
        wd_s[...] = wd[...]

    @pl.when(j == 1)
    def _():
        n = pieces[0].shape[0] // 2
        put_pieces(sp, [w.at[pl.ds(0, n), :] for w in pieces], wu_s)
        put_pieces(sp, [w.at[pl.ds(n, n), :] for w in pieces], wd_s)

    for r in range(rows // CHUNK):
        rs = pl.ds(r * CHUNK, CHUNK)
        h = mm(a2[rs, :], wu_s[...])
        d = mm_t(dy[rs, :], wd_s[...])
        sq = h * h
        t = jnp.tanh(h * (GC + (GC * 0.044715) * sq))
        half1 = 0.5 + 0.5 * t
        act = (h * half1).astype(BF16)
        slope = half1 + (0.5 * h) * (1.0 - t * t) * (GC + (3 * GC * 0.044715) * sq)
        back = (d * slope).astype(BF16)
        hact[rs, :] = act
        dhp[rs, :] = back
        acc[rs, :] += mm(act, wd_s[...])
        da_o[rs, :] += mm_t(back, wu_s[...])

    store_pieces(t_mm(a2[...], dhp[...]), perm, keep.at[0], send.at[0], sp)
    store_pieces(t_mm(dy[...], hact[...]), perm, keep.at[1], send.at[1], sp)

    @pl.when(j == nj - 1)
    def _():
        out_o[...] = acc[...].astype(out_o.dtype)


def back_one_kernel(
    sp, x2, da2, dy, gain, cos, sin, om, pq_l, pq_r, st_l, st_r, ex_l, ex_r, wo_l, wo_r,
    dx2_o, db_o, gain_o, dq_l, dq_r, dst_l, dst_r, dsm_o, wide_l, wide_r, scratch,
):
    i = pl.program_id(0)

    @pl.when(i == 0)
    def _():
        expand_states(sp, st_l, ex_l, wide_l, scratch)
        expand_states(sp, st_r, ex_r, wide_r, scratch)
        gain_o[...] = jnp.zeros_like(gain_o)
        dst_l[...] = jnp.zeros_like(dst_l)
        dst_r[...] = jnp.zeros_like(dst_r)

    xhat, rstd = norm_parts(x2[...])
    da = da2[...]
    gain_o[...] += row_sums(da * xhat)
    dx2 = dy[...].astype(F32) + norm_back(da, xhat, rstd, gain[...])
    dx2_o[...] = dx2
    datt = dx2.astype(BF16)
    db_o[...] = datt
    mask = doc_mask(sp, i)
    mask_b = mask.astype(BF16)
    own = own_lanes(64 * SEGS)
    back = omega_back(om[...])
    c, s = cos[...], sin[...]
    for pq, wide, wo, dq, dst in (
        (pq_l, wide_l, wo_l, dq_l, dst_l),
        (pq_r, wide_r, wo_r, dq_r, dst_r),
    ):
        dattn = mm_t(datt, wo[...])
        for g in range(wide.shape[0]):
            feat = lanes(pq, g)
            sprd = spread(feat, mask_b)
            nd = mm(sprd, wide[g])
            inv = 1.0 / lanes(nd, 1)
            attn = lanes(nd, 0) * inv
            dnum = lanes(dattn, g) * inv
            both = jnp.concatenate([dnum, -dnum * attn], axis=1).astype(BF16)
            dpq = collect(mm_t(both, wide[g]), mask)
            dwide = t_mm(sprd, both)
            dst[g] += lanes(dwide, 0) * own + pltpu.roll(lanes(dwide, 1) * own, 64, 1)
            dz = (dpq * gate(feat.astype(F32))).astype(BF16)
            dr = mm(dz, back)
            dq[:, 128 * g : 128 * (g + 1)] = (dr * c + swap_halves(dr * s)).astype(BF16)

    @pl.when(i == pl.num_programs(0) - 1)
    def _():
        at = shared_doc(sp)
        for g in range(dst_l.shape[0]):
            dsm_o[1, g] = dst_l[g, at, :].astype(BF16)
            dsm_o[0, g] = dst_r[g, at, :].astype(BF16)


def back_two_kernel(
    sp, cos, sin, om, pk_l, pk_r, v_l, v_r, dst_l, dst_r, ex,
    dk_l, dv_l, dk_r, dv_r, wide_l, wide_r, scratch,
):
    i = pl.program_id(0)

    @pl.when(i == 0)
    def _():
        expand_states(sp, dst_l, ex.at[0], wide_l, scratch)
        expand_states(sp, dst_r, ex.at[1], wide_r, scratch)

    mask = doc_mask(sp, i)
    mask_b = mask.astype(BF16)
    back = omega_back(om[...])
    c, s = cos[...], sin[...]
    ones = jnp.ones((BR, 128), BF16)
    for pk, v, wide, dk, dv in (
        (pk_l, v_l, wide_l, dk_l, dv_l),
        (pk_r, v_r, wide_r, dk_r, dv_r),
    ):
        for g in range(wide.shape[0]):
            feat = lanes(pk, g)
            dpk = collect(mm_t(jnp.concatenate([lanes(v, g), ones], axis=1), wide[g]), mask)
            dv[:, 128 * g : 128 * (g + 1)] = mm(spread(feat, mask_b), wide[g, :, :128]).astype(BF16)
            dz = (dpk * gate(feat.astype(F32))).astype(BF16)
            dr = mm(dz, back)
            dk[:, 128 * g : 128 * (g + 1)] = (dr * c + swap_halves(dr * s)).astype(BF16)


def outer_kernel(sp, left0, l0, r0, left1, l1, r1, keep, send, perm):
    for t, (left, sides) in enumerate(((left0, (l0, r0)), (left1, (l1, r1)))):
        for k, right in enumerate(sides):
            store_pieces(t_mm(left[...], right[...]), perm, keep.at[t, k], send.at[t, k], sp)


def input_kernel(x, gain, dx2, dq_l, dk_l, dv_l, dq_r, dk_r, dv_r, w_l, w_r, dx_o, gain_o):
    i = pl.program_id(0)

    @pl.when(i == 0)
    def _():
        gain_o[...] = jnp.zeros_like(gain_o)

    da = None
    for w, parts in ((w_l, (dq_l, dk_l, dv_l)), (w_r, (dq_r, dk_r, dv_r))):
        for k, part in enumerate(parts):
            term = mm_t(part[...], w[k])
            da = term if da is None else da + term
    xhat, rstd = norm_parts(x[...].astype(F32))
    gain_o[...] += row_sums(da * xhat)
    dx_o[...] = dx2[...] + norm_back(da, xhat, rstd, gain[...])


def whole(a, once=True):
    shape = tuple(a.shape)
    zeros = (0,) * len(shape)
    mode = dict(pipeline_mode=pl.Buffered(1)) if once else {}
    return pl.BlockSpec(shape, lambda i, *_: zeros, **mode)


def by_rows(a, br=BR):
    return pl.BlockSpec((br, a.shape[1]), lambda i, *_: (i, 0))


def call(kernel, grid, scalars, ins, outs, scratch, flops, vmem, into=None):
    args = [a for a, _ in ins]
    moved = sum(a.size * a.dtype.itemsize for a in args)
    moved += sum(s.size * s.dtype.itemsize for s, _ in outs)
    n_in = len(args) + 1
    extra = [] if into is None else [into]
    n_dep = len(extra)

    def body(*refs):
        return kernel(*refs[:n_in], *refs[n_in + n_dep :])

    return pl.pallas_call(
        body,
        out_shape=[s if isinstance(s, jax.ShapeDtypeStruct) else pltpu.HBM(s.shape, s.dtype) for s, _ in outs],
        grid_spec=pltpu.PrefetchScalarGridSpec(
            num_scalar_prefetch=1,
            grid=grid,
            in_specs=[s for _, s in ins] + [pl.BlockSpec(memory_space=pl.ANY)] * n_dep,
            out_specs=[s for _, s in outs],
            scratch_shapes=scratch,
        ),
        compiler_params=pltpu.CompilerParams(
            dimension_semantics=("arbitrary",) * len(grid), vmem_limit_bytes=vmem * MIB
        ),
        cost_estimate=pl.CostEstimate(flops=flops, bytes_accessed=moved, transcendentals=0),
            input_output_aliases={n_in: 0} if extra else {},
    )(scalars, *args, *extra)


def struct(shape, dtype):
    return jax.ShapeDtypeStruct(tuple(shape), dtype)


class Far:
    def __init__(self, shape, dtype):
        self.shape, self.dtype = tuple(shape), jnp.dtype(dtype)
        self.size = int(np.prod(shape))


def far(a):
    return pltpu.with_memory_space_constraint(a, pltpu.HBM)


class Links:
    def __init__(self, n_dp, n_mp):
        self.n_dp, self.n_mp = n_dp, n_mp
        self.fine = n_dp // PIECES

    def dp_xor(self, v, bits):
        return lax.ppermute(v, "dp", [(d, d ^ bits) for d in range(self.n_dp)])

    def mp_swap(self, v):
        return lax.ppermute(v, "mp", [(m, m ^ 1) for m in range(self.n_mp)])

    def both_swap(self, v, bits):
        n = self.n_mp
        pairs = [(d * n + m, (d ^ bits) * n + (m ^ 1)) for d in range(self.n_dp) for m in range(n)]
        return lax.ppermute(v, ("dp", "mp"), pairs)


def total(parts, dtype=BF16):
    return sum(v.astype(F32) for v in parts).astype(dtype)


def after(v, *deps):
    return lax.optimization_barrier((v,) + deps)[0]


class Sum:
    def __init__(self, links, keep, send):
        self.links, self.stage = links, 0
        self.keep, self.leave = (keep,), (send,)

    def launch(self):
        links = self.links

        def along_x(v):
            return links.dp_xor(v, 2 * links.fine)

        core = [lambda v: links.dp_xor(v, links.fine)]
        ways = [core, [along_x, links.mp_swap], [links.mp_swap, along_x]][self.stage]
        self.flight = [way(v) for way, v in zip(ways, self.leave)]

    def land(self):
        stage, got = self.stage, self.flight
        self.stage, self.flight = stage + 1, []
        if stage == 0:
            (keep,), (got,) = self.keep, got
            half = keep.shape[2] // 2
            self.keep = (total((keep[0, :, :half], got[0, :, :half])), total((keep[1, 0], got[1, 0])))
            self.leave = (total((keep[0, :, half:], got[0, :, half:])), total((keep[1, 1], got[1, 1])))
        elif stage == 1:
            (a, b), (ga, gb) = self.keep, got
            half = b.shape[0] // 2
            self.keep = (total((a[0], ga[0])), total((b[:half], gb[:half])))
            self.leave = (total((a[1], ga[1])), total((b[half:], gb[half:])))
        else:
            self.pairs = list(zip(self.keep, got))
            return tuple(got)
        return self.keep + self.leave


class LastSum:
    def __init__(self, links, sums, direct=False, rider=None):
        self.links, self.direct, self.stage = links, direct, 0
        pairs = [p for s in sums for p in s.pairs]
        self.count = len(pairs)
        n = pairs[0][0].shape[0] // (4 if direct else 2)
        cuts = [slice(r * n, (r + 1) * n) for r in range(4 if direct else 2)]
        extra = [] if rider is None else [rider]
        self.keep = jnp.concatenate([total([v[cuts[0]] for v in p]) for p in pairs], axis=0)
        self.leave = [
            jnp.concatenate([total([v[c] for v in p]) for p in pairs] + extra, axis=0) for c in cuts[1:]
        ]

    def launch(self):
        fine = self.links.fine
        ways = (8, 4, 12) if self.direct else (4, 8)[self.stage : self.stage + 1]
        self.flight = [self.links.dp_xor(v, bits * fine) for v, bits in zip(self.leave, ways)]

    def land(self):
        got, keep = self.flight, self.keep
        self.flight, self.stage = [], self.stage + 1
        rows = keep.shape[0]
        if self.direct or self.stage == 2:
            self.riders = [g[rows:] for g in got]
            self.keep, self.leave = total([keep] + [g[:rows] for g in got], F32), []
            return (self.keep,)
        a, g = [v.reshape((self.count, -1) + v.shape[1:]) for v in (keep, got[0])]
        half = a.shape[1] // 2
        near, far_ = [
            total((a[:, c], g[:, c])).reshape((-1,) + a.shape[2:]) for c in (slice(0, half), slice(half, 2 * half))
        ]
        self.keep, self.leave = near, [far_]
        return near, far_

    def result(self):
        sums, bit = self.keep.reshape((self.count, -1) + self.keep.shape[1:]), self.links.fine // 2
        me = lax.axis_index("dp")
        while bit:
            half = sums.shape[1] // 2
            upper = (me // bit) % 2
            out = lax.dynamic_slice_in_dim(sums, (1 - upper) * half, half, 1)
            stay = lax.dynamic_slice_in_dim(sums, upper * half, half, 1)
            sums = stay + self.links.dp_xor(out, bit)
            bit //= 2
        return sums


class Gains:
    def __init__(self, links, v):
        self.links, self.value = links, v

    def launch(self):
        links = self.links
        x = links.dp_xor(self.value, 2 * links.fine)
        self.flight = [x, links.mp_swap(self.value), links.both_swap(self.value, 2 * links.fine)]

    def land(self):
        self.value = self.value + self.flight[0] + self.flight[1] + self.flight[2]
        self.flight = []
        return (self.value,)

    def parts(self, n):
        hi = self.value.astype(BF16)
        lo = (self.value - hi.astype(F32)).astype(BF16)
        return jnp.concatenate([hi, lo], axis=0).reshape(-1, n)

    def take(self, riders):
        shape = (2,) + self.value.shape
        for r in riders:
            self.value = self.value + r.reshape(shape).astype(F32).sum(0)

    def result(self):
        bits = [self.links.fine] + [1 << b for b in range(self.links.fine.bit_length() - 1)]
        for bit in bits:
            self.value = self.value + self.links.dp_xor(self.value, bit)
        return self.value


def settle(done, *chains, first=None):
    sums = []
    if first is not None:
        flat = list(lax.optimization_barrier((*first.flight, *done)))
        first.flight, done = flat[: len(first.flight)], flat[len(first.flight) :]
        sums.extend(first.land())
    for c in chains:
        c.flight = list(lax.optimization_barrier((*c.flight, *done[:1])))[: len(c.flight)]
        sums.extend(c.land())
    return done, sums


def launch(*chains):
    for c in chains:
        c.launch()


def rotary_tables(total, head_size):
    places = np.arange(total, dtype=np.float32)
    steps = np.arange(head_size // 2, dtype=np.float32) * np.float32(2.0) / np.float32(head_size)
    rates = np.power(np.float32(10000.0), -steps).astype(np.float32)
    angles = (places[:, None] * rates[None, :]).astype(np.float64)
    cos, sin = np.cos(angles).astype(np.float32), np.sin(angles).astype(np.float32)
    return np.concatenate([cos] * 4, 1), np.concatenate([-sin, sin, -sin, sin], 1)


def on_device(
    n_dp, n_mp, inputs, seg_ids, omega, norm1_gain, qkv_weight, out_weight, norm2_gain, up_weight, down_weight, out_grad
):
    links = Links(n_dp, n_mp)
    x, dy = inputs[0], out_grad[0]
    rows, width = x.shape
    nb = rows // BR
    dp, mp = lax.axis_index("dp"), lax.axis_index("mp")
    quarter = dp % 4
    half = out_weight.shape[0]
    hd = omega.shape[0]
    groups = half // (2 * hd)
    ff = up_weight.shape[1]
    n_mlp = ff // BF

    starts = jnp.sum((seg_ids < jnp.arange(SEGS + 1)[:, None]).astype(jnp.int32), axis=1) - mp * rows
    scalars = jnp.concatenate([starts, jnp.stack([quarter, dp // links.fine, mp])]).astype(jnp.int32)
    wq_mine = jnp.transpose(qkv_weight, (1, 0, 2))

    def piece_of(w, axis=0, count=4):
        n = w.shape[axis] // count
        return lax.dynamic_slice_in_dim(w, (dp % count) * n, n, axis)

    wq_quarter = piece_of(wq_mine, 1).reshape(-1, half)

    cos_np, sin_np = rotary_tables(seg_ids.shape[1], hd)
    table = pl.BlockSpec((BR, 128), lambda i, sp: (sp[S_MP] * nb + i, 0))
    tables = [(far(jnp.asarray(cos_np)), table), (far(jnp.asarray(sin_np)), table)]
    om_t = jnp.transpose(omega)
    om = (om_t, whole(om_t))
    gain_rows = [g.reshape(1, -1) for g in (norm1_gain, norm2_gain)]
    gain_1, gain_2 = [(g, whole(g)) for g in gain_rows]

    def rowed(n, dtype, kind=Far):
        s = kind((rows, n), dtype)
        return (s, by_rows(s))

    def kept(shape, dtype, kind=Far):
        s = kind(shape, dtype)
        return (s, whole(s))

    def ws(a):
        return (far(a), whole(a))

    def rs(a):
        return (far(a), by_rows(a))

    def near(pair):
        a, spec = pair
        return (struct(a.shape, a.dtype), spec) if isinstance(a, Far) else (a, spec)

    def near_rows(a):
        return (a, by_rows(a))

    def near_whole(a):
        return (a, whole(a))

    state_out = kept((groups, 64 * SEGS, 128), F32)
    small_out = near(kept((groups, 64, 128), BF16))
    one_flops = 2 * rows * width * 3 * half
    def wq_of(w, k):
        return (far(w), pl.BlockSpec((None, width, half), lambda i, *_: (k, 0, 0), pipeline_mode=pl.Buffered(1)))

    rows_out, rows_near = rowed(half, BF16), near(rowed(half, BF16))
    third = one_flops // 3
    wq_y = links.mp_swap(wq_quarter)
    a1, pq_l = call(
        queries_first_kernel, (nb,), scalars, [rs(x), gain_1, wq_of(wq_mine, 0)] + tables + [om],
        [near(rowed(width, BF16)), rows_out], [], third, 14,
    )
    wq_y, a1, *weights = lax.optimization_barrier((wq_y, a1, out_weight, up_weight, down_weight))
    wq_x, wq_c = links.dp_xor(wq_y, 2), links.dp_xor(wq_y, 1)
    wo_y = links.mp_swap(piece_of(weights[0], 0, 2))
    mlp_parts = []
    for k in range(n_mlp):
        cols = slice(k * BF, (k + 1) * BF)
        mlp_parts.append(jnp.concatenate([piece_of(weights[1][:, cols]), piece_of(weights[2][cols])], axis=0))
    mlp_y = links.mp_swap(mlp_parts[0])
    pk_l, v_l, st_l, sm_l = call(
        keys_first_kernel, (nb,), scalars,
        [near_rows(a1), wq_of(wq_mine, 1), wq_of(wq_mine, 2)] + tables + [om],
        [rows_out, rows_out, state_out, small_out], [], 2 * third, 16,
    )

    def queries(a1, w):
        return call(
            queries_kernel, (nb,), scalars, [near_rows(a1), w] + tables + [om], [rows_out], [], third, 14,
        )[0]

    wq_x, wq_c, a1, sm_l, mlp_parts[1] = lax.optimization_barrier((wq_x, wq_c, a1, sm_l, mlp_parts[1]))
    ex_r = links.mp_swap(sm_l)
    wq_pieces = (wq_y, wq_c, wq_x, links.dp_xor(wq_x, 1))
    pk_r, v_r, st_r, sm_r, wq_other = call(
        keys_second_kernel, (nb,), scalars,
        [near_rows(a1)] + [near_whole(p) for p in wq_pieces] + tables + [om],
        [rows_out, rows_out, state_out, small_out, kept(wq_mine.shape, BF16)], [], 2 * third, 18,
    )
    wo_y, mlp_y, sm_r, a1 = lax.optimization_barrier((wo_y, mlp_y, sm_r, a1))
    ex_l = links.mp_swap(sm_r)
    wo_pieces = (wo_y, links.dp_xor(wo_y, 1))
    mlp_x, mlp_c = links.dp_xor(mlp_y, 2), links.dp_xor(mlp_y, 1)
    ex_l, ex_r, a1, mlp_parts[1] = lax.optimization_barrier((ex_l, ex_r, a1, mlp_parts[1]))
    next_y = links.mp_swap(mlp_parts[1])
    pq_r = queries(a1, wq_of(wq_other, 0))
    pq_r, *wo_pieces = lax.optimization_barrier((pq_r, *wo_pieces))
    wide_scratch = pltpu.VMEM((groups, 64 * SEGS, 256), BF16)
    state_scratch = pltpu.VMEM((64 * SEGS, 128), F32)
    at_l, at_r, x2, a2, wo_other = call(
        attend_kernel, (nb,), scalars,
        [rs(x), gain_2, rs(pq_l), rs(pq_r), ws(st_l), ws(st_r), near_whole(ex_l), near_whole(ex_r), ws(out_weight)]
        + [near_whole(p) for p in wo_pieces],
        [rows_out, rows_out, near(rowed(width, F32)), near(rowed(width, BF16)), kept(out_weight.shape, BF16)],
        [wide_scratch, wide_scratch, state_scratch], 2 * rows * width * 2 * half, 20,
    )
    mlp_x, mlp_c, next_y, a2 = lax.optimization_barrier((mlp_x, mlp_c, next_y, a2))
    mlp_pieces = [(mlp_y, mlp_c, mlp_x, links.dp_xor(mlp_x, 1))]
    next_x, next_c = links.dp_xor(next_y, 2), links.dp_xor(next_y, 1)

    grad_scratch = pltpu.VMEM((width, BF), BF16)

    def mlp(k, out_in, da_in):
        last = da_in is not None
        grad = Far((2, 2, width // 2, BF), BF16)
        grad_out = (grad, pl.BlockSpec((2, None, width // 2, BF), lambda j, *_: (0, j, 0, 0)))
        mine_u = pl.BlockSpec((width, BF), lambda j, *_: (0, k), pipeline_mode=pl.Buffered(1))
        mine_d = pl.BlockSpec((BF, width), lambda j, *_: (k, 0), pipeline_mode=pl.Buffered(1))
        return call(
            functools.partial(mlp_kernel, last=last, count=len(mlp_pieces[k])), (2,), scalars,
            [near_whole(a2), near_whole(dy), (far(up_weight), mine_u), (far(down_weight), mine_d)] + [near_whole(p) for p in mlp_pieces[k]]
            + [near_whole(out_in)] + ([near_whole(da_in)] if last else []),
            [(tuple if last else near)(kept((rows, width), BF16 if last else F32)), near(kept((rows, width), F32))] + [grad_out] * 2,
            [grad_scratch, pltpu.VMEM((BF, width), BF16), pltpu.VMEM((rows, BF), BF16), pltpu.VMEM((rows, BF), BF16),
             pltpu.VMEM((rows, width), F32), grad_scratch],
            2 * 6 * 2 * rows * width * BF, 38,
        )

    part_out, part_da, *grads = mlp(0, x2, None)
    next_x, next_c, part_da = lax.optimization_barrier((next_x, next_c, part_da))
    mlp_pieces.append((next_y, next_c, next_x, links.dp_xor(next_x, 1)))
    sum_a = Sum(links, *grads)
    launch(sum_a)
    output, da2, *grads = mlp(1, part_out, part_da)
    sum_b = Sum(links, *grads)
    launch(sum_b)
    (da2,), sums = settle((da2,), sum_a, sum_b)
    da2 = after(da2, *sums)
    launch(sum_a)

    gain8 = near(kept((8, width), F32))
    dx2, db, gain2, dq_l, dq_r, dst_l, dst_r, dsm = call(
        back_one_kernel, (nb,), scalars,
        [near_rows(x2), near_rows(da2), near_rows(dy), gain_2] + tables
        + [om, rs(pq_l), rs(pq_r), ws(st_l), ws(st_r), near_whole(ex_l), near_whole(ex_r), near_whole(out_weight), near_whole(wo_other)],
        [rowed(width, F32), rowed(width, BF16), gain8, near(rowed(half, BF16)), near(rowed(half, BF16)),
         state_out, state_out, near(kept((2, groups, 64, 128), BF16))],
        [wide_scratch, wide_scratch, state_scratch], 2 * rows * width * 2 * half, 32,
    )
    (db, dsm), sums = settle((db, dsm), sum_a)
    db = after(db, *sums)
    dex = links.mp_swap(dsm)
    launch(sum_a)

    def outer(first, second):
        n = first[1].shape[1]
        out = near(kept((2, 2, width // 2, n), BF16))
        return call(
            outer_kernel, (1,), scalars, [near_whole(a) for a in first + second], [out, out],
            [pltpu.VMEM((width, n), BF16)], 4 * 2 * rows * width * n, 12,
        )

    grads = outer((far(db), far(at_l), far(at_r)), (a1, dq_l, dq_r))
    (keep, send), sums = settle(grads, sum_a)
    sum_b.leave = [after(v, keep) for v in sum_b.leave]
    last_a = LastSum(links, [sum_a])
    dex = after(dex, last_a.keep, *last_a.leave, *sum_b.leave)
    sum_c = Sum(links, keep, send)
    launch(sum_b, sum_c, last_a)
    dk_l, dv_l, dk_r, dv_r = call(
        back_two_kernel, (nb,), scalars,
        tables + [om, rs(pk_l), rs(pk_r), rs(v_l), rs(v_r), ws(dst_l), ws(dst_r), near_whole(dex)],
        [near(rowed(half, BF16))] * 4, [wide_scratch, wide_scratch, state_scratch], 2 * rows * width * half, 18,
    )
    (dk_l, dk_r, dv_l, dv_r), sums = settle((dk_l, dk_r, dv_l, dv_r), sum_b, sum_c, last_a)
    dk_l = after(dk_l, *sums)
    launch(sum_b, sum_c, last_a)
    grads = outer((a1, dk_l, dk_r), (a1, dv_l, dv_r))
    (keep, send), sums = settle(grads, sum_b, last_a)
    sum_d = Sum(links, keep, send)
    last_b = LastSum(links, [sum_b])
    dx2 = after(dx2, keep, last_b.keep, *last_b.leave)
    launch(sum_d, last_b)

    def inward(part, dx2, so_far):
        n = nb // 2
        first = part * n

        def at(a):
            return (a, pl.BlockSpec((BR, a.shape[1]), lambda i, *_: (first + i, 0)))

        def body(sp, *refs):
            input_kernel(*refs)

        s = Far((rows, width), F32)
        return call(
            body, (n,), scalars,
            [at(x), gain_1, at(dx2), at(dq_l), at(dk_l), at(dv_l), at(dq_r), at(dk_r), at(dv_r), near_whole(wq_mine), near_whole(wq_other)],
            [(s, at(s)[1]), gain8], [], one_flops, 18, into=so_far,
        )

    input_grad, gain1a = inward(0, dx2, None)
    (input_grad, gain1a), sums = settle((input_grad, gain1a), sum_d, sum_c, last_b)
    dx2 = after(dx2, *sums)
    launch(sum_d, sum_c, last_b)
    input_grad, gain1b = inward(1, dx2, input_grad)
    (gain1b,), sums = settle((gain1b,), sum_c, last_b, first=sum_d)
    gains = Gains(links, after(jnp.stack([(gain1a + gain1b).sum(0), gain2.sum(0)]), *sum_d.leave))
    launch(sum_d, gains)
    settle((), sum_d, gains)
    sum_cd = LastSum(links, [sum_c, sum_d], True, gains.parts(half))
    launch(sum_cd)
    settle((), sum_cd)
    gains.take(sum_cd.riders)
    (up_a, down_a), (up_b, down_b) = last_a.result(), last_b.result()
    out_sum, q_sum, k_sum, v_sum = sum_cd.result()
    up_sum = jnp.concatenate([up_a, up_b], axis=1)
    down_sum = jnp.transpose(jnp.concatenate([down_a, down_b], axis=1))
    out_sum = jnp.transpose(out_sum)
    share = width // (n_dp * n_mp)
    gains = lax.dynamic_slice_in_dim(gains.result(), (dp * n_mp + mp) * share, share, 1)
    qkv_sum = jnp.stack([q_sum, k_sum, v_sum], axis=1)
    return (output[None], input_grad[None], gains[0], qkv_sum, out_sum, gains[1], up_sum, down_sum)


def solution(mesh):
    n_dp, n_mp = mesh.shape["dp"], mesh.shape["mp"]
    return jax.shard_map(
        functools.partial(on_device, n_dp, n_mp),
        mesh=mesh,
        in_specs=(
            P("dp", "mp", None),
            P("dp", None),
            P(),
            P(),
            P(None, None, "mp"),
            P("mp", None),
            P(),
            P(None, "mp"),
            P("mp", None),
            P("dp", "mp", None),
        ),
        out_specs=(
            P("dp", "mp", None),
            P("dp", "mp", None),
            P(("dp", "mp")),
            P("dp", None, "mp"),
            P("mp", "dp"),
            P(("dp", "mp")),
            P("dp", "mp"),
            P("mp", "dp"),
        ),
        check_vma=False,
    )
```
